32 devices in a mesh: grp: 2 (over y), row: 4 (over z), col: 4 (over x, core).
Axes of the slice: x: 2, y: 2, z: 4, core: 2. Of those that a mesh axis runs over, the one named last changes fastest.
Arguments:
- sigma_anc: float32 [16384, 8192], P(('grp', 'row'), 'col'), parts along dimension 0, may hold values from -0.15625 to 0.15625
- panel: float32 [32, 6, 256, 256], P(('grp', 'col'), None, 'row'), parts along dimension 0, may hold values from -6 to 6
- diag_inv: float32 [32, 256, 256], P(('grp', 'col'), 'row'), parts along dimension 0, as said below
- structure: int32 [16, 6], P('col'), may hold values from 0 to 31, as said below
Outputs:
- sigma_off: float32 [32, 6, 256, 256], P(('grp', 'col'), None, 'row'), parts along dimension 0
- sigma_diag: float32 [32, 256, 256], P(('grp', 'col'), 'row'), parts along dimension 0
The draws below stay inside these ranges and needn't reach their ends.
There are 2 independent parts, one for each index of `grp`. The reference program is written for one: setup_inputs(seed, part) draws one part's arguments, and reference() takes and returns one part's arrays. A program takes and returns all parts, laid end to end along the dimension named above; an argument that names none is the same for every part. Nothing has to cross between parts.
Inputs may be any that keep to these rules, and one draw needn't show every extreme that they name: `structure`: each row lists 6 different ancestor blocks in ascending order; the last is always 32 - 1. `diag_inv`: each matrix is lower triangular with its diagonal between 0.5 and 2.
All inputs are finite; a program needn't handle non-finite values.
Results may differ from the reference program's by a relative error of at most 0.000094.
Values sent between devices are 32-bit elements; how exact they have to be, the bound alone decides.
No kernel may reach another device: no remote copies, remote signals or barrier semaphores. Data moves between devices by JAX's collectives and lax.ppermute only.
A program may use at most 320 MiB of HBM per device.

```python
import jax
import jax.numpy as jnp
from jax import lax

W = 256
NB = 6
NA = 32
NS = 16


def draw_structure(key, part):
    key = jax.random.fold_in(key, 11)
    node_keys = jax.random.split(key, NS)
    shuffled = jax.vmap(lambda subkey: jax.random.permutation(subkey, NA - 1))(node_keys)
    chosen = jnp.sort(shuffled[:, :NB - 1].astype(jnp.int32), axis=1)
    top_block = jnp.full((NS, 1), NA - 1, jnp.int32)
    return jnp.concatenate([chosen, top_block], axis=1)


def draw_diag_inv(key, part):
    key = jax.random.fold_in(key, 23)
    first_key, second_key = jax.random.split(key)
    row_ids = lax.broadcasted_iota(jnp.int32, (NS, W, W), 1)
    col_ids = lax.broadcasted_iota(jnp.int32, (NS, W, W), 2)
    below = 0.5 * jax.random.normal(first_key, (NS, W, W), jnp.float32) / jnp.sqrt(jnp.float32(W))
    middle = jnp.exp(jax.random.uniform(second_key, (NS, W, W), jnp.float32, jnp.log(0.5), jnp.log(2.0)))
    zeros_all = jnp.zeros((NS, W, W), jnp.float32)
    return jnp.where(row_ids > col_ids, below, jnp.where(row_ids == col_ids, middle, zeros_all)).astype(jnp.float32)


def shard_levels(stream_key, dims, cuts, smallest, largest):
    level = 1.0
    for dim, parts in cuts:
        draws = jax.random.uniform(jax.random.fold_in(jax.random.fold_in(stream_key, 6), dim), (parts,), jnp.float32, smallest / len(cuts), largest / len(cuts))
        level = level * jnp.repeat(jnp.exp(draws), dims[dim] // parts).reshape((-1,) + (1,) * (len(dims) - 1 - dim))
    return level


def noise(own_key, extent, spread, limit, cuts=(), dtype=jnp.bfloat16):
    values = jax.random.normal(own_key, extent, jnp.float32) * spread
    if len(cuts) > 0:
        values = shard_levels(own_key, extent, cuts, -0.22, 0.18) * values
    return jnp.clip(values, min=-limit, max=limit).astype(dtype)


def setup_inputs(seed: int = 0, part: int = 0) -> dict:
    arg_keys = jax.random.split(jax.random.key(seed), 5)
    part_splits = jax.random.split(jax.random.fold_in(arg_keys[4], part), 5)
    return {
        "sigma_anc": noise(part_splits[0], (NA * W, NA * W), (NB * W) ** -0.5, 0.15625, ((0, 4), (1, 4)), jnp.float32),
        "panel": noise(part_splits[1], (NS, NB, W, W), 1.0, 6.0, ((0, 4), (2, 4)), jnp.float32),
        "diag_inv": draw_diag_inv(jax.random.fold_in(jax.random.fold_in(arg_keys[4], part), 71), part),
        "structure": draw_structure(jax.random.fold_in(arg_keys[4], 71), part),
    }


def reference(sigma_anc, panel, diag_inv, structure):
    precise = lax.Precision.HIGHEST
    scaled = jnp.einsum('jqbv,jvw->jqbw', panel, diag_inv, precision=precise)
    ancestor_blocks = sigma_anc.reshape(NA, W, NA, W)

    def one_node(inputs):
        members, factor = inputs
        row_sel = jnp.take(ancestor_blocks, members, axis=0)
        chosen = jnp.take(row_sel, members, axis=2)
        return jnp.einsum('pbqc,qcw->pbw', chosen, factor, precision=precise)

    product = lax.map(one_node, (structure, scaled))
    sigma_diag = jnp.einsum('jkv,jkw->jvw', diag_inv, diag_inv, precision=precise) + jnp.einsum('jqbv,jqbw->jvw', scaled, product, precision=precise)
    return -product, sigma_diag
```

```python
import functools

import jax
import jax.numpy as jnp
from jax import lax
from jax.experimental import pallas as pl
from jax.experimental.pallas import tpu as pltpu
from jax.sharding import PartitionSpec as P

SLOTS = 10
BUFS = 4


def split(value):
    high = value.astype(jnp.bfloat16)
    return high, (value - high.astype(jnp.float32)).astype(jnp.bfloat16)


def triple_dot(left, right):
    left_high, left_low = split(left)
    right_high, right_low = split(right)
    dot = functools.partial(jnp.dot, preferred_element_type=jnp.float32)
    return dot(left_high, right_high) + (dot(left_high, right_low) + dot(left_low, right_high))


def product_kernel(base, slots, rows, nodes, spot, struct, sigma, panel, out, todo, last_of, sbuf, xbuf, obuf, ssem, xsem, osem):
    width = sbuf.shape[1]
    strip = width // rows
    own_rows, own_cols = sigma.shape[0] // width, sigma.shape[1] // width
    homes = out.shape[0]
    per_home = out.shape[1]
    entries = struct.shape[1]
    my_row, my_col = spot[0], spot[1]

    def put(slot):
        return pltpu.make_async_copy(
            obuf.at[slot], out.at[slot // per_home, lax.rem(slot, per_home)], osem.at[slot]
        )

    def enlist(home, slot, node, row_block, count):
        def member(q, found):
            block = struct[node, q]
            hit = block // own_cols == my_col

            @pl.when(hit)
            def _():
                where = count + found
                todo[where, 0] = row_block
                todo[where, 1] = block - my_col * own_cols
                todo[where, 2] = node
                todo[where, 3] = q
                todo[where, 4] = slot
                todo[where, 5] = jnp.where(found == 0, 1, 0)
                todo[where, 6] = 0

            return found + hit.astype(jnp.int32)

        found = lax.fori_loop(0, entries, member, jnp.int32(0))

        @pl.when(found == 0)
        def _():
            obuf[slot] = jnp.zeros(obuf.shape[1:], jnp.float32)
            put(slot).start()

        @pl.when(found > 0)
        def _():
            todo[count + found - 1, 6] = 1

        last_of[slot] = 1
        return count + found

    def clear(slot, carry):
        last_of[slot] = 0
        return carry

    lax.fori_loop(0, homes * per_home, clear, 0)

    def per_home_group(home, count):
        def per_pair(pair, state):
            rank, count = state
            node, p = home * nodes + pair // entries, lax.rem(pair, entries)
            block = struct[node, p]
            mine = block // own_rows == my_row
            moving = mine & (p < entries - 1)
            slot = rank - base
            live = moving & (slot >= 0) & (slot < slots)
            row_block = block - my_row * own_rows
            count = lax.cond(
                live, lambda: enlist(home, home * per_home + slot, node, row_block, count), lambda: count
            )
            if per_home > slots:
                fixed = mine & (p == entries - 1)
                count = lax.cond(
                    fixed,
                    lambda: enlist(home, home * per_home + slots + pair // entries, node, row_block, count),
                    lambda: count,
                )
            return rank + moving.astype(jnp.int32), count

        return lax.fori_loop(0, nodes * entries, per_pair, (jnp.int32(0), count))[1]

    count = lax.fori_loop(0, homes, per_home_group, jnp.int32(0))

    def fetch(item, act):
        buf = lax.rem(item, BUFS)
        top = pl.multiple_of(todo[item, 0] * width, width)
        left = pl.multiple_of(todo[item, 1] * width, width)
        act(pltpu.make_async_copy(sigma.at[pl.ds(top, width), pl.ds(left, width)], sbuf.at[buf], ssem.at[buf]))
        node, q = todo[item, 2], todo[item, 3]
        for row in range(rows):
            act(
                pltpu.make_async_copy(
                    panel.at[row * homes + node // nodes, lax.rem(node, nodes), q],
                    xbuf.at[buf, pl.ds(row * strip, strip)],
                    xsem.at[buf, row],
                )
            )

    for ahead in range(BUFS - 1):
        @pl.when(ahead < count)
        def _():
            fetch(jnp.int32(ahead), lambda copy: copy.start())

    def step(item, carry):
        buf = lax.rem(item, BUFS)

        @pl.when(item + BUFS - 1 < count)
        def _():
            fetch(item + BUFS - 1, lambda copy: copy.start())

        fetch(item, lambda copy: copy.wait())
        slot = todo[item, 4]
        term = triple_dot(sbuf[buf], xbuf[buf])

        @pl.when(todo[item, 5] == 1)
        def _():
            obuf[slot] = term

        @pl.when(todo[item, 5] == 0)
        def _():
            obuf[slot] += term

        @pl.when(todo[item, 6] == 1)
        def _():
            put(slot).start()

        return carry

    lax.fori_loop(0, count, step, 0)

    def drain(slot, carry):
        @pl.when(last_of[slot] == 1)
        def _():
            put(slot).wait()

        return carry

    lax.fori_loop(0, homes * per_home, drain, 0)


def local_product(spot, struct, sigma, panel, homes, rows, base, slots, fixed):
    nodes, entries, width = panel.shape[1], panel.shape[2], panel.shape[4]
    per_home = slots + fixed
    total = homes * per_home
    longest = total * entries + BUFS
    return pl.pallas_call(
        functools.partial(product_kernel, base, slots, rows, nodes),
        out_shape=jax.ShapeDtypeStruct((homes, per_home, width, width), jnp.float32),
        in_specs=[
            pl.BlockSpec(memory_space=pltpu.SMEM),
            pl.BlockSpec(memory_space=pltpu.SMEM),
            pl.BlockSpec(memory_space=pl.ANY),
            pl.BlockSpec(memory_space=pl.ANY),
        ],
        out_specs=pl.BlockSpec(memory_space=pl.ANY),
        scratch_shapes=[
            pltpu.SMEM((longest, 7), jnp.int32),
            pltpu.SMEM((total,), jnp.int32),
            pltpu.VMEM((BUFS, width, width), jnp.float32),
            pltpu.VMEM((BUFS, width, width), jnp.float32),
            pltpu.VMEM((total, width, width), jnp.float32),
            pltpu.SemaphoreType.DMA((BUFS,)),
            pltpu.SemaphoreType.DMA((BUFS, rows)),
            pltpu.SemaphoreType.DMA((total,)),
        ],
        compiler_params=pltpu.CompilerParams(vmem_limit_bytes=48 * 1024 * 1024),
        cost_estimate=pl.CostEstimate(
            flops=6 * 40 * width**3, bytes_accessed=80 * 4 * width * width, transcendentals=0
        ),
    )(spot, struct, sigma, panel)


def per_device(rows, homes, sigma_anc, panel, diag_inv, structure):
    precise = lax.Precision.HIGH
    nodes, entries, strip, width = panel.shape
    own_rows = sigma_anc.shape[0] // width
    struct = lax.all_gather(structure, "col", axis=0, tiled=True)
    every_panel = lax.all_gather(panel, ("row", "col"), axis=0, tiled=False)
    whole_inverse = lax.all_gather(diag_inv, "row", axis=1, tiled=True)

    my_row = lax.axis_index("row").astype(jnp.int32)
    my_col = lax.axis_index("col").astype(jnp.int32)
    spot = jnp.stack([my_row, my_col])

    most = nodes * min(entries - 1, own_rows)
    slots = min(SLOTS, most)

    holders = struct[:, : entries - 1].reshape(homes, -1) // own_rows
    loads = jnp.sum(holders[:, :, None] == jnp.arange(rows, dtype=jnp.int32), axis=1)
    heaviest = jnp.max(loads)

    holder = structure.reshape(-1) // own_rows
    pair = jnp.arange(nodes * entries, dtype=jnp.int32)
    moving = pair % entries < entries - 1
    earlier = (holder[:, None] == holder[None, :]) & moving[None, :] & (pair[None, :] < pair[:, None])
    rank = jnp.sum(earlier.astype(jnp.int32), axis=1)

    def one_round(base, fixed):
        partial = local_product(spot, struct, sigma_anc, every_panel, homes, rows, base, slots, fixed)
        per_home = slots + fixed
        whole = lax.psum_scatter(partial, "col", scatter_dimension=0, tiled=False)
        strips = whole.reshape(per_home, rows, strip, width).transpose(1, 0, 2, 3)
        return lax.all_to_all(strips, "row", split_axis=0, concat_axis=0, tiled=True)

    first = one_round(0, nodes)
    source = holder * (slots + nodes) + jnp.where(moving, jnp.minimum(rank, slots - 1), slots + pair // entries)
    raw = jnp.take(first.reshape(-1, strip, width), source, axis=0)

    for base in range(slots, most, slots):
        def more(raw, base=base):
            arrived = one_round(base, 0).reshape(-1, strip, width)
            inside = moving & (rank >= base) & (rank < base + slots)
            source = holder * slots + jnp.clip(rank - base, 0, slots - 1)
            return jnp.where(inside[:, None, None], jnp.take(arrived, source, axis=0), raw)

        raw = lax.cond(heaviest > base, more, lambda raw: raw, raw)

    raw = raw.reshape(nodes, entries, strip, width)
    scaled = jnp.einsum("jqbv,jvw->jqbw", panel, whole_inverse, precision=precise)
    product = jnp.einsum("jqbv,jvw->jqbw", raw, whole_inverse, precision=precise)
    terms = jnp.einsum("jkv,jkw->jvw", diag_inv, diag_inv, precision=precise) + jnp.einsum(
        "jqbv,jqbw->jvw", scaled, product, precision=precise
    )
    sigma_diag = lax.psum_scatter(terms, "row", scatter_dimension=1, tiled=True)
    return -product, sigma_diag


def solution(mesh):
    placed = (
        P(("grp", "row"), "col"),
        P(("grp", "col"), None, "row", None),
        P(("grp", "col"), "row", None),
        P("col", None),
    )
    return jax.shard_map(
        functools.partial(per_device, mesh.shape["row"], mesh.shape["col"]),
        mesh=mesh,
        in_specs=placed,
        out_specs=(P(("grp", "col"), None, "row", None), P(("grp", "col"), "row", None)),
        check_vma=False,
    )
```

```python
import functools

import jax
import jax.numpy as jnp
from jax import lax
from jax.experimental import pallas as pl
from jax.experimental.pallas import tpu as pltpu
from jax.sharding import PartitionSpec as P

SLOTS = 13
PIECES = 2
BANDS = 2
BUFS = 4


def split(value):
    high = value.astype(jnp.bfloat16)
    return high, (value - high.astype(jnp.float32)).astype(jnp.bfloat16)


def triple_dot(left, right):
    left_high, left_low = split(left)
    right_high, right_low = split(right)
    dot = functools.partial(jnp.dot, preferred_element_type=jnp.float32)
    wide = right.shape[1]
    if wide > 128:
        return dot(left_high, right_high) + (dot(left_high, right_low) + dot(left_low, right_high))
    both = dot(left_high, jnp.concatenate([right_high, right_low], axis=1))
    return both[:, :wide] + (both[:, wide:] + dot(left_low, right_high))


def product_kernel(base, sizes, rows, nodes, spot, struct, sigma, panel, *refs):
    pieces = len(sizes)
    chips = len(refs[:-8]) // (2 * pieces)
    outs = refs[: 2 * chips * pieces]
    todo, live, sbuf, xbuf, obuf, ssem, xsem, osem = refs[2 * chips * pieces :]
    width = sbuf.shape[1]
    strip = width // rows
    own_rows, own_cols = sigma.shape[0] // width, sigma.shape[1] // width
    slots = sum(sizes)
    entries = struct.shape[1]
    homes = 2 * chips
    my_row, my_col = spot[0], spot[1]
    spans = []
    for group in range(homes):
        start = 0
        for piece in range(pieces):
            spans.append((group * slots + start, sizes[piece]))
            start += sizes[piece]

    def put(slot, act):
        for out, (first, size) in zip(outs, spans):
            @pl.when((slot >= first) & (slot < first + size))
            def _():
                act(pltpu.make_async_copy(obuf.at[slot], out.at[slot - first], osem.at[slot]))

    def enlist(slot, node, row_block, count):
        def member(q, found):
            block = struct[node, q]
            hit = block // own_cols == my_col

            @pl.when(hit)
            def _():
                where = count + found
                todo[where, 0] = row_block
                todo[where, 1] = block - my_col * own_cols
                todo[where, 2] = node
                todo[where, 3] = q
                todo[where, 4] = slot
                todo[where, 5] = jnp.where(found == 0, 1, 0)
                todo[where, 6] = 0

            return found + hit.astype(jnp.int32)

        found = lax.fori_loop(0, entries, member, jnp.int32(0))

        @pl.when(found == 0)
        def _():
            obuf[slot] = jnp.zeros(obuf.shape[1:], jnp.float32)
            put(slot, lambda copy: copy.start())

        @pl.when(found > 0)
        def _():
            todo[count + found - 1, 6] = 1

        live[slot] = 1
        return count + found

    def clear(slot, carry):
        live[slot] = 0
        return carry

    lax.fori_loop(0, homes * slots, clear, 0)

    def per_home(home, count):
        distance = lax.rem(home // 2 - my_col // 2 + chips, chips)
        side = lax.rem(home + my_col, 2)
        group = distance * 2 + side

        def per_pair(pair, state):
            rank, count = state
            node, p = home * nodes + pair // entries, lax.rem(pair, entries)
            block = struct[node, p]
            mine = block // own_rows == my_row
            slot = rank - base
            taken = mine & (slot >= 0) & (slot < slots)
            count = lax.cond(
                taken,
                lambda: enlist(group * slots + slot, node, block - my_row * own_rows, count),
                lambda: count,
            )
            return rank + mine.astype(jnp.int32), count

        return lax.fori_loop(0, nodes * entries, per_pair, (jnp.int32(0), count))[1]

    count = lax.fori_loop(0, homes, per_home, jnp.int32(0))

    def fetch(item, act):
        buf = lax.rem(item, BUFS)
        top = pl.multiple_of(todo[item, 0] * width, width)
        left = pl.multiple_of(todo[item, 1] * width, width)
        act(pltpu.make_async_copy(sigma.at[pl.ds(top, width), pl.ds(left, width)], sbuf.at[buf], ssem.at[buf]))
        node, q = todo[item, 2], todo[item, 3]
        for row in range(rows):
            act(
                pltpu.make_async_copy(
                    panel.at[row * homes + node // nodes, lax.rem(node, nodes), q],
                    xbuf.at[buf, pl.ds(row * strip, strip)],
                    xsem.at[buf, row],
                )
            )

    for ahead in range(BUFS - 1):
        @pl.when(ahead < count)
        def _():
            fetch(jnp.int32(ahead), lambda copy: copy.start())

    def step(item, carry):
        buf = lax.rem(item, BUFS)

        @pl.when(item + BUFS - 1 < count)
        def _():
            fetch(item + BUFS - 1, lambda copy: copy.start())

        fetch(item, lambda copy: copy.wait())
        slot = todo[item, 4]
        term = triple_dot(sbuf[buf], xbuf[buf])

        @pl.when(todo[item, 5] == 1)
        def _():
            obuf[slot] = term

        @pl.when(todo[item, 5] == 0)
        def _():
            obuf[slot] += term

        @pl.when(todo[item, 6] == 1)
        def _():
            put(slot, lambda copy: copy.start())

        return carry

    lax.fori_loop(0, count, step, 0)

    def drain(slot, carry):
        @pl.when(live[slot] == 1)
        def _():
            put(slot, lambda copy: copy.wait())

        return carry

    lax.fori_loop(0, homes * slots, drain, 0)


def local_product(spot, struct, sigma, panel, homes, rows, base, sizes):
    nodes, entries, strip, band = panel.shape[1:]
    width = strip * rows
    total = homes * sum(sizes)
    shapes = [jax.ShapeDtypeStruct((size, width, band), jnp.float32) for _ in range(homes) for size in sizes]
    hbm = pl.BlockSpec(memory_space=pl.ANY)
    smem = pl.BlockSpec(memory_space=pltpu.SMEM)
    return pl.pallas_call(
        functools.partial(product_kernel, base, sizes, rows, nodes),
        out_shape=shapes,
        in_specs=[smem, smem, hbm, hbm],
        out_specs=[hbm] * len(shapes),
        scratch_shapes=[
            pltpu.SMEM((total * entries + BUFS, 7), jnp.int32),
            pltpu.SMEM((total,), jnp.int32),
            pltpu.VMEM((BUFS, width, width), jnp.float32),
            pltpu.VMEM((BUFS, width, band), jnp.float32),
            pltpu.VMEM((total, width, band), jnp.float32),
            pltpu.SemaphoreType.DMA((BUFS,)),
            pltpu.SemaphoreType.DMA((BUFS, rows)),
            pltpu.SemaphoreType.DMA((total,)),
        ],
        compiler_params=pltpu.CompilerParams(vmem_limit_bytes=40 * 1024 * 1024),
        cost_estimate=pl.CostEstimate(
            flops=6 * 400 * width * width * band, bytes_accessed=400 * 4 * width * width, transcendentals=0
        ),
    )(spot, struct, sigma, panel)


def per_device(rows, homes, sigma_anc, panel, diag_inv, structure):
    precise = lax.Precision.HIGH
    nodes, entries, strip, width = panel.shape
    own_rows = sigma_anc.shape[0] // width
    chips = homes // 2
    band = width // BANDS

    struct = lax.all_gather(structure, "col", axis=0, tiled=True)
    panels = [
        lax.all_gather(panel[..., part * band : (part + 1) * band], ("row", "col"), axis=0, tiled=False)
        for part in range(BANDS)
    ]
    whole_inverse = lax.all_gather(diag_inv, "row", axis=1, tiled=True)

    my_row = lax.axis_index("row").astype(jnp.int32)
    my_col = lax.axis_index("col").astype(jnp.int32)
    spot = jnp.stack([my_row, my_col])

    most = nodes * min(entries, own_rows)
    slots = min(SLOTS, most)
    each = -(-slots // PIECES)
    sizes = [min(each, slots - first) for first in range(0, slots, each)]

    holders = struct.reshape(homes, -1) // own_rows
    loads = jnp.sum(holders[:, :, None] == jnp.arange(rows, dtype=jnp.int32), axis=1)
    heaviest = jnp.max(loads)

    holder = structure.reshape(-1) // own_rows
    pair = jnp.arange(nodes * entries, dtype=jnp.int32)
    earlier = (holder[:, None] == holder[None, :]) & (pair[None, :] < pair[:, None])
    rank = jnp.sum(earlier.astype(jnp.int32), axis=1)

    across = [(col, col ^ 1) for col in range(homes)]

    def one_round(base, into):
        found = []
        for part in range(BANDS):
            blocks = local_product(spot, struct, sigma_anc, panels[part], homes, rows, base, sizes)
            raw = into[part]
            for piece, size in enumerate(sizes):
                kept = [blocks[(2 * away) * len(sizes) + piece] for away in range(chips)]
                given = [blocks[(2 * away + 1) * len(sizes) + piece] for away in range(chips)]
                total = None
                for away in list(range(1, chips)) + [0]:
                    summed = kept[away] + lax.ppermute(given[away], "col", across)
                    if away:
                        summed = lax.ppermute(
                            summed, "col", [(col, (col + 2 * away) % homes) for col in range(homes)]
                        )
                    total = summed if total is None else total + summed
                strips = total.reshape(size, rows, strip, band).transpose(1, 0, 2, 3)
                arrived = lax.all_to_all(strips, "row", split_axis=0, concat_axis=0, tiled=True)
                first = base + sum(sizes[:piece])
                inside = (rank >= first) & (rank < first + size)
                source = holder * size + jnp.clip(rank - first, 0, size - 1)
                taken = jnp.take(arrived.reshape(rows * size, strip, band), source, axis=0)
                raw = taken if raw is None else jnp.where(inside[:, None, None], taken, raw)
            found.append(raw)
        return found

    raw = one_round(0, [None] * BANDS)
    for base in range(slots, most, slots):
        raw = lax.cond(heaviest > base, functools.partial(one_round, base), lambda raw: raw, raw)

    scaled = jnp.einsum("jqbv,jvw->jqbw", panel, whole_inverse, precision=precise)
    product = 0.0
    for part in range(BANDS):
        product = product + jnp.einsum(
            "jqbv,jvw->jqbw",
            raw[part].reshape(nodes, entries, strip, band),
            whole_inverse[:, part * band : (part + 1) * band],
            precision=precise,
        )
    terms = jnp.einsum("jkv,jkw->jvw", diag_inv, diag_inv, precision=precise) + jnp.einsum(
        "jqbv,jqbw->jvw", scaled, product, precision=precise
    )
    sigma_diag = lax.psum_scatter(terms, "row", scatter_dimension=1, tiled=True)
    return -product, sigma_diag


def solution(mesh):
    placed = (
        P(("grp", "row"), "col"),
        P(("grp", "col"), None, "row", None),
        P(("grp", "col"), "row", None),
        P("col", None),
    )
    return jax.shard_map(
        functools.partial(per_device, mesh.shape["row"], mesh.shape["col"]),
        mesh=mesh,
        in_specs=placed,
        out_specs=(P(("grp", "col"), None, "row", None), P(("grp", "col"), "row", None)),
        check_vma=False,
    )
```

```python
import functools

import jax
import jax.numpy as jnp
from jax import lax
from jax.experimental import pallas as pl
from jax.experimental.pallas import tpu as pltpu
from jax.sharding import PartitionSpec as P

PIECES = (2, 3, 4, 4)
EXTRA = (4, 7)
BUFS = 4
FIELDS = 7
MIB = 1024 * 1024


def split(value):
    high = value.astype(jnp.bfloat16)
    return high, (value - high.astype(jnp.float32)).astype(jnp.bfloat16)


def triple_dot(left, right):
    left_high, left_low = split(left)
    right_high, right_low = split(right)
    dot = functools.partial(jnp.dot, preferred_element_type=jnp.float32)
    return dot(left_high, right_high) + (dot(left_high, right_low) + dot(left_low, right_high))


def plan_kernel(spans, nodes, own_rows, own_cols, spot, struct, todo, ends, empty, empties):
    entries = struct.shape[1]
    homes = struct.shape[0] // nodes
    chips = homes // 2
    my_row, my_col = spot[0], spot[1]

    def piece_list(piece, first, size, count, none):
        def per_home(home, state):
            distance = lax.rem(home // 2 - my_col // 2 + chips, chips)
            group = distance * 2 + lax.rem(home + my_col, 2)

            def per_pair(pair, state):
                rank, count, none = state
                node, p = home * nodes + pair // entries, lax.rem(pair, entries)
                block = struct[node, p]
                mine = block // own_rows == my_row
                slot = rank - first

                def enlist():
                    where = group * size + slot

                    def member(q, found):
                        other = struct[node, q]
                        hit = other // own_cols == my_col

                        @pl.when(hit)
                        def _():
                            at = (count + found) * FIELDS
                            todo[at] = block - my_row * own_rows
                            todo[at + 1] = other - my_col * own_cols
                            todo[at + 2] = node
                            todo[at + 3] = q
                            todo[at + 4] = where
                            todo[at + 5] = jnp.where(found == 0, 1, 0)
                            todo[at + 6] = 0

                        return found + hit.astype(jnp.int32)

                    found = lax.fori_loop(0, entries, member, jnp.int32(0))

                    @pl.when(found == 0)
                    def _():
                        empty[none] = where

                    @pl.when(found > 0)
                    def _():
                        todo[(count + found - 1) * FIELDS + 6] = 1

                    return count + found, none + jnp.where(found == 0, 1, 0)

                count, none = lax.cond(mine & (slot >= 0) & (slot < size), enlist, lambda: (count, none))
                return rank + mine.astype(jnp.int32), count, none

            return lax.fori_loop(0, nodes * entries, per_pair, (jnp.int32(0),) + state)[1:]

        return lax.fori_loop(0, homes, per_home, (count, none))

    count = none = jnp.int32(0)
    for piece, (first, size) in enumerate(spans):
        count, none = piece_list(piece, first, size, count, none)
        ends[piece] = count
        empties[piece] = none


def make_plan(spot, struct, spans, nodes, own_rows, own_cols):
    total = struct.shape[0] // nodes * sum(size for _, size in spans)
    smem = pl.BlockSpec(memory_space=pltpu.SMEM)
    lengths = (total * struct.shape[1] * FIELDS, len(spans), total, len(spans))
    return pl.pallas_call(
        functools.partial(plan_kernel, spans, nodes, own_rows, own_cols),
        out_shape=[jax.ShapeDtypeStruct((length,), jnp.int32) for length in lengths],
        in_specs=[smem, smem],
        out_specs=[smem] * 4,
    )(spot, struct)


def product_kernel(piece, rows, nodes, homes, todo, ends, empty, empties, sigma, panel, *refs):
    outs = refs[:homes]
    sbuf, xbuf, obuf, ssem, xsem, osem = refs[homes:]
    width = sbuf.shape[1]
    strip = width // rows
    size = outs[0].shape[0]
    begin = ends[piece - 1] if piece else 0
    end = ends[piece]
    none_begin = empties[piece - 1] if piece else 0
    none_end = empties[piece]

    def put(slot):
        for group, out in enumerate(outs):
            @pl.when(slot // size == group)
            def _():
                pltpu.make_async_copy(obuf.at[slot], out.at[slot - group * size], osem.at[slot]).start()

    def settle(slot):
        pltpu.make_async_copy(obuf.at[slot], outs[0].at[0], osem.at[slot]).wait()

    def fetch(item, act):
        buf = lax.rem(item, BUFS)
        at = item * FIELDS
        top = pl.multiple_of(todo[at] * width, width)
        left = pl.multiple_of(todo[at + 1] * width, width)
        act(pltpu.make_async_copy(sigma.at[pl.ds(top, width), pl.ds(left, width)], sbuf.at[buf], ssem.at[buf]))
        node, q = todo[at + 2], todo[at + 3]
        for row in range(rows):
            act(
                pltpu.make_async_copy(
                    panel.at[row * homes + node // nodes, lax.rem(node, nodes), q],
                    xbuf.at[buf, pl.ds(row * strip, strip)],
                    xsem.at[buf, row],
                )
            )

    for ahead in range(BUFS - 1):
        @pl.when(begin + ahead < end)
        def _():
            fetch(begin + ahead, lambda copy: copy.start())

    def blank(item, carry):
        slot = empty[item]
        obuf[slot] = jnp.zeros(obuf.shape[1:], jnp.float32)
        put(slot)
        return carry

    lax.fori_loop(none_begin, none_end, blank, 0)

    def step(item, carry):
        buf = lax.rem(item, BUFS)

        @pl.when(item + BUFS - 1 < end)
        def _():
            fetch(item + BUFS - 1, lambda copy: copy.start())

        fetch(item, lambda copy: copy.wait())
        at = item * FIELDS
        slot = todo[at + 4]
        term = triple_dot(sbuf[buf], xbuf[buf])

        @pl.when(todo[at + 5] == 1)
        def _():
            obuf[slot] = term

        @pl.when(todo[at + 5] == 0)
        def _():
            obuf[slot] += term

        @pl.when(todo[at + 6] == 1)
        def _():
            put(slot)

        return carry

    lax.fori_loop(begin, end, step, 0)

    def drain(item, carry):
        @pl.when(todo[item * FIELDS + 6] == 1)
        def _():
            settle(todo[item * FIELDS + 4])

        return carry

    lax.fori_loop(begin, end, drain, 0)

    def drain_blank(item, carry):
        settle(empty[item])
        return carry

    lax.fori_loop(none_begin, none_end, drain_blank, 0)


def local_product(plan, sigma, panel, homes, rows, piece, size):
    nodes, _, strip, width = panel.shape[1:]
    total = homes * size
    hbm = pl.BlockSpec(memory_space=pl.ANY)
    smem = pl.BlockSpec(memory_space=pltpu.SMEM)
    return pl.pallas_call(
        functools.partial(product_kernel, piece, rows, nodes, homes),
        out_shape=[jax.ShapeDtypeStruct((size, width, width), jnp.float32)] * homes,
        in_specs=[smem] * 4 + [hbm, hbm],
        out_specs=[hbm] * homes,
        scratch_shapes=[
            pltpu.VMEM((BUFS, width, width), jnp.float32),
            pltpu.VMEM((BUFS, width, width), jnp.float32),
            pltpu.VMEM((total, width, width), jnp.float32),
            pltpu.SemaphoreType.DMA((BUFS,)),
            pltpu.SemaphoreType.DMA((BUFS, rows)),
            pltpu.SemaphoreType.DMA((total,)),
        ],
        compiler_params=pltpu.CompilerParams(vmem_limit_bytes=50 * MIB),
        cost_estimate=pl.CostEstimate(
            flops=2 * 60 * size * width**3, bytes_accessed=60 * size * width * width, transcendentals=0
        ),
    )(*plan, sigma, panel)


def finish_kernel(count, which, where, panel, whole, own, *refs):
    arrived, (off, terms, raw) = refs[:count], refs[count:]
    nodes, entries, strip, width = panel.shape
    for node in range(nodes):
        def pick(entry, carry):
            at = node * entries + entry
            for piece, blocks in enumerate(arrived):
                @pl.when(which[at] == piece)
                def _():
                    raw[pl.ds(pl.multiple_of(entry * strip, strip), strip), :] = blocks[where[at]]

            return carry

        lax.fori_loop(0, entries, pick, 0)
        inverse = whole[node]
        product = triple_dot(raw[...], inverse)
        scaled = triple_dot(panel[node].reshape(entries * strip, width), inverse)
        off[node] = -product.reshape(entries, strip, width)
        mine = own[node]
        terms[node] = triple_dot(scaled.T, product) + triple_dot(mine.T, mine)


def finish(which, where, panel, whole, own, arrived):
    nodes, entries, strip, width = panel.shape
    vmem = pl.BlockSpec(memory_space=pltpu.VMEM)
    smem = pl.BlockSpec(memory_space=pltpu.SMEM)
    return pl.pallas_call(
        functools.partial(finish_kernel, len(arrived)),
        out_shape=[
            jax.ShapeDtypeStruct(panel.shape, jnp.float32),
            jax.ShapeDtypeStruct(whole.shape, jnp.float32),
        ],
        in_specs=[smem, smem] + [vmem] * (3 + len(arrived)),
        out_specs=[vmem, vmem],
        scratch_shapes=[pltpu.VMEM((entries * strip, width), jnp.float32)],
        compiler_params=pltpu.CompilerParams(vmem_limit_bytes=40 * MIB),
        cost_estimate=pl.CostEstimate(
            flops=6 * nodes * 3 * entries * strip * width * width, bytes_accessed=16 * MIB, transcendentals=0
        ),
    )(which, where, panel, whole, own, *arrived)


def per_device(rows, homes, sigma_anc, panel, diag_inv, structure):
    nodes, entries, strip, width = panel.shape
    own_rows, own_cols = sigma_anc.shape[0] // width, sigma_anc.shape[1] // width
    chips = homes // 2

    struct = lax.all_gather(structure, "col", axis=0, tiled=True)
    every_panel = lax.all_gather(panel, ("row", "col"), axis=0, tiled=False)
    own_inverse, every_panel = lax.optimization_barrier((diag_inv, every_panel))
    whole_inverse = lax.all_gather(own_inverse, "row", axis=1, tiled=True)

    my_row = lax.axis_index("row").astype(jnp.int32)
    my_col = lax.axis_index("col").astype(jnp.int32)
    spot = jnp.stack([my_row, my_col])

    most = nodes * min(entries, own_rows)
    rounds, spans, reach = [], [], 0
    for sizes in (PIECES,) + tuple((size,) for size in EXTRA):
        held = []
        for size in sizes:
            size = min(size, most - reach)
            if size > 0:
                held.append(len(spans))
                spans.append((reach, size))
                reach += size
        if held:
            rounds.append(held)
    if reach < most:
        rounds.append([len(spans)])
        spans.append((reach, most - reach))
    plan = make_plan(spot, struct, tuple(spans), nodes, own_rows, own_cols)

    holders = struct.reshape(homes, -1) // own_rows
    loads = jnp.sum(holders[:, :, None] == jnp.arange(rows, dtype=jnp.int32), axis=1)
    heaviest = jnp.max(loads)

    holder = structure.reshape(-1) // own_rows
    pair = jnp.arange(nodes * entries, dtype=jnp.int32)
    earlier = (holder[:, None] == holder[None, :]) & (pair[None, :] < pair[:, None])
    rank = jnp.sum(earlier.astype(jnp.int32), axis=1)
    which = jnp.zeros_like(rank)
    where = holder * spans[0][1] + rank
    for piece, (first, size) in enumerate(spans[1:], 1):
        which = jnp.where(rank >= first, piece, which)
        where = jnp.where(rank >= first, holder * size + rank - first, where)

    sibling = [(col, col ^ 1) for col in range(homes)]

    def exchange(pieces, inverse):
        arrived = []
        lists = plan
        for turn, piece in enumerate(pieces):
            size = spans[piece][1]
            blocks = local_product(lists, sigma_anc, every_panel, homes, rows, piece, size)
            total = None
            for away in list(range(1, chips)) + [0]:
                summed = blocks[2 * away] + lax.ppermute(blocks[2 * away + 1], "col", sibling)
                if away:
                    first, summed = lax.optimization_barrier((lists[0], summed))
                    lists = [first] + list(lists[1:])
                    summed = lax.ppermute(summed, "col", [(col, (col + 2 * away) % homes) for col in range(homes)])
                total = summed if total is None else total + summed
            if turn == 1:
                total, inverse = lax.optimization_barrier((total, inverse))
            strips = total.reshape(size, rows, strip, width).transpose(1, 0, 2, 3)
            landed = lax.all_to_all(strips, "row", split_axis=0, concat_axis=0, tiled=True)
            arrived.append(landed.reshape(rows * size, strip, width))
        return arrived, inverse

    arrived, whole_inverse = exchange(rounds[0], whole_inverse)

    def ending(extra):
        def branch():
            more = list(arrived)
            for held in rounds[1 : 1 + extra]:
                more += exchange(held, whole_inverse)[0]
            return finish(which, where, panel, whole_inverse, diag_inv, more)

        return branch

    if len(rounds) == 1:
        off, terms = ending(0)()
    else:
        level = sum((heaviest > spans[held[0]][0]).astype(jnp.int32) for held in rounds[1:])
        off, terms = lax.switch(level, [ending(extra) for extra in range(len(rounds))])
    sigma_diag = lax.psum_scatter(terms, "row", scatter_dimension=1, tiled=True)
    return off, sigma_diag


def solution(mesh):
    placed = (
        P(("grp", "row"), "col"),
        P(("grp", "col"), None, "row", None),
        P(("grp", "col"), "row", None),
        P("col", None),
    )
    return jax.shard_map(
        functools.partial(per_device, mesh.shape["row"], mesh.shape["col"]),
        mesh=mesh,
        in_specs=placed,
        out_specs=(P(("grp", "col"), None, "row", None), P(("grp", "col"), "row", None)),
        check_vma=False,
    )
```

```python
import functools

import jax
import jax.numpy as jnp
from jax import lax
from jax.experimental import pallas as pl
from jax.experimental.pallas import tpu as pltpu
from jax.sharding import PartitionSpec as P

PIECES = (3, 4, 4, 2)
EXTRA = (4, 7)
BUFS = 4
FIELDS = 9
MIB = 1024 * 1024


def split(value):
    high = value.astype(jnp.bfloat16)
    return high, (value - high.astype(jnp.float32)).astype(jnp.bfloat16)


def triple_dot(left, right):
    left_high, left_low = split(left)
    right_high, right_low = split(right)
    dot = functools.partial(jnp.dot, preferred_element_type=jnp.float32)
    return dot(left_high, right_high) + (dot(left_high, right_low) + dot(left_low, right_high))


def plan_kernel(spans, nodes, own_rows, own_cols, spot, struct, todo, ends, empty, empties):
    entries = struct.shape[1]
    homes = struct.shape[0] // nodes
    chips = homes // 2
    my_row, my_col = spot[0], spot[1]

    def piece_list(first, size, state):
        def per_home(home, state):
            distance = lax.rem(home // 2 - my_col // 2 + chips, chips)
            group = distance * 2 + lax.rem(home + my_col, 2)

            def per_node(member, state):
                rank, count, blocks, none = state
                node = home * nodes + member
                low = high = rank
                for p in range(entries):
                    mine = (struct[node, p] // own_rows == my_row).astype(jnp.int32)
                    high += mine
                held = high - low
                start = jnp.maximum(low, first)
                stop = jnp.minimum(high, first + size)
                columns = jnp.int32(0)
                for q in range(entries):
                    columns += (struct[node, q] // own_cols == my_col).astype(jnp.int32)

                def enlist():
                    def per_column(q, state):
                        order, count, blocks = state
                        other = struct[node, q]

                        def per_row(p, state):
                            at_rank, count = state
                            block = struct[node, p]
                            mine = block // own_rows == my_row

                            @pl.when(mine & (at_rank >= start) & (at_rank < stop))
                            def _():
                                at = count * FIELDS
                                todo[at] = block - my_row * own_rows
                                todo[at + 1] = other - my_col * own_cols
                                todo[at + 2] = node
                                todo[at + 3] = q
                                todo[at + 4] = group * size + at_rank - first
                                todo[at + 5] = (order == 0).astype(jnp.int32)
                                todo[at + 6] = (order == columns - 1).astype(jnp.int32)
                                todo[at + 7] = (at_rank == start).astype(jnp.int32)
                                todo[at + 8] = blocks

                            taken = mine & (at_rank >= start) & (at_rank < stop)
                            return at_rank + mine.astype(jnp.int32), count + taken.astype(jnp.int32)

                        def column():
                            return lax.fori_loop(0, entries, per_row, (low, count))[1]

                        hit = other // own_cols == my_col
                        count = lax.cond(hit, column, lambda: count)
                        step = hit.astype(jnp.int32)
                        return order + step, count, blocks + step

                    def all_empty():
                        def one(at_rank, none):
                            empty[none] = group * size + at_rank - first
                            return none + 1

                        return lax.fori_loop(start, stop, one, none)

                    _, more, further = lax.fori_loop(0, entries, per_column, (jnp.int32(0), count, blocks))
                    return more, further, lax.cond(columns == 0, all_empty, lambda: none)

                count, blocks, none = lax.cond(start < stop, enlist, lambda: (count, blocks, none))
                return high, count, blocks, none

            return lax.fori_loop(0, nodes, per_node, (jnp.int32(0),) + state)[1:]

        return lax.fori_loop(0, homes, per_home, state)

    count = none = jnp.int32(0)
    for piece, (first, size) in enumerate(spans):
        count, _, none = piece_list(first, size, (count, jnp.int32(0), none))
        ends[piece] = count
        empties[piece] = none


def make_plan(spot, struct, spans, nodes, own_rows, own_cols):
    total = struct.shape[0] // nodes * sum(size for _, size in spans)
    smem = pl.BlockSpec(memory_space=pltpu.SMEM)
    lengths = (total * struct.shape[1] * FIELDS, len(spans), total, len(spans))
    return pl.pallas_call(
        functools.partial(plan_kernel, spans, nodes, own_rows, own_cols),
        out_shape=[jax.ShapeDtypeStruct((length,), jnp.int32) for length in lengths],
        in_specs=[smem, smem],
        out_specs=[smem] * 4,
    )(spot, struct)


def product_kernel(piece, rows, nodes, homes, todo, ends, empty, empties, sigma, panel, *refs):
    outs = refs[:homes]
    sbuf, xbuf, deep, obuf, ssem, xsem, osem = refs[homes:]
    width = sbuf.shape[1]
    strip = width // rows
    size = outs[0].shape[0]
    begin = ends[piece - 1] if piece else 0
    end = ends[piece]
    none_begin = empties[piece - 1] if piece else 0
    none_end = empties[piece]

    def put(slot):
        for group, out in enumerate(outs):
            @pl.when(slot // size == group)
            def _():
                pltpu.make_async_copy(obuf.at[slot], out.at[slot - group * size], osem.at[slot]).start()

    def settle(slot):
        pltpu.make_async_copy(obuf.at[slot], outs[0].at[0], osem.at[slot]).wait()

    def fetch(item, act):
        buf = lax.rem(item, BUFS)
        at = item * FIELDS
        top = pl.multiple_of(todo[at] * width, width)
        left = pl.multiple_of(todo[at + 1] * width, width)
        act(pltpu.make_async_copy(sigma.at[pl.ds(top, width), pl.ds(left, width)], sbuf.at[buf], ssem.at[buf]))

        @pl.when(todo[at + 7] == 1)
        def _():
            node, q = todo[at + 2], todo[at + 3]
            xslot = lax.rem(todo[at + 8], BUFS)
            for row in range(rows):
                act(
                    pltpu.make_async_copy(
                        panel.at[row * homes + node // nodes, lax.rem(node, nodes), q],
                        xbuf.at[xslot, pl.ds(row * strip, strip)],
                        xsem.at[xslot, row],
                    )
                )

    for ahead in range(BUFS - 1):
        @pl.when(begin + ahead < end)
        def _():
            fetch(begin + ahead, lambda copy: copy.start())

    def blank(item, carry):
        slot = empty[item]
        obuf[slot] = jnp.zeros(obuf.shape[1:], jnp.float32)
        put(slot)
        return carry

    lax.fori_loop(none_begin, none_end, blank, 0)

    def step(item, carry):
        buf = lax.rem(item, BUFS)

        @pl.when(item + BUFS - 1 < end)
        def _():
            fetch(item + BUFS - 1, lambda copy: copy.start())

        fetch(item, lambda copy: copy.wait())
        at = item * FIELDS
        slot = todo[at + 4]

        @pl.when(todo[at + 7] == 1)
        def _():
            high, low = split(xbuf[lax.rem(todo[at + 8], BUFS)])
            deep[:width] = high
            deep[width : 2 * width] = low
            deep[2 * width :] = high

        high, low = split(sbuf[buf])
        term = jnp.dot(
            jnp.concatenate([high, high, low], axis=1), deep[...], preferred_element_type=jnp.float32
        )

        @pl.when(todo[at + 5] == 1)
        def _():
            obuf[slot] = term

        @pl.when(todo[at + 5] == 0)
        def _():
            obuf[slot] += term

        @pl.when(todo[at + 6] == 1)
        def _():
            put(slot)

        return carry

    lax.fori_loop(begin, end, step, 0)

    def drain(item, carry):
        @pl.when(todo[item * FIELDS + 6] == 1)
        def _():
            settle(todo[item * FIELDS + 4])

        return carry

    lax.fori_loop(begin, end, drain, 0)

    def drain_blank(item, carry):
        settle(empty[item])
        return carry

    lax.fori_loop(none_begin, none_end, drain_blank, 0)


def local_product(plan, sigma, panel, homes, rows, piece, size):
    nodes, _, strip, width = panel.shape[1:]
    total = homes * size
    hbm = pl.BlockSpec(memory_space=pl.ANY)
    smem = pl.BlockSpec(memory_space=pltpu.SMEM)
    return pl.pallas_call(
        functools.partial(product_kernel, piece, rows, nodes, homes),
        out_shape=[jax.ShapeDtypeStruct((size, width, width), jnp.float32)] * homes,
        in_specs=[smem] * 4 + [hbm, hbm],
        out_specs=[hbm] * homes,
        scratch_shapes=[
            pltpu.VMEM((BUFS, width, width), jnp.float32),
            pltpu.VMEM((BUFS, width, width), jnp.float32),
            pltpu.VMEM((3 * width, width), jnp.bfloat16),
            pltpu.VMEM((total, width, width), jnp.float32),
            pltpu.SemaphoreType.DMA((BUFS,)),
            pltpu.SemaphoreType.DMA((BUFS, rows)),
            pltpu.SemaphoreType.DMA((total,)),
        ],
        compiler_params=pltpu.CompilerParams(vmem_limit_bytes=50 * MIB),
        cost_estimate=pl.CostEstimate(flops=width, bytes_accessed=width, transcendentals=0),
    )(*plan, sigma, panel)


def prepare_kernel(panel, whole, own, scaled, gram):
    nodes, entries, strip, width = panel.shape
    for node in range(nodes):
        scaled[node] = triple_dot(panel[node].reshape(entries * strip, width), whole[node])
        mine = own[node]
        gram[node] = triple_dot(mine.T, mine)


def prepare(panel, whole, own):
    nodes, entries, strip, width = panel.shape
    vmem = pl.BlockSpec(memory_space=pltpu.VMEM)
    return pl.pallas_call(
        prepare_kernel,
        out_shape=[
            jax.ShapeDtypeStruct((nodes, entries * strip, width), jnp.float32),
            jax.ShapeDtypeStruct(whole.shape, jnp.float32),
        ],
        in_specs=[vmem] * 3,
        out_specs=[vmem] * 2,
        compiler_params=pltpu.CompilerParams(vmem_limit_bytes=40 * MIB),
        cost_estimate=pl.CostEstimate(flops=6 * nodes * entries * strip * width**2, bytes_accessed=width, transcendentals=0),
    )(panel, whole, own)


def finish_kernel(count, entries, which, where, scaled, gram, whole, *refs):
    arrived, (off, terms, raw) = refs[:count], refs[count:]
    nodes, tall, width = scaled.shape
    strip = tall // entries
    for node in range(nodes):
        def pick(entry, carry):
            at = node * entries + entry
            for piece, blocks in enumerate(arrived):
                @pl.when(which[at] == piece)
                def _():
                    raw[pl.ds(pl.multiple_of(entry * strip, strip), strip), :] = blocks[where[at]]

            return carry

        lax.fori_loop(0, entries, pick, 0)
        product = triple_dot(raw[...], whole[node])
        off[node] = -product.reshape(entries, strip, width)
        terms[node] = gram[node] + triple_dot(scaled[node].T, product)


def finish(which, where, entries, scaled, gram, whole, arrived):
    nodes, tall, width = scaled.shape
    vmem = pl.BlockSpec(memory_space=pltpu.VMEM)
    smem = pl.BlockSpec(memory_space=pltpu.SMEM)
    return pl.pallas_call(
        functools.partial(finish_kernel, len(arrived), entries),
        out_shape=[
            jax.ShapeDtypeStruct((nodes, entries, tall // entries, width), jnp.float32),
            jax.ShapeDtypeStruct(whole.shape, jnp.float32),
        ],
        in_specs=[smem, smem] + [vmem] * (3 + len(arrived)),
        out_specs=[vmem, vmem],
        scratch_shapes=[pltpu.VMEM((tall, width), jnp.float32)],
        compiler_params=pltpu.CompilerParams(vmem_limit_bytes=40 * MIB),
        cost_estimate=pl.CostEstimate(flops=6 * nodes * 2 * tall * width**2, bytes_accessed=8 * MIB, transcendentals=0),
    )(which, where, scaled, gram, whole, *arrived)


def per_device(rows, homes, sigma_anc, panel, diag_inv, structure):
    nodes, entries, strip, width = panel.shape
    own_rows, own_cols = sigma_anc.shape[0] // width, sigma_anc.shape[1] // width
    chips = homes // 2

    struct = lax.all_gather(structure, "col", axis=0, tiled=True)
    every_panel = lax.all_gather(panel, ("row", "col"), axis=0, tiled=False)
    own_inverse, every_panel = lax.optimization_barrier((diag_inv, every_panel))
    whole_inverse = lax.all_gather(own_inverse, "row", axis=1, tiled=True)

    my_row = lax.axis_index("row").astype(jnp.int32)
    my_col = lax.axis_index("col").astype(jnp.int32)
    spot = jnp.stack([my_row, my_col])

    most = nodes * min(entries, own_rows)
    rounds, spans, reach = [], [], 0
    for sizes in (PIECES,) + tuple((size,) for size in EXTRA):
        held = []
        for size in sizes:
            size = min(size, most - reach)
            if size > 0:
                held.append(len(spans))
                spans.append((reach, size))
                reach += size
        if held:
            rounds.append(held)
    if reach < most:
        rounds.append([len(spans)])
        spans.append((reach, most - reach))
    plan = make_plan(spot, struct, tuple(spans), nodes, own_rows, own_cols)

    holders = struct.reshape(homes, -1) // own_rows
    loads = jnp.sum(holders[:, :, None] == jnp.arange(rows, dtype=jnp.int32), axis=1)
    heaviest = jnp.max(loads)

    holder = structure.reshape(-1) // own_rows
    pair = jnp.arange(nodes * entries, dtype=jnp.int32)
    earlier = (holder[:, None] == holder[None, :]) & (pair[None, :] < pair[:, None])
    rank = jnp.sum(earlier.astype(jnp.int32), axis=1)
    which = jnp.zeros_like(rank)
    where = holder * spans[0][1] + rank
    for piece, (first, size) in enumerate(spans[1:], 1):
        which = jnp.where(rank >= first, piece, which)
        where = jnp.where(rank >= first, holder * size + rank - first, where)

    sibling = [(col, col ^ 1) for col in range(homes)]

    def exchange(pieces, inverse):
        arrived = []
        lists = plan
        for turn, piece in enumerate(pieces):
            size = spans[piece][1]
            blocks = local_product(lists, sigma_anc, every_panel, homes, rows, piece, size)
            total = None
            for away in list(range(1, chips)) + [0]:
                summed = blocks[2 * away] + lax.ppermute(blocks[2 * away + 1], "col", sibling)
                if away:
                    first, summed = lax.optimization_barrier((lists[0], summed))
                    lists = [first] + list(lists[1:])
                    summed = lax.ppermute(summed, "col", [(col, (col + 2 * away) % homes) for col in range(homes)])
                total = summed if total is None else total + summed
            if turn == 1:
                total, inverse = lax.optimization_barrier((total, inverse))
            strips = total.reshape(size, rows, strip, width).transpose(1, 0, 2, 3)
            landed = lax.all_to_all(strips, "row", split_axis=0, concat_axis=0, tiled=True)
            arrived.append(landed.reshape(rows * size, strip, width))
        return arrived, inverse

    arrived, whole_inverse = exchange(rounds[0], whole_inverse)
    scaled, gram = prepare(panel, whole_inverse, diag_inv)

    def ending(extra):
        def branch():
            more = list(arrived)
            for held in rounds[1 : 1 + extra]:
                more += exchange(held, whole_inverse)[0]
            return finish(which, where, entries, scaled, gram, whole_inverse, more)

        return branch

    if len(rounds) == 1:
        off, terms = ending(0)()
    else:
        level = sum((heaviest > spans[held[0]][0]).astype(jnp.int32) for held in rounds[1:])
        off, terms = lax.switch(level, [ending(extra) for extra in range(len(rounds))])
    sigma_diag = lax.psum_scatter(terms, "row", scatter_dimension=1, tiled=True)
    return off, sigma_diag


def solution(mesh):
    placed = (
        P(("grp", "row"), "col"),
        P(("grp", "col"), None, "row", None),
        P(("grp", "col"), "row", None),
        P("col", None),
    )
    return jax.shard_map(
        functools.partial(per_device, mesh.shape["row"], mesh.shape["col"]),
        mesh=mesh,
        in_specs=placed,
        out_specs=(P(("grp", "col"), None, "row", None), P(("grp", "col"), "row", None)),
        check_vma=False,
    )
```

```python
import functools

import jax
import jax.numpy as jnp
from jax import lax
from jax.experimental import pallas as pl
from jax.experimental.pallas import tpu as pltpu
from jax.sharding import PartitionSpec as P

PIECES = (3, 4, 4, 2)
EXTRA = (4, 7)
BUFS = 12
FIELDS = 9
MIB = 1024 * 1024


def split(value):
    high = value.astype(jnp.bfloat16)
    return high, (value - high.astype(jnp.float32)).astype(jnp.bfloat16)


def triple_dot(left, right):
    left_high, left_low = split(left)
    right_high, right_low = split(right)
    dot = functools.partial(jnp.dot, preferred_element_type=jnp.float32)
    return dot(left_high, right_high) + (dot(left_high, right_low) + dot(left_low, right_high))


def plan_kernel(spans, nodes, own_rows, own_cols, spot, struct, todo, ends, empty, empties):
    entries = struct.shape[1]
    homes = struct.shape[0] // nodes
    chips = homes // 2
    my_row, my_col = spot[0], spot[1]

    def piece_list(first, size, state):
        def per_home(home, state):
            distance = lax.rem(home // 2 - my_col // 2 + chips, chips)
            group = distance * 2 + lax.rem(home + my_col, 2)

            def per_node(member, state):
                rank, count, blocks, none = state
                node = home * nodes + member
                low = high = rank
                for p in range(entries):
                    mine = (struct[node, p] // own_rows == my_row).astype(jnp.int32)
                    high += mine
                held = high - low
                start = jnp.maximum(low, first)
                stop = jnp.minimum(high, first + size)
                columns = jnp.int32(0)
                for q in range(entries):
                    columns += (struct[node, q] // own_cols == my_col).astype(jnp.int32)

                def enlist():
                    def per_column(q, state):
                        order, count, blocks = state
                        other = struct[node, q]

                        def per_row(p, state):
                            at_rank, count = state
                            block = struct[node, p]
                            mine = block // own_rows == my_row

                            @pl.when(mine & (at_rank >= start) & (at_rank < stop))
                            def _():
                                at = count * FIELDS
                                todo[at] = block - my_row * own_rows
                                todo[at + 1] = other - my_col * own_cols
                                todo[at + 2] = node
                                todo[at + 3] = q
                                todo[at + 4] = group * size + at_rank - first
                                todo[at + 5] = (order == 0).astype(jnp.int32)
                                todo[at + 6] = (order == columns - 1).astype(jnp.int32)
                                todo[at + 7] = (at_rank == start).astype(jnp.int32)
                                todo[at + 8] = blocks

                            taken = mine & (at_rank >= start) & (at_rank < stop)
                            return at_rank + mine.astype(jnp.int32), count + taken.astype(jnp.int32)

                        def column():
                            return lax.fori_loop(0, entries, per_row, (low, count))[1]

                        hit = other // own_cols == my_col
                        count = lax.cond(hit, column, lambda: count)
                        step = hit.astype(jnp.int32)
                        return order + step, count, blocks + step

                    def all_empty():
                        def one(at_rank, none):
                            empty[none] = group * size + at_rank - first
                            return none + 1

                        return lax.fori_loop(start, stop, one, none)

                    _, more, further = lax.fori_loop(0, entries, per_column, (jnp.int32(0), count, blocks))
                    return more, further, lax.cond(columns == 0, all_empty, lambda: none)

                count, blocks, none = lax.cond(start < stop, enlist, lambda: (count, blocks, none))
                return high, count, blocks, none

            return lax.fori_loop(0, nodes, per_node, (jnp.int32(0),) + state)[1:]

        return lax.fori_loop(0, homes, per_home, state)

    count = none = jnp.int32(0)
    for piece, (first, size) in enumerate(spans):
        count, _, none = piece_list(first, size, (count, jnp.int32(0), none))
        ends[piece] = count
        empties[piece] = none


def make_plan(spot, struct, spans, nodes, own_rows, own_cols):
    total = struct.shape[0] // nodes * sum(size for _, size in spans)
    smem = pl.BlockSpec(memory_space=pltpu.SMEM)
    lengths = (total * struct.shape[1] * FIELDS, len(spans), total, len(spans))
    return pl.pallas_call(
        functools.partial(plan_kernel, spans, nodes, own_rows, own_cols),
        out_shape=[jax.ShapeDtypeStruct((length,), jnp.int32) for length in lengths],
        in_specs=[smem, smem],
        out_specs=[smem] * 4,
    )(spot, struct)


def product_kernel(turn, sizes, rows, nodes, homes, todo, ends, empty, empties, sigma, panel, *refs):
    outs = refs[: homes * len(sizes)]
    sbuf, xbuf, deep, obuf, ssem, xsem, osem = refs[homes * len(sizes) :]
    width = sbuf.shape[1]
    strip = width // rows
    slots = sum(sizes)
    begin = ends[turn - 1] if turn else 0
    end = ends[turn]
    none_begin = empties[turn - 1] if turn else 0
    none_end = empties[turn]

    def put(slot):
        group = slot // slots
        inside = slot - group * slots
        first = 0
        for piece, size in enumerate(sizes):
            @pl.when((inside >= first) & (inside < first + size))
            def _(piece=piece, first=first):
                for other in range(homes):
                    @pl.when(group == other)
                    def _():
                        out = outs[piece * homes + other]
                        pltpu.make_async_copy(obuf.at[slot], out.at[inside - first], osem.at[slot]).start()

            first += size

    def settle(slot):
        pltpu.make_async_copy(obuf.at[slot], outs[0].at[0], osem.at[slot]).wait()

    def fetch(item, act):
        buf = lax.rem(item, BUFS)
        at = item * FIELDS
        top = pl.multiple_of(todo[at] * width, width)
        left = pl.multiple_of(todo[at + 1] * width, width)
        act(pltpu.make_async_copy(sigma.at[pl.ds(top, width), pl.ds(left, width)], sbuf.at[buf], ssem.at[buf]))

        @pl.when(todo[at + 7] == 1)
        def _():
            node, q = todo[at + 2], todo[at + 3]
            xslot = lax.rem(todo[at + 8], BUFS)
            for row in range(rows):
                act(
                    pltpu.make_async_copy(
                        panel.at[row * homes + node // nodes, lax.rem(node, nodes), q],
                        xbuf.at[xslot, pl.ds(row * strip, strip)],
                        xsem.at[xslot, row],
                    )
                )

    for ahead in range(BUFS - 1):
        @pl.when(begin + ahead < end)
        def _():
            fetch(begin + ahead, lambda copy: copy.start())

    def blank(item, carry):
        slot = empty[item]
        obuf[slot] = jnp.zeros(obuf.shape[1:], jnp.float32)
        put(slot)
        return carry

    lax.fori_loop(none_begin, none_end, blank, 0)

    def step(item, carry):
        buf = lax.rem(item, BUFS)

        @pl.when(item + BUFS - 1 < end)
        def _():
            fetch(item + BUFS - 1, lambda copy: copy.start())

        fetch(item, lambda copy: copy.wait())
        at = item * FIELDS
        slot = todo[at + 4]

        @pl.when(todo[at + 7] == 1)
        def _():
            high, low = split(xbuf[lax.rem(todo[at + 8], BUFS)])
            deep[:width] = high
            deep[width : 2 * width] = low
            deep[2 * width :] = high

        high, low = split(sbuf[buf])
        term = jnp.dot(
            jnp.concatenate([high, high, low], axis=1), deep[...], preferred_element_type=jnp.float32
        )

        @pl.when(todo[at + 5] == 1)
        def _():
            obuf[slot] = term

        @pl.when(todo[at + 5] == 0)
        def _():
            obuf[slot] += term

        @pl.when(todo[at + 6] == 1)
        def _():
            put(slot)

        return carry

    lax.fori_loop(begin, end, step, 0)

    def drain(item, carry):
        @pl.when(todo[item * FIELDS + 6] == 1)
        def _():
            settle(todo[item * FIELDS + 4])

        return carry

    lax.fori_loop(begin, end, drain, 0)

    def drain_blank(item, carry):
        settle(empty[item])
        return carry

    lax.fori_loop(none_begin, none_end, drain_blank, 0)


def local_product(plan, sigma, panel, homes, rows, turn, sizes):
    nodes, _, strip, width = panel.shape[1:]
    total = homes * sum(sizes)
    hbm = pl.BlockSpec(memory_space=pl.ANY)
    smem = pl.BlockSpec(memory_space=pltpu.SMEM)
    return pl.pallas_call(
        functools.partial(product_kernel, turn, sizes, rows, nodes, homes),
        out_shape=[jax.ShapeDtypeStruct((size, width, width), jnp.float32) for size in sizes for _ in range(homes)],
        in_specs=[smem] * 4 + [hbm, hbm],
        out_specs=[hbm] * (homes * len(sizes)),
        scratch_shapes=[
            pltpu.VMEM((BUFS, width, width), jnp.float32),
            pltpu.VMEM((BUFS, width, width), jnp.float32),
            pltpu.VMEM((3 * width, width), jnp.bfloat16),
            pltpu.VMEM((total, width, width), jnp.float32),
            pltpu.SemaphoreType.DMA((BUFS,)),
            pltpu.SemaphoreType.DMA((BUFS, rows)),
            pltpu.SemaphoreType.DMA((total,)),
        ],
        compiler_params=pltpu.CompilerParams(vmem_limit_bytes=50 * MIB),
        cost_estimate=pl.CostEstimate(
            flops=6 * 60 * width**3, bytes_accessed=60 * 8 * width * width, transcendentals=0
        ),
    )(*plan, sigma, panel)


def prepare_kernel(panel, whole, own, scaled, gram):
    nodes, entries, strip, width = panel.shape
    for node in range(nodes):
        scaled[node] = triple_dot(panel[node].reshape(entries * strip, width), whole[node])
        mine = own[node]
        gram[node] = triple_dot(mine.T, mine)


def prepare(panel, whole, own):
    nodes, entries, strip, width = panel.shape
    vmem = pl.BlockSpec(memory_space=pltpu.VMEM)
    return pl.pallas_call(
        prepare_kernel,
        out_shape=[
            jax.ShapeDtypeStruct((nodes, entries * strip, width), jnp.float32),
            jax.ShapeDtypeStruct(whole.shape, jnp.float32),
        ],
        in_specs=[vmem] * 3,
        out_specs=[vmem] * 2,
        compiler_params=pltpu.CompilerParams(vmem_limit_bytes=40 * MIB),
        cost_estimate=pl.CostEstimate(flops=6 * nodes * entries * strip * width**2, bytes_accessed=width, transcendentals=0),
    )(panel, whole, own)


def finish_kernel(count, sources, entries, which, origin, where, scaled, gram, whole, *refs):
    arrived, (off, terms, raw) = refs[:count], refs[count:]
    nodes, tall, width = scaled.shape
    strip = tall // entries
    for node in range(nodes):
        def pick(entry, carry):
            at = node * entries + entry
            for piece in range(count // sources):
                @pl.when(which[at] == piece)
                def _(piece=piece):
                    for source in range(sources):
                        @pl.when(origin[at] == source)
                        def _():
                            blocks = arrived[piece * sources + source]
                            raw[pl.ds(pl.multiple_of(entry * strip, strip), strip), :] = blocks[where[at]]

            return carry

        lax.fori_loop(0, entries, pick, 0)
        product = triple_dot(raw[...], whole[node])
        off[node] = -product.reshape(entries, strip, width)
        terms[node] = gram[node] + triple_dot(scaled[node].T, product)


def finish(table, sources, entries, scaled, gram, whole, arrived):
    nodes, tall, width = scaled.shape
    vmem = pl.BlockSpec(memory_space=pltpu.VMEM)
    smem = pl.BlockSpec(memory_space=pltpu.SMEM)
    return pl.pallas_call(
        functools.partial(finish_kernel, len(arrived), sources, entries),
        out_shape=[
            jax.ShapeDtypeStruct((nodes, entries, tall // entries, width), jnp.float32),
            jax.ShapeDtypeStruct(whole.shape, jnp.float32),
        ],
        in_specs=[smem] * 3 + [vmem] * (3 + len(arrived)),
        out_specs=[vmem, vmem],
        scratch_shapes=[pltpu.VMEM((tall, width), jnp.float32)],
        compiler_params=pltpu.CompilerParams(vmem_limit_bytes=40 * MIB),
        cost_estimate=pl.CostEstimate(flops=6 * nodes * 2 * tall * width**2, bytes_accessed=8 * MIB, transcendentals=0),
    )(*table, scaled, gram, whole, *arrived)


def per_device(rows, homes, sigma_anc, panel, diag_inv, structure):
    nodes, entries, strip, width = panel.shape
    own_rows, own_cols = sigma_anc.shape[0] // width, sigma_anc.shape[1] // width
    chips = homes // 2

    struct = lax.all_gather(structure, "col", axis=0, tiled=True)
    every_panel = lax.all_gather(panel, ("row", "col"), axis=0, tiled=False)
    own_inverse, every_panel = lax.optimization_barrier((diag_inv, every_panel))
    whole_inverse = lax.all_gather(own_inverse, "row", axis=1, tiled=True)

    my_row = lax.axis_index("row").astype(jnp.int32)
    my_col = lax.axis_index("col").astype(jnp.int32)
    spot = jnp.stack([my_row, my_col])

    most = nodes * min(entries, own_rows)
    rounds, reach = [], 0
    for sizes in (PIECES,) + tuple((size,) for size in EXTRA) + ((most,),):
        held = []
        for size in sizes:
            size = min(size, most - reach)
            if size > 0:
                held.append((reach, size))
                reach += size
        if held:
            rounds.append(held)
    spans = tuple((held[0][0], sum(size for _, size in held)) for held in rounds)
    plan = make_plan(spot, struct, spans, nodes, own_rows, own_cols)

    holders = struct.reshape(homes, -1) // own_rows
    loads = jnp.sum(holders[:, :, None] == jnp.arange(rows, dtype=jnp.int32), axis=1)
    heaviest = jnp.max(loads)

    direct = rows <= 8
    holder = structure.reshape(-1) // own_rows
    pair = jnp.arange(nodes * entries, dtype=jnp.int32)
    earlier = (holder[:, None] == holder[None, :]) & (pair[None, :] < pair[:, None])
    rank = jnp.sum(earlier.astype(jnp.int32), axis=1)
    which, where = jnp.zeros_like(rank), rank
    width_of = jnp.zeros_like(rank)
    for piece, (first, size) in enumerate(span for held in rounds for span in held):
        which = jnp.where(rank >= first, piece, which)
        where = jnp.where(rank >= first, rank - first, where)
        width_of = jnp.where(rank >= first, size, width_of)
    if direct:
        origin = lax.rem(my_row - holder + rows, rows)
    else:
        origin, where = jnp.zeros_like(rank), holder * width_of + where
    table = (which, origin, where)

    sibling = [(col, col ^ 1) for col in range(homes)]

    def to_rows(total, size):
        strips = total.reshape(size, rows, strip, width)
        if not direct:
            strips = lax.all_to_all(strips.transpose(1, 0, 2, 3), "row", split_axis=0, concat_axis=0, tiled=True)
            return [strips.reshape(rows * size, strip, width)]
        landed = []
        for distance in range(rows):
            part = lax.dynamic_index_in_dim(strips, lax.rem(my_row + distance, rows), 1, keepdims=False)
            if distance:
                part = lax.ppermute(part, "row", [(row, (row + distance) % rows) for row in range(rows)])
            landed.append(part)
        return landed

    def exchange(turn, inverse):
        sizes = tuple(size for _, size in rounds[turn])
        blocks = local_product(plan, sigma_anc, every_panel, homes, rows, turn, sizes)
        arrived, crossed = [], []
        for piece, size in enumerate(sizes):
            mine = blocks[piece * homes : (piece + 1) * homes]
            total = None
            for away in range(1, chips):
                summed = mine[2 * away] + lax.ppermute(mine[2 * away + 1], "col", sibling)
                if piece >= 2:
                    summed, crossed[piece - 2] = lax.optimization_barrier((summed, crossed[piece - 2]))
                moved = lax.ppermute(summed, "col", [(col, (col + 2 * away) % homes) for col in range(homes)])
                total = moved if total is None else total + moved
            crossed.append(total)
            arrived.append(mine[0] + lax.ppermute(mine[1], "col", sibling))
        landed = []
        for piece, size in enumerate(sizes):
            total = arrived[piece] if crossed[piece] is None else arrived[piece] + crossed[piece]
            if piece == 1 and turn == 0:
                total, inverse = lax.optimization_barrier((total, inverse))
            landed += to_rows(total, size)
        return landed, inverse

    landed, whole_inverse = exchange(0, whole_inverse)
    scaled, gram = prepare(panel, whole_inverse, diag_inv)
    sources = rows if direct else 1

    def ending(extra):
        def branch():
            more = list(landed)
            for turn in range(1, 1 + extra):
                more += exchange(turn, whole_inverse)[0]
            return finish(table, sources, entries, scaled, gram, whole_inverse, more)

        return branch

    if len(rounds) == 1:
        off, terms = ending(0)()
    else:
        level = sum((heaviest > first).astype(jnp.int32) for first, _ in spans[1:])
        off, terms = lax.switch(level, [ending(extra) for extra in range(len(rounds))])
    sigma_diag = lax.psum_scatter(terms, "row", scatter_dimension=1, tiled=True)
    return off, sigma_diag


def solution(mesh):
    placed = (
        P(("grp", "row"), "col"),
        P(("grp", "col"), None, "row", None),
        P(("grp", "col"), "row", None),
        P("col", None),
    )
    return jax.shard_map(
        functools.partial(per_device, mesh.shape["row"], mesh.shape["col"]),
        mesh=mesh,
        in_specs=placed,
        out_specs=(P(("grp", "col"), None, "row", None), P(("grp", "col"), "row", None)),
        check_vma=False,
    )
```

```python
import functools

import jax
import jax.numpy as jnp
from jax import lax
from jax.experimental import pallas as pl
from jax.experimental.pallas import tpu as pltpu
from jax.sharding import PartitionSpec as P

PIECES = (3, 4, 4, 2)
EXTRA = (4, 7)
BUFS = 12
FIELDS = 9
MIB = 1024 * 1024


def split(value):
    high = value.astype(jnp.bfloat16)
    return high, (value - high.astype(jnp.float32)).astype(jnp.bfloat16)


def triple_dot(left, right):
    left_high, left_low = split(left)
    right_high, right_low = split(right)
    dot = functools.partial(jnp.dot, preferred_element_type=jnp.float32)
    return dot(left_high, right_high) + (dot(left_high, right_low) + dot(left_low, right_high))


def plan_kernel(spans, nodes, own_rows, own_cols, spot, struct, todo, ends, empty, empties):
    entries = struct.shape[1]
    homes = struct.shape[0] // nodes
    chips = homes // 2
    my_row, my_col = spot[0], spot[1]

    def piece_list(first, size, state):
        def per_home(home, state):
            distance = lax.rem(home // 2 - my_col // 2 + chips, chips)
            group = distance * 2 + lax.rem(home + my_col, 2)

            def per_node(member, state):
                rank, count, blocks, none = state
                node = home * nodes + member
                low = high = rank
                for p in range(entries):
                    mine = (struct[node, p] // own_rows == my_row).astype(jnp.int32)
                    high += mine
                held = high - low
                start = jnp.maximum(low, first)
                stop = jnp.minimum(high, first + size)
                columns = jnp.int32(0)
                for q in range(entries):
                    columns += (struct[node, q] // own_cols == my_col).astype(jnp.int32)

                def enlist():
                    def per_column(q, state):
                        order, count, blocks = state
                        other = struct[node, q]

                        def per_row(p, state):
                            at_rank, count = state
                            block = struct[node, p]
                            mine = block // own_rows == my_row

                            @pl.when(mine & (at_rank >= start) & (at_rank < stop))
                            def _():
                                at = count * FIELDS
                                todo[at] = block - my_row * own_rows
                                todo[at + 1] = other - my_col * own_cols
                                todo[at + 2] = node
                                todo[at + 3] = q
                                todo[at + 4] = group * size + at_rank - first
                                todo[at + 5] = (order == 0).astype(jnp.int32)
                                todo[at + 6] = (order == columns - 1).astype(jnp.int32)
                                todo[at + 7] = (at_rank == start).astype(jnp.int32)
                                todo[at + 8] = blocks

                            taken = mine & (at_rank >= start) & (at_rank < stop)
                            return at_rank + mine.astype(jnp.int32), count + taken.astype(jnp.int32)

                        def column():
                            return lax.fori_loop(0, entries, per_row, (low, count))[1]

                        hit = other // own_cols == my_col
                        count = lax.cond(hit, column, lambda: count)
                        step = hit.astype(jnp.int32)
                        return order + step, count, blocks + step

                    def all_empty():
                        def one(at_rank, none):
                            empty[none] = group * size + at_rank - first
                            return none + 1

                        return lax.fori_loop(start, stop, one, none)

                    _, more, further = lax.fori_loop(0, entries, per_column, (jnp.int32(0), count, blocks))
                    return more, further, lax.cond(columns == 0, all_empty, lambda: none)

                count, blocks, none = lax.cond(start < stop, enlist, lambda: (count, blocks, none))
                return high, count, blocks, none

            return lax.fori_loop(0, nodes, per_node, (jnp.int32(0),) + state)[1:]

        return lax.fori_loop(0, homes, per_home, state)

    count = none = jnp.int32(0)
    for piece, (first, size) in enumerate(spans):
        count, _, none = piece_list(first, size, (count, jnp.int32(0), none))
        ends[piece] = count
        empties[piece] = none


def make_plan(spot, struct, spans, nodes, own_rows, own_cols):
    total = struct.shape[0] // nodes * sum(size for _, size in spans)
    smem = pl.BlockSpec(memory_space=pltpu.SMEM)
    lengths = (total * struct.shape[1] * FIELDS, len(spans), total, len(spans))
    return pl.pallas_call(
        functools.partial(plan_kernel, spans, nodes, own_rows, own_cols),
        out_shape=[jax.ShapeDtypeStruct((length,), jnp.int32) for length in lengths],
        in_specs=[smem, smem],
        out_specs=[smem] * 4,
    )(spot, struct)


def product_kernel(turn, sizes, rows, nodes, homes, todo, ends, empty, empties, sigma, panel, *refs):
    outs = refs[: homes * len(sizes)]
    sbuf, xbuf, deep, obuf, ssem, xsem, osem = refs[homes * len(sizes) :]
    width = sbuf.shape[1]
    slots = sum(sizes)
    begin = ends[turn - 1] if turn else 0
    end = ends[turn]
    none_begin = empties[turn - 1] if turn else 0
    none_end = empties[turn]

    def put(slot):
        group = slot // slots
        inside = slot - group * slots
        first = 0
        for piece, size in enumerate(sizes):
            @pl.when((inside >= first) & (inside < first + size))
            def _(piece=piece, first=first):
                for other in range(homes):
                    @pl.when(group == other)
                    def _():
                        out = outs[piece * homes + other]
                        pltpu.make_async_copy(obuf.at[slot], out.at[inside - first], osem.at[slot]).start()

            first += size

    def settle(slot):
        pltpu.make_async_copy(obuf.at[slot], outs[0].at[0], osem.at[slot]).wait()

    def fetch(item, act):
        buf = lax.rem(item, BUFS)
        at = item * FIELDS
        top = pl.multiple_of(todo[at] * width, width)
        left = pl.multiple_of(todo[at + 1] * width, width)
        act(pltpu.make_async_copy(sigma.at[pl.ds(top, width), pl.ds(left, width)], sbuf.at[buf], ssem.at[buf]))

        @pl.when(todo[at + 7] == 1)
        def _():
            node, q = todo[at + 2], todo[at + 3]
            xslot = lax.rem(todo[at + 8], BUFS)
            source = panel.at[:, node // nodes, lax.rem(node, nodes), q]
            act(pltpu.make_async_copy(source, xbuf.at[xslot], xsem.at[xslot]))

    for ahead in range(BUFS - 1):
        @pl.when(begin + ahead < end)
        def _():
            fetch(begin + ahead, lambda copy: copy.start())

    def blank(item, carry):
        slot = empty[item]
        obuf[slot] = jnp.zeros(obuf.shape[1:], jnp.float32)
        put(slot)
        return carry

    lax.fori_loop(none_begin, none_end, blank, 0)

    def step(item, carry):
        buf = lax.rem(item, BUFS)

        @pl.when(item + BUFS - 1 < end)
        def _():
            fetch(item + BUFS - 1, lambda copy: copy.start())

        fetch(item, lambda copy: copy.wait())
        at = item * FIELDS
        slot = todo[at + 4]

        @pl.when(todo[at + 7] == 1)
        def _():
            high, low = split(xbuf[lax.rem(todo[at + 8], BUFS)].reshape(width, width))
            deep[:width] = high
            deep[width : 2 * width] = low
            deep[2 * width :] = high

        high, low = split(sbuf[buf])
        term = jnp.dot(
            jnp.concatenate([high, high, low], axis=1), deep[...], preferred_element_type=jnp.float32
        )

        obuf[slot] = term + jnp.where(todo[at + 5] == 1, 0.0, obuf[slot])

        @pl.when(todo[at + 6] == 1)
        def _():
            put(slot)

        return carry

    lax.fori_loop(begin, end, step, 0)

    def drain(item, carry):
        @pl.when(todo[item * FIELDS + 6] == 1)
        def _():
            settle(todo[item * FIELDS + 4])

        return carry

    lax.fori_loop(begin, end, drain, 0)

    def drain_blank(item, carry):
        settle(empty[item])
        return carry

    lax.fori_loop(none_begin, none_end, drain_blank, 0)


def local_product(plan, sigma, panel, homes, rows, turn, sizes):
    nodes, _, strip, width = panel.shape[2:]
    total = homes * sum(sizes)
    hbm = pl.BlockSpec(memory_space=pl.ANY)
    smem = pl.BlockSpec(memory_space=pltpu.SMEM)
    return pl.pallas_call(
        functools.partial(product_kernel, turn, sizes, rows, nodes, homes),
        out_shape=[jax.ShapeDtypeStruct((size, width, width), jnp.float32) for size in sizes for _ in range(homes)],
        in_specs=[smem] * 4 + [hbm, hbm],
        out_specs=[hbm] * (homes * len(sizes)),
        scratch_shapes=[
            pltpu.VMEM((BUFS, width, width), jnp.float32),
            pltpu.VMEM((BUFS, rows, strip, width), jnp.float32),
            pltpu.VMEM((3 * width, width), jnp.bfloat16),
            pltpu.VMEM((total, width, width), jnp.float32),
            pltpu.SemaphoreType.DMA((BUFS,)),
            pltpu.SemaphoreType.DMA((BUFS,)),
            pltpu.SemaphoreType.DMA((total,)),
        ],
        compiler_params=pltpu.CompilerParams(vmem_limit_bytes=50 * MIB),
        cost_estimate=pl.CostEstimate(
            flops=6 * 60 * width**3, bytes_accessed=60 * 8 * width * width, transcendentals=0
        ),
    )(*plan, sigma, panel)


def prepare_kernel(panel, whole, own, scaled, gram):
    nodes, entries, strip, width = panel.shape
    for node in range(nodes):
        scaled[node] = triple_dot(panel[node].reshape(entries * strip, width), whole[node])
        mine = own[node]
        gram[node] = triple_dot(mine.T, mine)


def prepare(panel, whole, own):
    nodes, entries, strip, width = panel.shape
    vmem = pl.BlockSpec(memory_space=pltpu.VMEM)
    return pl.pallas_call(
        prepare_kernel,
        out_shape=[
            jax.ShapeDtypeStruct((nodes, entries * strip, width), jnp.float32),
            jax.ShapeDtypeStruct(whole.shape, jnp.float32),
        ],
        in_specs=[vmem] * 3,
        out_specs=[vmem] * 2,
        compiler_params=pltpu.CompilerParams(vmem_limit_bytes=40 * MIB),
        cost_estimate=pl.CostEstimate(flops=6 * nodes * entries * strip * width**2, bytes_accessed=width, transcendentals=0),
    )(panel, whole, own)


def finish_kernel(count, sources, entries, which, origin, where, scaled, gram, whole, *refs):
    arrived, (off, terms, raw) = refs[:count], refs[count:]
    nodes, tall, width = scaled.shape
    strip = tall // entries
    for node in range(nodes):
        def pick(entry, carry):
            at = node * entries + entry
            for piece in range(count // sources):
                @pl.when(which[at] == piece)
                def _(piece=piece):
                    for source in range(sources):
                        @pl.when(origin[at] == source)
                        def _():
                            blocks = arrived[piece * sources + source]
                            raw[pl.ds(pl.multiple_of(entry * strip, strip), strip), :] = blocks[where[at]]

            return carry

        lax.fori_loop(0, entries, pick, 0)
        product = triple_dot(raw[...], whole[node])
        off[node] = -product.reshape(entries, strip, width)
        terms[node] = gram[node] + triple_dot(scaled[node].T, product)


def finish(table, sources, entries, scaled, gram, whole, arrived):
    nodes, tall, width = scaled.shape
    vmem = pl.BlockSpec(memory_space=pltpu.VMEM)
    smem = pl.BlockSpec(memory_space=pltpu.SMEM)
    return pl.pallas_call(
        functools.partial(finish_kernel, len(arrived), sources, entries),
        out_shape=[
            jax.ShapeDtypeStruct((nodes, entries, tall // entries, width), jnp.float32),
            jax.ShapeDtypeStruct(whole.shape, jnp.float32),
        ],
        in_specs=[smem] * 3 + [vmem] * (3 + len(arrived)),
        out_specs=[vmem, vmem],
        scratch_shapes=[pltpu.VMEM((tall, width), jnp.float32)],
        compiler_params=pltpu.CompilerParams(vmem_limit_bytes=40 * MIB),
        cost_estimate=pl.CostEstimate(flops=6 * nodes * 2 * tall * width**2, bytes_accessed=8 * MIB, transcendentals=0),
    )(*table, scaled, gram, whole, *arrived)


def per_device(rows, homes, sigma_anc, panel, diag_inv, structure):
    nodes, entries, strip, width = panel.shape
    own_rows, own_cols = sigma_anc.shape[0] // width, sigma_anc.shape[1] // width
    chips = homes // 2

    struct = lax.all_gather(structure, "col", axis=0, tiled=True)
    every_panel = lax.all_gather(panel, ("row", "col"), axis=0, tiled=False)
    own_inverse, every_panel = lax.optimization_barrier((diag_inv, every_panel))
    every_panel = every_panel.reshape((rows, homes) + panel.shape)
    whole_inverse = lax.all_gather(own_inverse, "row", axis=1, tiled=True)

    my_row = lax.axis_index("row").astype(jnp.int32)
    my_col = lax.axis_index("col").astype(jnp.int32)
    spot = jnp.stack([my_row, my_col])

    most = nodes * min(entries, own_rows)
    rounds, reach = [], 0
    for sizes in (PIECES,) + tuple((size,) for size in EXTRA) + ((most,),):
        held = []
        for size in sizes:
            size = min(size, most - reach)
            if size > 0:
                held.append((reach, size))
                reach += size
        if held:
            rounds.append(held)
    spans = tuple((held[0][0], sum(size for _, size in held)) for held in rounds)
    plan = make_plan(spot, struct, spans, nodes, own_rows, own_cols)

    holders = struct.reshape(homes, -1) // own_rows
    loads = jnp.sum(holders[:, :, None] == jnp.arange(rows, dtype=jnp.int32), axis=1)
    heaviest = jnp.max(loads)

    direct = False
    holder = structure.reshape(-1) // own_rows
    pair = jnp.arange(nodes * entries, dtype=jnp.int32)
    earlier = (holder[:, None] == holder[None, :]) & (pair[None, :] < pair[:, None])
    rank = jnp.sum(earlier.astype(jnp.int32), axis=1)
    which, where = jnp.zeros_like(rank), rank
    width_of = jnp.zeros_like(rank)
    for piece, (first, size) in enumerate(span for held in rounds for span in held):
        which = jnp.where(rank >= first, piece, which)
        where = jnp.where(rank >= first, rank - first, where)
        width_of = jnp.where(rank >= first, size, width_of)
    if direct:
        origin = lax.rem(my_row - holder + rows, rows)
    else:
        origin, where = jnp.zeros_like(rank), holder * width_of + where
    table = (which, origin, where)

    sibling = [(col, col ^ 1) for col in range(homes)]

    def to_rows(total, size):
        strips = total.reshape(size, rows, strip, width)
        if not direct:
            strips = lax.all_to_all(strips.transpose(1, 0, 2, 3), "row", split_axis=0, concat_axis=0, tiled=True)
            return [strips.reshape(rows * size, strip, width)]
        landed = []
        for distance in range(rows):
            part = lax.dynamic_index_in_dim(strips, lax.rem(my_row + distance, rows), 1, keepdims=False)
            if distance:
                part = lax.ppermute(part, "row", [(row, (row + distance) % rows) for row in range(rows)])
            landed.append(part)
        return landed

    def exchange(turn, inverse):
        sizes = tuple(size for _, size in rounds[turn])
        blocks = local_product(plan, sigma_anc, every_panel, homes, rows, turn, sizes)
        arrived, crossed = [], []
        for piece, size in enumerate(sizes):
            mine = blocks[piece * homes : (piece + 1) * homes]
            total = None
            for away in range(1, chips):
                summed = mine[2 * away] + lax.ppermute(mine[2 * away + 1], "col", sibling)
                if piece >= 2:
                    ahead = piece - 1 if piece == len(sizes) - 1 else piece - 2
                    summed, crossed[ahead] = lax.optimization_barrier((summed, crossed[ahead]))
                moved = lax.ppermute(summed, "col", [(col, (col + 2 * away) % homes) for col in range(homes)])
                total = moved if total is None else total + moved
            crossed.append(total)
            arrived.append(mine[0] + lax.ppermute(mine[1], "col", sibling))
        landed = []
        for piece, size in enumerate(sizes):
            total = arrived[piece] if crossed[piece] is None else arrived[piece] + crossed[piece]
            if piece == 1 and turn == 0:
                total, inverse = lax.optimization_barrier((total, inverse))
            landed += to_rows(total, size)
        return landed, inverse

    landed, whole_inverse = exchange(0, whole_inverse)
    scaled, gram = prepare(panel, whole_inverse, diag_inv)
    sources = rows if direct else 1

    def ending(extra):
        def branch():
            more = list(landed)
            for turn in range(1, 1 + extra):
                more += exchange(turn, whole_inverse)[0]
            return finish(table, sources, entries, scaled, gram, whole_inverse, more)

        return branch

    if len(rounds) == 1:
        off, terms = ending(0)()
    else:
        level = sum((heaviest > first).astype(jnp.int32) for first, _ in spans[1:])
        off, terms = lax.switch(level, [ending(extra) for extra in range(len(rounds))])
    sigma_diag = lax.psum_scatter(terms, "row", scatter_dimension=1, tiled=True)
    return off, sigma_diag


def solution(mesh):
    placed = (
        P(("grp", "row"), "col"),
        P(("grp", "col"), None, "row", None),
        P(("grp", "col"), "row", None),
        P("col", None),
    )
    return jax.shard_map(
        functools.partial(per_device, mesh.shape["row"], mesh.shape["col"]),
        mesh=mesh,
        in_specs=placed,
        out_specs=(P(("grp", "col"), None, "row", None), P(("grp", "col"), "row", None)),
        check_vma=False,
    )
```

```python
import functools

import jax
import jax.numpy as jnp
from jax import lax
from jax.experimental import pallas as pl
from jax.experimental.pallas import tpu as pltpu
from jax.sharding import PartitionSpec as P

PIECES = (3, 4, 4, 2)
EXTRA = (4, 7)
BUFS = 12
FIELDS = 9
MIB = 1024 * 1024


def split(value):
    high = value.astype(jnp.bfloat16)
    return high, (value - high.astype(jnp.float32)).astype(jnp.bfloat16)


def triple_dot(left, right):
    left_high, left_low = split(left)
    right_high, right_low = split(right)
    dot = functools.partial(jnp.dot, preferred_element_type=jnp.float32)
    return dot(left_high, right_high) + (dot(left_high, right_low) + dot(left_low, right_high))


def plan_kernel(spans, nodes, own_rows, own_cols, spot, struct, todo, ends, empty, empties):
    entries = struct.shape[1]
    homes = struct.shape[0] // nodes
    chips = homes // 2
    my_row, my_col = spot[0], spot[1]

    def piece_list(first, size, state):
        def per_home(home, state):
            distance = lax.rem(home // 2 - my_col // 2 + chips, chips)
            group = distance * 2 + lax.rem(home + my_col, 2)

            def per_node(member, state):
                rank, count, blocks, none = state
                node = home * nodes + member
                low = high = rank
                for p in range(entries):
                    mine = (struct[node, p] // own_rows == my_row).astype(jnp.int32)
                    high += mine
                held = high - low
                start = jnp.maximum(low, first)
                stop = jnp.minimum(high, first + size)
                columns = jnp.int32(0)
                for q in range(entries):
                    columns += (struct[node, q] // own_cols == my_col).astype(jnp.int32)

                def enlist():
                    def per_column(q, state):
                        order, count, blocks = state
                        other = struct[node, q]

                        def per_row(p, state):
                            at_rank, count = state
                            block = struct[node, p]
                            mine = block // own_rows == my_row

                            @pl.when(mine & (at_rank >= start) & (at_rank < stop))
                            def _():
                                at = count * FIELDS
                                todo[at] = block - my_row * own_rows
                                todo[at + 1] = other - my_col * own_cols
                                todo[at + 2] = node
                                todo[at + 3] = q
                                todo[at + 4] = group * size + at_rank - first
                                todo[at + 5] = (order == 0).astype(jnp.int32)
                                todo[at + 6] = (order == columns - 1).astype(jnp.int32)
                                todo[at + 7] = (at_rank == start).astype(jnp.int32)
                                todo[at + 8] = blocks

                            taken = mine & (at_rank >= start) & (at_rank < stop)
                            return at_rank + mine.astype(jnp.int32), count + taken.astype(jnp.int32)

                        def column():
                            return lax.fori_loop(0, entries, per_row, (low, count))[1]

                        hit = other // own_cols == my_col
                        count = lax.cond(hit, column, lambda: count)
                        step = hit.astype(jnp.int32)
                        return order + step, count, blocks + step

                    def all_empty():
                        def one(at_rank, none):
                            empty[none] = group * size + at_rank - first
                            return none + 1

                        return lax.fori_loop(start, stop, one, none)

                    _, more, further = lax.fori_loop(0, entries, per_column, (jnp.int32(0), count, blocks))
                    return more, further, lax.cond(columns == 0, all_empty, lambda: none)

                count, blocks, none = lax.cond(start < stop, enlist, lambda: (count, blocks, none))
                return high, count, blocks, none

            return lax.fori_loop(0, nodes, per_node, (jnp.int32(0),) + state)[1:]

        return lax.fori_loop(0, homes, per_home, state)

    count = none = jnp.int32(0)
    for piece, (first, size) in enumerate(spans):
        count, _, none = piece_list(first, size, (count, jnp.int32(0), none))
        ends[piece] = count
        empties[piece] = none


def make_plan(spot, struct, spans, nodes, own_rows, own_cols):
    total = struct.shape[0] // nodes * sum(size for _, size in spans)
    smem = pl.BlockSpec(memory_space=pltpu.SMEM)
    lengths = (total * struct.shape[1] * FIELDS, len(spans), total, len(spans))
    return pl.pallas_call(
        functools.partial(plan_kernel, spans, nodes, own_rows, own_cols),
        out_shape=[jax.ShapeDtypeStruct((length,), jnp.int32) for length in lengths],
        in_specs=[smem, smem],
        out_specs=[smem] * 4,
    )(spot, struct)


def product_kernel(turn, sizes, rows, nodes, homes, todo, ends, empty, empties, sigma, panel, *refs):
    outs = refs[: homes * len(sizes)]
    sbuf, xbuf, deep, obuf, ssem, xsem, osem = refs[homes * len(sizes) :]
    width = sbuf.shape[1]
    slots = sum(sizes)
    begin = ends[turn - 1] if turn else 0
    end = ends[turn]
    none_begin = empties[turn - 1] if turn else 0
    none_end = empties[turn]

    def put(slot):
        group = slot // slots
        inside = slot - group * slots
        first = 0
        for piece, size in enumerate(sizes):
            @pl.when((inside >= first) & (inside < first + size))
            def _(piece=piece, first=first):
                for other in range(homes):
                    @pl.when(group == other)
                    def _():
                        out = outs[piece * homes + other]
                        pltpu.make_async_copy(obuf.at[slot], out.at[inside - first], osem.at[slot]).start()

            first += size

    def settle(slot):
        pltpu.make_async_copy(obuf.at[slot], outs[0].at[0], osem.at[slot]).wait()

    def fetch(item, act):
        buf = lax.rem(item, BUFS)
        at = item * FIELDS
        top = pl.multiple_of(todo[at] * width, width)
        left = pl.multiple_of(todo[at + 1] * width, width)
        act(pltpu.make_async_copy(sigma.at[pl.ds(top, width), pl.ds(left, width)], sbuf.at[buf], ssem.at[buf]))

        @pl.when(todo[at + 7] == 1)
        def _():
            node, q = todo[at + 2], todo[at + 3]
            xslot = lax.rem(todo[at + 8], BUFS)
            source = panel.at[:, node // nodes, lax.rem(node, nodes), q]
            act(pltpu.make_async_copy(source, xbuf.at[xslot], xsem.at[xslot]))

    for ahead in range(BUFS - 1):
        @pl.when(begin + ahead < end)
        def _():
            fetch(begin + ahead, lambda copy: copy.start())

    def blank(item, carry):
        slot = empty[item]
        obuf[slot] = jnp.zeros(obuf.shape[1:], jnp.float32)
        put(slot)
        return carry

    lax.fori_loop(none_begin, none_end, blank, 0)

    def step(item, carry):
        buf = lax.rem(item, BUFS)

        @pl.when(item + BUFS - 1 < end)
        def _():
            fetch(item + BUFS - 1, lambda copy: copy.start())

        fetch(item, lambda copy: copy.wait())
        at = item * FIELDS
        slot = todo[at + 4]

        @pl.when(todo[at + 7] == 1)
        def _():
            high, low = split(xbuf[lax.rem(todo[at + 8], BUFS)].reshape(width, width))
            deep[:width] = high
            deep[width : 2 * width] = low
            deep[2 * width :] = high

        high, low = split(sbuf[buf])
        term = jnp.dot(
            jnp.concatenate([high, high, low], axis=1), deep[...], preferred_element_type=jnp.float32
        )

        obuf[slot] = term + jnp.where(todo[at + 5] == 1, 0.0, obuf[slot])

        @pl.when(todo[at + 6] == 1)
        def _():
            put(slot)

        return carry

    lax.fori_loop(begin, end, step, 0)

    def drain(item, carry):
        @pl.when(todo[item * FIELDS + 6] == 1)
        def _():
            settle(todo[item * FIELDS + 4])

        return carry

    lax.fori_loop(begin, end, drain, 0)

    def drain_blank(item, carry):
        settle(empty[item])
        return carry

    lax.fori_loop(none_begin, none_end, drain_blank, 0)


def local_product(plan, sigma, panel, homes, rows, turn, sizes):
    nodes, _, strip, width = panel.shape[2:]
    total = homes * sum(sizes)
    hbm = pl.BlockSpec(memory_space=pl.ANY)
    smem = pl.BlockSpec(memory_space=pltpu.SMEM)
    return pl.pallas_call(
        functools.partial(product_kernel, turn, sizes, rows, nodes, homes),
        out_shape=[jax.ShapeDtypeStruct((size, width, width), jnp.float32) for size in sizes for _ in range(homes)],
        in_specs=[smem] * 4 + [hbm, hbm],
        out_specs=[hbm] * (homes * len(sizes)),
        scratch_shapes=[
            pltpu.VMEM((BUFS, width, width), jnp.float32),
            pltpu.VMEM((BUFS, rows, strip, width), jnp.float32),
            pltpu.VMEM((3 * width, width), jnp.bfloat16),
            pltpu.VMEM((total, width, width), jnp.float32),
            pltpu.SemaphoreType.DMA((BUFS,)),
            pltpu.SemaphoreType.DMA((BUFS,)),
            pltpu.SemaphoreType.DMA((total,)),
        ],
        compiler_params=pltpu.CompilerParams(vmem_limit_bytes=50 * MIB),
        cost_estimate=pl.CostEstimate(
            flops=6 * 60 * width**3, bytes_accessed=60 * 8 * width * width, transcendentals=0
        ),
    )(*plan, sigma, panel)


def corner_kernel(base, sizes, own_rows, spot, own_struct, panel, whole, own, *refs):
    totals, (out, gram, xbuf, xsem) = refs[: len(sizes)], refs[len(sizes) :]
    nodes, entries = own_struct.shape
    width = whole.shape[1]
    my_row, my_col = spot[0], spot[1]
    slots = sum(sizes)

    def walk(act):
        def per_pair(pair, rank):
            node, p = pair // entries, lax.rem(pair, entries)
            mine = own_struct[node, p] // own_rows == my_row
            slot = rank - base

            @pl.when(mine & (slot >= 0) & (slot < slots))
            def _():
                act(node, slot, pltpu.make_async_copy(panel.at[:, my_col, node, p], xbuf.at[slot], xsem.at[slot]))

            return rank + mine.astype(jnp.int32)

        lax.fori_loop(0, nodes * entries, per_pair, jnp.int32(0))

    walk(lambda node, slot, copy: copy.start())
    gram[...] = jnp.zeros(gram.shape, jnp.float32)

    def gather(node, slot, copy):
        copy.wait()
        left = xbuf[slot].reshape(width, width).T
        first = 0
        for total, size in zip(totals, sizes):
            @pl.when((slot >= first) & (slot < first + size))
            def _():
                gram[node] += triple_dot(left, total[slot - first])

            first += size

    walk(gather)
    for node in range(nodes):
        inverse = whole[node]
        part = triple_dot(inverse.T, triple_dot(gram[node], inverse))
        if base == 0:
            mine = own[node]
            part += triple_dot(mine.T, mine)
        out[node] = part


def corner(spot, own_struct, panel, whole, own, totals, base, sizes, own_rows):
    rows, _, nodes, _, strip, width = panel.shape
    vmem = pl.BlockSpec(memory_space=pltpu.VMEM)
    smem = pl.BlockSpec(memory_space=pltpu.SMEM)
    return pl.pallas_call(
        functools.partial(corner_kernel, base, sizes, own_rows),
        out_shape=jax.ShapeDtypeStruct(whole.shape, jnp.float32),
        in_specs=[smem, smem, pl.BlockSpec(memory_space=pl.ANY)] + [vmem] * (2 + len(totals)),
        out_specs=vmem,
        scratch_shapes=[
            pltpu.VMEM(whole.shape, jnp.float32),
            pltpu.VMEM((sum(sizes), rows, strip, width), jnp.float32),
            pltpu.SemaphoreType.DMA((sum(sizes),)),
        ],
        compiler_params=pltpu.CompilerParams(vmem_limit_bytes=40 * MIB),
        cost_estimate=pl.CostEstimate(flops=6 * 22 * width**3, bytes_accessed=8 * MIB, transcendentals=0),
    )(spot, own_struct, panel, whole, own, *totals)


def finish_kernel(pieces, shape, which, where, whole, *refs):
    nodes, entries, strip, width = shape
    arrived, corners, (off, diag, raw) = refs[:pieces], refs[pieces:-3], refs[-3:]
    for node in range(nodes):
        def pick(entry, carry):
            at = node * entries + entry
            for piece, blocks in enumerate(arrived):
                @pl.when(which[at] == piece)
                def _(blocks=blocks):
                    raw[pl.ds(pl.multiple_of(entry * strip, strip), strip), :] = blocks[where[at]]

            return carry

        lax.fori_loop(0, entries, pick, 0)
        off[node] = -triple_dot(raw[...], whole[node]).reshape(entries, strip, width)
        parts = [blocks[row * nodes + node] for blocks in corners for row in range(blocks.shape[0] // nodes)]
        diag[node] = functools.reduce(lambda left, right: left + right, parts)


def finish(table, shape, whole, arrived, corners):
    nodes, entries, strip, width = shape
    vmem = pl.BlockSpec(memory_space=pltpu.VMEM)
    smem = pl.BlockSpec(memory_space=pltpu.SMEM)
    return pl.pallas_call(
        functools.partial(finish_kernel, len(arrived), shape),
        out_shape=[
            jax.ShapeDtypeStruct(shape, jnp.float32),
            jax.ShapeDtypeStruct((nodes, strip, width), jnp.float32),
        ],
        in_specs=[smem] * 2 + [vmem] * (1 + len(arrived) + len(corners)),
        out_specs=[vmem, vmem],
        scratch_shapes=[pltpu.VMEM((entries * strip, width), jnp.float32)],
        compiler_params=pltpu.CompilerParams(vmem_limit_bytes=40 * MIB),
        cost_estimate=pl.CostEstimate(flops=6 * nodes * entries * strip * width**2, bytes_accessed=8 * MIB, transcendentals=0),
    )(*table, whole, *arrived, *corners)


def per_device(rows, homes, sigma_anc, panel, diag_inv, structure):
    nodes, entries, strip, width = panel.shape
    own_rows, own_cols = sigma_anc.shape[0] // width, sigma_anc.shape[1] // width
    chips = homes // 2

    struct = lax.all_gather(structure, "col", axis=0, tiled=True)
    every_panel = lax.all_gather(panel, ("row", "col"), axis=0, tiled=False)
    own_inverse, every_panel = lax.optimization_barrier((diag_inv, every_panel))
    every_panel = every_panel.reshape((rows, homes) + panel.shape)
    whole_inverse = lax.all_gather(own_inverse, "row", axis=1, tiled=True)

    my_row = lax.axis_index("row").astype(jnp.int32)
    my_col = lax.axis_index("col").astype(jnp.int32)
    spot = jnp.stack([my_row, my_col])

    most = nodes * min(entries, own_rows)
    rounds, reach = [], 0
    for sizes in (PIECES,) + tuple((size,) for size in EXTRA) + ((most,),):
        held = []
        for size in sizes:
            size = min(size, most - reach)
            if size > 0:
                held.append((reach, size))
                reach += size
        if held:
            rounds.append(held)
    spans = tuple((held[0][0], sum(size for _, size in held)) for held in rounds)
    plan = make_plan(spot, struct, spans, nodes, own_rows, own_cols)

    holders = struct.reshape(homes, -1) // own_rows
    loads = jnp.sum(holders[:, :, None] == jnp.arange(rows, dtype=jnp.int32), axis=1)
    heaviest = jnp.max(loads)

    holder = structure.reshape(-1) // own_rows
    pair = jnp.arange(nodes * entries, dtype=jnp.int32)
    earlier = (holder[:, None] == holder[None, :]) & (pair[None, :] < pair[:, None])
    rank = jnp.sum(earlier.astype(jnp.int32), axis=1)
    which, where = jnp.zeros_like(rank), rank
    width_of = jnp.zeros_like(rank)
    for piece, (first, size) in enumerate(span for held in rounds for span in held):
        which = jnp.where(rank >= first, piece, which)
        where = jnp.where(rank >= first, rank - first, where)
        width_of = jnp.where(rank >= first, size, width_of)
    table = (which, holder * width_of + where)

    sibling = [(col, col ^ 1) for col in range(homes)]

    def to_rows(total):
        strips = total.reshape(-1, rows, strip, width).transpose(1, 0, 2, 3)
        landed = lax.all_to_all(strips, "row", split_axis=0, concat_axis=0, tiled=True)
        return landed.reshape(-1, strip, width)

    def exchange(turn, inverse):
        sizes = tuple(size for _, size in rounds[turn])
        blocks = local_product(plan, sigma_anc, every_panel, homes, rows, turn, sizes)
        arrived, crossed = [], []
        for piece, size in enumerate(sizes):
            mine = blocks[piece * homes : (piece + 1) * homes]
            total = None
            for away in range(1, chips):
                summed = mine[2 * away] + lax.ppermute(mine[2 * away + 1], "col", sibling)
                if piece >= 2:
                    ahead = piece - 1 if piece == len(sizes) - 1 else piece - 2
                    summed, crossed[ahead] = lax.optimization_barrier((summed, crossed[ahead]))
                moved = lax.ppermute(summed, "col", [(col, (col + 2 * away) % homes) for col in range(homes)])
                total = moved if total is None else total + moved
            crossed.append(total)
            arrived.append(mine[0] + lax.ppermute(mine[1], "col", sibling))
        landed, totals = [], []
        for piece in range(len(sizes)):
            total = arrived[piece] if crossed[piece] is None else arrived[piece] + crossed[piece]
            totals.append(total)
            if piece == 1 and turn == 0:
                total, inverse = lax.optimization_barrier((total, inverse))
            if piece:
                total, landed[-1] = lax.optimization_barrier((total, landed[-1]))
            landed.append(to_rows(total))
        part = corner(spot, structure, every_panel, inverse, diag_inv, totals, spans[turn][0], sizes, own_rows)
        part, landed[-1] = lax.optimization_barrier((part, landed[-1]))
        return landed, to_rows(part), inverse

    landed, part, whole_inverse = exchange(0, whole_inverse)

    def ending(extra):
        def branch():
            more, parts = list(landed), [part]
            for turn in range(1, 1 + extra):
                further, another, _ = exchange(turn, whole_inverse)
                more += further
                parts.append(another)
            return finish(table, panel.shape, whole_inverse, more, parts)

        return branch

    if len(rounds) == 1:
        return tuple(ending(0)())
    level = sum((heaviest > first).astype(jnp.int32) for first, _ in spans[1:])
    return tuple(lax.switch(level, [ending(extra) for extra in range(len(rounds))]))


def solution(mesh):
    placed = (
        P(("grp", "row"), "col"),
        P(("grp", "col"), None, "row", None),
        P(("grp", "col"), "row", None),
        P("col", None),
    )
    return jax.shard_map(
        functools.partial(per_device, mesh.shape["row"], mesh.shape["col"]),
        mesh=mesh,
        in_specs=placed,
        out_specs=(P(("grp", "col"), None, "row", None), P(("grp", "col"), "row", None)),
        check_vma=False,
    )
```

```python
import functools

import jax
import jax.numpy as jnp
from jax import lax
from jax.experimental import pallas as pl
from jax.experimental.pallas import tpu as pltpu
from jax.sharding import PartitionSpec as P

SLOTS = (10, 11, 12, 14)
BUFS = 12
FIELDS = 9
MIB = 1024 * 1024


def split(value):
    high = value.astype(jnp.bfloat16)
    return high, (value - high.astype(jnp.float32)).astype(jnp.bfloat16)


def triple_dot(left, right):
    left_high, left_low = split(left)
    right_high, right_low = split(right)
    dot = functools.partial(jnp.dot, preferred_element_type=jnp.float32)
    return dot(left_high, right_high) + (dot(left_high, right_low) + dot(left_low, right_high))


def plan_kernel(nodes, own_rows, own_cols, spot, struct, todo, ends, empty, empties):
    entries = struct.shape[1]
    homes = struct.shape[0] // nodes
    chips = homes // 2
    my_row, my_col = spot[0], spot[1]

    def piece_list(first, size, state):
        def per_home(home, state):
            distance = lax.rem(home // 2 - my_col // 2 + chips, chips)
            group = distance * 2 + lax.rem(home + my_col, 2)

            def per_node(member, state):
                rank, count, blocks, none = state
                node = home * nodes + member
                low = high = rank
                for p in range(entries):
                    mine = (struct[node, p] // own_rows == my_row).astype(jnp.int32)
                    high += mine
                held = high - low
                start = jnp.maximum(low, first)
                stop = jnp.minimum(high, first + size)
                columns = jnp.int32(0)
                for q in range(entries):
                    columns += (struct[node, q] // own_cols == my_col).astype(jnp.int32)

                def enlist():
                    def per_column(q, state):
                        order, count, blocks = state
                        other = struct[node, q]

                        def per_row(p, state):
                            at_rank, count = state
                            block = struct[node, p]
                            mine = block // own_rows == my_row

                            @pl.when(mine & (at_rank >= start) & (at_rank < stop))
                            def _():
                                at = count * FIELDS
                                todo[at] = block - my_row * own_rows
                                todo[at + 1] = other - my_col * own_cols
                                todo[at + 2] = node
                                todo[at + 3] = q
                                todo[at + 4] = group * size + at_rank - first
                                todo[at + 5] = (order == 0).astype(jnp.int32)
                                todo[at + 6] = (order == columns - 1).astype(jnp.int32)
                                todo[at + 7] = (at_rank == start).astype(jnp.int32)
                                todo[at + 8] = blocks

                            taken = mine & (at_rank >= start) & (at_rank < stop)
                            return at_rank + mine.astype(jnp.int32), count + taken.astype(jnp.int32)

                        def column():
                            return lax.fori_loop(0, entries, per_row, (low, count))[1]

                        hit = other // own_cols == my_col
                        count = lax.cond(hit, column, lambda: count)
                        step = hit.astype(jnp.int32)
                        return order + step, count, blocks + step

                    def all_empty():
                        def one(at_rank, none):
                            empty[none] = group * size + at_rank - first
                            return none + 1

                        return lax.fori_loop(start, stop, one, none)

                    _, more, further = lax.fori_loop(0, entries, per_column, (jnp.int32(0), count, blocks))
                    return more, further, lax.cond(columns == 0, all_empty, lambda: none)

                count, blocks, none = lax.cond(start < stop, enlist, lambda: (count, blocks, none))
                return high, count, blocks, none

            return lax.fori_loop(0, nodes, per_node, (jnp.int32(0),) + state)[1:]

        return lax.fori_loop(0, homes, per_home, state)

    count = none = jnp.int32(0)
    for piece, (first, size) in enumerate(((0, spot[2]), (spot[2], spot[3]))):
        count, _, none = piece_list(first, size, (count, jnp.int32(0), none))
        ends[piece] = count
        empties[piece] = none


def make_plan(spot, struct, most, nodes, own_rows, own_cols):
    total = struct.shape[0] // nodes * most
    smem = pl.BlockSpec(memory_space=pltpu.SMEM)
    lengths = (total * struct.shape[1] * FIELDS, 2, total, 2)
    return pl.pallas_call(
        functools.partial(plan_kernel, nodes, own_rows, own_cols),
        out_shape=[jax.ShapeDtypeStruct((length,), jnp.int32) for length in lengths],
        in_specs=[smem, smem],
        out_specs=[smem] * 4,
    )(spot, struct)


def product_kernel(piece, nodes, homes, todo, ends, empty, empties, sigma, panel, *refs):
    outs = refs[:homes]
    sbuf, xbuf, deep, obuf, ssem, xsem, osem = refs[homes:]
    width = sbuf.shape[1]
    size = outs[0].shape[0]
    begin = ends[piece - 1] if piece else 0
    end = ends[piece]
    none_begin = empties[piece - 1] if piece else 0
    none_end = empties[piece]

    def put(slot):
        group = slot // size
        for other, out in enumerate(outs):
            @pl.when(group == other)
            def _(out=out):
                pltpu.make_async_copy(obuf.at[slot], out.at[slot - group * size], osem.at[slot]).start()

    def settle(slot):
        pltpu.make_async_copy(obuf.at[slot], outs[0].at[0], osem.at[slot]).wait()

    def fetch(item, act):
        buf = lax.rem(item, BUFS)
        at = item * FIELDS
        top = pl.multiple_of(todo[at] * width, width)
        left = pl.multiple_of(todo[at + 1] * width, width)
        act(pltpu.make_async_copy(sigma.at[pl.ds(top, width), pl.ds(left, width)], sbuf.at[buf], ssem.at[buf]))

        @pl.when(todo[at + 7] == 1)
        def _():
            node, q = todo[at + 2], todo[at + 3]
            xslot = lax.rem(todo[at + 8], BUFS)
            source = panel.at[:, node // nodes, lax.rem(node, nodes), q]
            act(pltpu.make_async_copy(source, xbuf.at[xslot], xsem.at[xslot]))

    for ahead in range(BUFS - 1):
        @pl.when(begin + ahead < end)
        def _():
            fetch(begin + ahead, lambda copy: copy.start())

    def blank(item, carry):
        slot = empty[item]
        obuf[slot] = jnp.zeros(obuf.shape[1:], jnp.float32)
        put(slot)
        return carry

    lax.fori_loop(none_begin, none_end, blank, 0)

    def step(item, carry):
        buf = lax.rem(item, BUFS)

        @pl.when(item + BUFS - 1 < end)
        def _():
            fetch(item + BUFS - 1, lambda copy: copy.start())

        fetch(item, lambda copy: copy.wait())
        at = item * FIELDS
        slot = todo[at + 4]

        @pl.when(todo[at + 7] == 1)
        def _():
            high, low = split(xbuf[lax.rem(todo[at + 8], BUFS)].reshape(width, width))
            deep[:width] = high
            deep[width : 2 * width] = low
            deep[2 * width :] = high

        high, low = split(sbuf[buf])
        term = jnp.dot(
            jnp.concatenate([high, high, low], axis=1), deep[...], preferred_element_type=jnp.float32
        )

        obuf[slot] = term + jnp.where(todo[at + 5] == 1, 0.0, obuf[slot])

        @pl.when(todo[at + 6] == 1)
        def _():
            put(slot)

        return carry

    lax.fori_loop(begin, end, step, 0)

    def drain(item, carry):
        @pl.when(todo[item * FIELDS + 6] == 1)
        def _():
            settle(todo[item * FIELDS + 4])

        return carry

    lax.fori_loop(begin, end, drain, 0)

    def drain_blank(item, carry):
        settle(empty[item])
        return carry

    lax.fori_loop(none_begin, none_end, drain_blank, 0)


def local_product(plan, sigma, panel, homes, piece, size):
    rows, _, nodes, _, strip, width = panel.shape
    total = homes * size
    hbm = pl.BlockSpec(memory_space=pl.ANY)
    smem = pl.BlockSpec(memory_space=pltpu.SMEM)
    return pl.pallas_call(
        functools.partial(product_kernel, piece, nodes, homes),
        out_shape=[jax.ShapeDtypeStruct((size, width, width), jnp.float32)] * homes,
        in_specs=[smem] * 4 + [hbm, hbm],
        out_specs=[hbm] * homes,
        scratch_shapes=[
            pltpu.VMEM((BUFS, width, width), jnp.float32),
            pltpu.VMEM((BUFS, rows, strip, width), jnp.float32),
            pltpu.VMEM((3 * width, width), jnp.bfloat16),
            pltpu.VMEM((total, width, width), jnp.float32),
            pltpu.SemaphoreType.DMA((BUFS,)),
            pltpu.SemaphoreType.DMA((BUFS,)),
            pltpu.SemaphoreType.DMA((total,)),
        ],
        compiler_params=pltpu.CompilerParams(vmem_limit_bytes=50 * MIB),
        cost_estimate=pl.CostEstimate(
            flops=6 * 60 * width**3, bytes_accessed=60 * 8 * width * width, transcendentals=0
        ),
    )(*plan, sigma, panel)


def corner_kernel(sizes, own_rows, spot, own_struct, panel, whole, own, *refs):
    totals, (out, gram, xbuf, xsem) = refs[: len(sizes)], refs[len(sizes) :]
    nodes, entries = own_struct.shape
    width = whole.shape[1]
    my_row, my_col = spot[0], spot[1]

    def walk(act):
        def per_pair(pair, rank):
            node, p = pair // entries, lax.rem(pair, entries)
            mine = own_struct[node, p] // own_rows == my_row

            @pl.when(mine)
            def _():
                act(node, rank, pltpu.make_async_copy(panel.at[:, my_col, node, p], xbuf.at[rank], xsem.at[rank]))

            return rank + mine.astype(jnp.int32)

        lax.fori_loop(0, nodes * entries, per_pair, jnp.int32(0))

    walk(lambda node, slot, copy: copy.start())
    gram[...] = jnp.zeros(gram.shape, jnp.float32)

    def gather(node, slot, copy):
        copy.wait()
        left = xbuf[slot].reshape(width, width).T
        first = 0
        for total, size in zip(totals, sizes):
            @pl.when((slot >= first) & (slot < first + size))
            def _():
                gram[node] += triple_dot(left, total[slot - first])

            first += size

    walk(gather)
    for node in range(nodes):
        inverse = whole[node]
        mine = own[node]
        out[node] = triple_dot(inverse.T, triple_dot(gram[node], inverse)) + triple_dot(mine.T, mine)


def corner(spot, own_struct, panel, whole, own, totals, sizes, own_rows):
    rows, _, nodes, _, strip, width = panel.shape
    vmem = pl.BlockSpec(memory_space=pltpu.VMEM)
    smem = pl.BlockSpec(memory_space=pltpu.SMEM)
    return pl.pallas_call(
        functools.partial(corner_kernel, sizes, own_rows),
        out_shape=jax.ShapeDtypeStruct(whole.shape, jnp.float32),
        in_specs=[smem, smem, pl.BlockSpec(memory_space=pl.ANY)] + [vmem] * (2 + len(totals)),
        out_specs=vmem,
        scratch_shapes=[
            pltpu.VMEM(whole.shape, jnp.float32),
            pltpu.VMEM((sum(sizes), rows, strip, width), jnp.float32),
            pltpu.SemaphoreType.DMA((sum(sizes),)),
        ],
        compiler_params=pltpu.CompilerParams(vmem_limit_bytes=40 * MIB),
        cost_estimate=pl.CostEstimate(flops=6 * 22 * width**3, bytes_accessed=8 * MIB, transcendentals=0),
    )(spot, own_struct, panel, whole, own, *totals)


def finish_kernel(sizes, shape, holder, rank, whole, *refs):
    nodes, entries, strip, width = shape
    arrived, (off, raw) = refs[: len(sizes)], refs[len(sizes) :]
    for node in range(nodes):
        def pick(entry, carry):
            at = node * entries + entry
            first = 0
            for blocks, size in zip(arrived, sizes):
                slot = rank[at] - first

                @pl.when((slot >= 0) & (slot < size))
                def _(blocks=blocks, size=size, slot=slot):
                    raw[pl.ds(pl.multiple_of(entry * strip, strip), strip), :] = blocks[holder[at] * size + slot]

                first += size
            return carry

        lax.fori_loop(0, entries, pick, 0)
        off[node] = -triple_dot(raw[...], whole[node]).reshape(entries, strip, width)


def finish(holder, rank, shape, whole, arrived, sizes):
    nodes, entries, strip, width = shape
    vmem = pl.BlockSpec(memory_space=pltpu.VMEM)
    smem = pl.BlockSpec(memory_space=pltpu.SMEM)
    return pl.pallas_call(
        functools.partial(finish_kernel, sizes, shape),
        out_shape=jax.ShapeDtypeStruct(shape, jnp.float32),
        in_specs=[smem] * 2 + [vmem] * (1 + len(arrived)),
        out_specs=vmem,
        scratch_shapes=[pltpu.VMEM((entries * strip, width), jnp.float32)],
        compiler_params=pltpu.CompilerParams(vmem_limit_bytes=40 * MIB),
        cost_estimate=pl.CostEstimate(flops=6 * nodes * entries * strip * width**2, bytes_accessed=8 * MIB, transcendentals=0),
    )(holder, rank, whole, *arrived)


def per_device(rows, homes, sigma_anc, panel, diag_inv, structure):
    nodes, entries, strip, width = panel.shape
    own_rows, own_cols = sigma_anc.shape[0] // width, sigma_anc.shape[1] // width
    chips = homes // 2

    struct = lax.all_gather(structure, "col", axis=0, tiled=True)
    every_panel = lax.all_gather(panel, ("row", "col"), axis=0, tiled=False)
    every_panel = every_panel.reshape((rows, homes) + panel.shape)

    most = nodes * min(entries, own_rows)
    levels = sorted({min(slots, most) for slots in SLOTS + (most,)})
    holders = struct.reshape(homes, -1) // own_rows
    loads = jnp.sum(holders[:, :, None] == jnp.arange(rows, dtype=jnp.int32), axis=1)
    heaviest = jnp.max(loads)
    level = sum((heaviest > slots).astype(jnp.int32) for slots in levels[:-1])

    def pieces_of(slots):
        return slots // 2, slots - slots // 2

    my_row = lax.axis_index("row").astype(jnp.int32)
    my_col = lax.axis_index("col").astype(jnp.int32)
    chosen = jnp.asarray([pieces_of(slots) for slots in levels], jnp.int32)[level]
    spot = jnp.concatenate([jnp.stack([my_row, my_col]), chosen])
    plan = make_plan(spot, struct, most, nodes, own_rows, own_cols)

    holder = structure.reshape(-1) // own_rows
    pair = jnp.arange(nodes * entries, dtype=jnp.int32)
    earlier = (holder[:, None] == holder[None, :]) & (pair[None, :] < pair[:, None])
    rank = jnp.sum(earlier.astype(jnp.int32), axis=1)

    sibling = [(col, col ^ 1) for col in range(homes)]

    def to_rows(total):
        strips = total.reshape(-1, rows, strip, width).transpose(1, 0, 2, 3)
        landed = lax.all_to_all(strips, "row", split_axis=0, concat_axis=0, tiled=True)
        return landed.reshape(-1, strip, width)

    def between_cores(blocks):
        return [
            blocks[2 * away] + lax.ppermute(blocks[2 * away + 1], "col", sibling) for away in range(1, chips)
        ]

    def at_home(blocks):
        return blocks[0] + lax.ppermute(blocks[1], "col", sibling)

    def between_chips(sums):
        return [
            lax.ppermute(value, "col", [(col, (col + 2 * away) % homes) for col in range(homes)])
            for away, value in enumerate(sums, 1)
        ]

    def add(first, others):
        return functools.reduce(lambda left, right: left + right, others, first)

    def with_slots(slots, sigma_anc, every_panel, diag_inv, structure, spot, holder, rank, *plan):
        sizes = pieces_of(slots)
        inverse = lax.all_gather(diag_inv, "row", axis=1, tiled=True)

        early = local_product(plan, sigma_anc, every_panel, homes, 0, sizes[0])
        sums = between_cores(early)
        sums, todo = lax.optimization_barrier((sums, plan[0]))
        crossed = between_chips(sums)
        late = local_product((todo,) + plan[1:], sigma_anc, every_panel, homes, 1, sizes[1])
        late, crossed, inverse = lax.optimization_barrier((late, crossed, inverse))
        first = add(at_home(early), crossed)

        sums = between_cores(late)
        first, sums = lax.optimization_barrier((first, sums))
        landed, crossed = lax.optimization_barrier((to_rows(first), between_chips(sums)))
        second = add(at_home(late), crossed)

        part = corner(spot, structure, every_panel, inverse, diag_inv, (first, second), sizes, own_rows)
        arrived = (landed, to_rows(second))
        off = finish(holder, rank, panel.shape, inverse, arrived, sizes)
        return off, lax.psum_scatter(part, "row", scatter_dimension=1, tiled=True)

    branches = [functools.partial(with_slots, slots) for slots in levels]
    operands = (sigma_anc, every_panel, diag_inv, structure, spot, holder, rank) + tuple(plan)
    if len(branches) == 1:
        return branches[0](*operands)
    return lax.switch(level, branches, *operands)


def solution(mesh):
    placed = (
        P(("grp", "row"), "col"),
        P(("grp", "col"), None, "row", None),
        P(("grp", "col"), "row", None),
        P("col", None),
    )
    return jax.shard_map(
        functools.partial(per_device, mesh.shape["row"], mesh.shape["col"]),
        mesh=mesh,
        in_specs=placed,
        out_specs=(P(("grp", "col"), None, "row", None), P(("grp", "col"), "row", None)),
        check_vma=False,
    )
```

```python
import functools

import jax
import jax.numpy as jnp
from jax import lax
from jax.experimental import pallas as pl
from jax.experimental.pallas import tpu as pltpu
from jax.sharding import PartitionSpec as P

SLOTS = (10, 11, 12, 14)
FIRST = 3
BUFS = 12
FIELDS = 9
MIB = 1024 * 1024


def split(value):
    high = value.astype(jnp.bfloat16)
    return high, (value - high.astype(jnp.float32)).astype(jnp.bfloat16)


def triple_dot(left, right):
    left_high, left_low = split(left)
    right_high, right_low = split(right)
    dot = functools.partial(jnp.dot, preferred_element_type=jnp.float32)
    return dot(left_high, right_high) + (dot(left_high, right_low) + dot(left_low, right_high))


def plan_kernel(nodes, own_rows, own_cols, spot, struct, todo, ends, empty, empties):
    entries = struct.shape[1]
    homes = struct.shape[0] // nodes
    chips = homes // 2
    my_row, my_col = spot[0], spot[1]

    def piece_list(first, size, state):
        def per_home(home, state):
            distance = lax.rem(home // 2 - my_col // 2 + chips, chips)
            group = distance * 2 + lax.rem(home + my_col, 2)

            def per_node(member, state):
                rank, count, blocks, none = state
                node = home * nodes + member
                low = high = rank
                for p in range(entries):
                    mine = (struct[node, p] // own_rows == my_row).astype(jnp.int32)
                    high += mine
                held = high - low
                start = jnp.maximum(low, first)
                stop = jnp.minimum(high, first + size)
                columns = jnp.int32(0)
                for q in range(entries):
                    columns += (struct[node, q] // own_cols == my_col).astype(jnp.int32)

                def enlist():
                    def per_column(q, state):
                        order, count, blocks = state
                        other = struct[node, q]

                        def per_row(p, state):
                            at_rank, count = state
                            block = struct[node, p]
                            mine = block // own_rows == my_row

                            @pl.when(mine & (at_rank >= start) & (at_rank < stop))
                            def _():
                                at = count * FIELDS
                                todo[at] = block - my_row * own_rows
                                todo[at + 1] = other - my_col * own_cols
                                todo[at + 2] = node
                                todo[at + 3] = q
                                todo[at + 4] = group * size + at_rank - first
                                todo[at + 5] = (order == 0).astype(jnp.int32)
                                todo[at + 6] = (order == columns - 1).astype(jnp.int32)
                                todo[at + 7] = (at_rank == start).astype(jnp.int32)
                                todo[at + 8] = blocks

                            taken = mine & (at_rank >= start) & (at_rank < stop)
                            return at_rank + mine.astype(jnp.int32), count + taken.astype(jnp.int32)

                        def column():
                            return lax.fori_loop(0, entries, per_row, (low, count))[1]

                        hit = other // own_cols == my_col
                        count = lax.cond(hit, column, lambda: count)
                        step = hit.astype(jnp.int32)
                        return order + step, count, blocks + step

                    def all_empty():
                        def one(at_rank, none):
                            empty[none] = group * size + at_rank - first
                            return none + 1

                        return lax.fori_loop(start, stop, one, none)

                    _, more, further = lax.fori_loop(0, entries, per_column, (jnp.int32(0), count, blocks))
                    return more, further, lax.cond(columns == 0, all_empty, lambda: none)

                count, blocks, none = lax.cond(start < stop, enlist, lambda: (count, blocks, none))
                return high, count, blocks, none

            return lax.fori_loop(0, nodes, per_node, (jnp.int32(0),) + state)[1:]

        return lax.fori_loop(0, homes, per_home, state)

    count = none = jnp.int32(0)
    for piece, (first, size) in enumerate(((0, spot[2]), (spot[2], spot[3]))):
        count, _, none = piece_list(first, size, (count, jnp.int32(0), none))
        ends[piece] = count
        empties[piece] = none


def make_plan(spot, struct, most, nodes, own_rows, own_cols):
    total = struct.shape[0] // nodes * most
    smem = pl.BlockSpec(memory_space=pltpu.SMEM)
    lengths = (total * struct.shape[1] * FIELDS, 2, total, 2)
    return pl.pallas_call(
        functools.partial(plan_kernel, nodes, own_rows, own_cols),
        out_shape=[jax.ShapeDtypeStruct((length,), jnp.int32) for length in lengths],
        in_specs=[smem, smem],
        out_specs=[smem] * 4,
    )(spot, struct)


def product_kernel(part, sizes, nodes, homes, todo, ends, empty, empties, sigma, panel, *refs):
    outs = refs[: homes * len(sizes)]
    sbuf, xbuf, deep, obuf, ssem, xsem, osem = refs[homes * len(sizes) :]
    width = sbuf.shape[1]
    slots = sum(sizes)
    begin = ends[part - 1] if part else 0
    end = ends[part]
    none_begin = empties[part - 1] if part else 0
    none_end = empties[part]

    def put(slot):
        group = slot // slots
        inside = slot - group * slots
        first = 0
        for piece, size in enumerate(sizes):
            @pl.when((inside >= first) & (inside < first + size))
            def _(piece=piece, first=first):
                for other in range(homes):
                    @pl.when(group == other)
                    def _(out=outs[piece * homes + other]):
                        pltpu.make_async_copy(obuf.at[slot], out.at[inside - first], osem.at[slot]).start()

            first += size

    def settle(slot):
        pltpu.make_async_copy(obuf.at[slot], outs[0].at[0], osem.at[slot]).wait()

    def fetch(item, act):
        buf = lax.rem(item, BUFS)
        at = item * FIELDS
        top = pl.multiple_of(todo[at] * width, width)
        left = pl.multiple_of(todo[at + 1] * width, width)
        act(pltpu.make_async_copy(sigma.at[pl.ds(top, width), pl.ds(left, width)], sbuf.at[buf], ssem.at[buf]))

        @pl.when(todo[at + 7] == 1)
        def _():
            node, q = todo[at + 2], todo[at + 3]
            xslot = lax.rem(todo[at + 8], BUFS)
            source = panel.at[:, node // nodes, lax.rem(node, nodes), q]
            act(pltpu.make_async_copy(source, xbuf.at[xslot], xsem.at[xslot]))

    for ahead in range(BUFS - 2):
        @pl.when(begin + ahead < end)
        def _():
            fetch(begin + ahead, lambda copy: copy.start())

    def blank(item, carry):
        slot = empty[item]
        obuf[slot] = jnp.zeros(obuf.shape[1:], jnp.float32)
        put(slot)
        return carry

    lax.fori_loop(none_begin, none_end, blank, 0)

    def ready(item):
        @pl.when(item + BUFS - 2 < end)
        def _():
            fetch(item + BUFS - 2, lambda copy: copy.start())

        fetch(item, lambda copy: copy.wait())
        at = item * FIELDS

        @pl.when(todo[at + 7] == 1)
        def _():
            turn = lax.rem(todo[at + 8], 2)
            high, low = split(xbuf[lax.rem(todo[at + 8], BUFS)].reshape(width, width))
            deep[turn, :width] = high
            deep[turn, width : 2 * width] = low
            deep[turn, 2 * width :] = high

    def multiply(item):
        high, low = split(sbuf[lax.rem(item, BUFS)])
        return jnp.dot(
            jnp.concatenate([high, high, low], axis=1),
            deep[lax.rem(todo[item * FIELDS + 8], 2)],
            preferred_element_type=jnp.float32,
        )

    def keep(item, term):
        at = item * FIELDS
        slot = todo[at + 4]
        obuf[slot] = term + jnp.where(todo[at + 5] == 1, 0.0, obuf[slot])

    def send(item):
        @pl.when(todo[item * FIELDS + 6] == 1)
        def _():
            put(todo[item * FIELDS + 4])

    def two(pair, carry):
        item = begin + 2 * pair
        ready(item)
        ready(item + 1)
        one, other = multiply(item), multiply(item + 1)
        keep(item, one)
        keep(item + 1, other)
        send(item)
        send(item + 1)
        return carry

    lax.fori_loop(0, (end - begin) // 2, two, 0)

    @pl.when(lax.rem(end - begin, 2) == 1)
    def _():
        ready(end - 1)
        keep(end - 1, multiply(end - 1))
        send(end - 1)

    def drain(item, carry):
        @pl.when(todo[item * FIELDS + 6] == 1)
        def _():
            settle(todo[item * FIELDS + 4])

        return carry

    lax.fori_loop(begin, end, drain, 0)

    def drain_blank(item, carry):
        settle(empty[item])
        return carry

    lax.fori_loop(none_begin, none_end, drain_blank, 0)


def local_product(plan, sigma, panel, homes, part, sizes):
    rows, _, nodes, _, strip, width = panel.shape
    total = homes * sum(sizes)
    hbm = pl.BlockSpec(memory_space=pl.ANY)
    smem = pl.BlockSpec(memory_space=pltpu.SMEM)
    return pl.pallas_call(
        functools.partial(product_kernel, part, sizes, nodes, homes),
        out_shape=[jax.ShapeDtypeStruct((size, width, width), jnp.float32) for size in sizes for _ in range(homes)],
        in_specs=[smem] * 4 + [hbm, hbm],
        out_specs=[hbm] * (homes * len(sizes)),
        scratch_shapes=[
            pltpu.VMEM((BUFS, width, width), jnp.float32),
            pltpu.VMEM((BUFS, rows, strip, width), jnp.float32),
            pltpu.VMEM((2, 3 * width, width), jnp.bfloat16),
            pltpu.VMEM((total, width, width), jnp.float32),
            pltpu.SemaphoreType.DMA((BUFS,)),
            pltpu.SemaphoreType.DMA((BUFS,)),
            pltpu.SemaphoreType.DMA((total,)),
        ],
        compiler_params=pltpu.CompilerParams(vmem_limit_bytes=50 * MIB),
        cost_estimate=pl.CostEstimate(
            flops=6 * 60 * width**3, bytes_accessed=60 * 8 * width * width, transcendentals=0
        ),
    )(*plan, sigma, panel)


def corner_kernel(base, sizes, own_rows, spot, own_struct, panel, *refs):
    totals, refs = refs[: len(sizes)], refs[len(sizes) :]
    if base:
        before, whole, own, out, gram, xbuf, xsem = refs
    else:
        gram, xbuf, xsem = refs
    nodes, entries = own_struct.shape
    width = gram.shape[1]
    my_row, my_col = spot[0], spot[1]
    slots = sum(sizes)

    def walk(act):
        def per_pair(pair, rank):
            node, p = pair // entries, lax.rem(pair, entries)
            mine = own_struct[node, p] // own_rows == my_row
            slot = rank - base

            @pl.when(mine & (slot >= 0) & (slot < slots))
            def _():
                act(node, slot, pltpu.make_async_copy(panel.at[:, my_col, node, p], xbuf.at[slot], xsem.at[slot]))

            return rank + mine.astype(jnp.int32)

        lax.fori_loop(0, nodes * entries, per_pair, jnp.int32(0))

    walk(lambda node, slot, copy: copy.start())
    gram[...] = before[...] if base else jnp.zeros(gram.shape, jnp.float32)

    def gather(node, slot, copy):
        copy.wait()
        left = xbuf[slot].reshape(width, width).T
        first = 0
        for total, size in zip(totals, sizes):
            @pl.when((slot >= first) & (slot < first + size))
            def _(total=total, first=first):
                gram[node] += triple_dot(left, total[slot - first])

            first += size

    walk(gather)
    if base:
        for node in range(nodes):
            inverse, mine = whole[node], own[node]
            out[node] = triple_dot(inverse.T, triple_dot(gram[node], inverse)) + triple_dot(mine.T, mine)


def corner(spot, own_struct, panel, totals, base, sizes, own_rows, *ending):
    rows, _, nodes, _, strip, width = panel.shape
    vmem = pl.BlockSpec(memory_space=pltpu.VMEM)
    smem = pl.BlockSpec(memory_space=pltpu.SMEM)
    blocks = (nodes, width, width)
    return pl.pallas_call(
        functools.partial(corner_kernel, base, sizes, own_rows),
        out_shape=jax.ShapeDtypeStruct(blocks, jnp.float32),
        in_specs=[smem, smem, pl.BlockSpec(memory_space=pl.ANY)] + [vmem] * (len(totals) + len(ending)),
        out_specs=vmem,
        scratch_shapes=([pltpu.VMEM(blocks, jnp.float32)] if base else [])
        + [
            pltpu.VMEM((sum(sizes), rows, strip, width), jnp.float32),
            pltpu.SemaphoreType.DMA((sum(sizes),)),
        ],
        compiler_params=pltpu.CompilerParams(vmem_limit_bytes=50 * MIB),
        cost_estimate=pl.CostEstimate(flops=6 * 8 * width**3, bytes_accessed=8 * MIB, transcendentals=0),
    )(spot, own_struct, panel, *totals, *ending)


def finish_kernel(sizes, shape, rows, holder, rank, whole, *refs):
    nodes, entries, strip, width = shape
    arrived, (off, diag, raw) = refs[: len(sizes)], refs[len(sizes) :]
    for node in range(nodes):
        def pick(entry, carry):
            at = node * entries + entry
            first = 0
            for blocks, size in zip(arrived, sizes):
                slot = rank[at] - first
                stride = blocks.shape[0] // rows

                @pl.when((slot >= 0) & (slot < size))
                def _(blocks=blocks, stride=stride, slot=slot):
                    raw[pl.ds(pl.multiple_of(entry * strip, strip), strip), :] = blocks[holder[at] * stride + slot]

                first += size
            return carry

        lax.fori_loop(0, entries, pick, 0)
        off[node] = -triple_dot(raw[...], whole[node]).reshape(entries, strip, width)
        stride = sizes[-1] + nodes
        parts = [arrived[-1][row * stride + sizes[-1] + node] for row in range(rows)]
        diag[node] = functools.reduce(lambda left, right: left + right, parts)


def finish(holder, rank, shape, rows, whole, arrived, sizes):
    nodes, entries, strip, width = shape
    vmem = pl.BlockSpec(memory_space=pltpu.VMEM)
    smem = pl.BlockSpec(memory_space=pltpu.SMEM)
    return pl.pallas_call(
        functools.partial(finish_kernel, sizes, shape, rows),
        out_shape=[
            jax.ShapeDtypeStruct(shape, jnp.float32),
            jax.ShapeDtypeStruct((nodes, strip, width), jnp.float32),
        ],
        in_specs=[smem] * 2 + [vmem] * (1 + len(arrived)),
        out_specs=[vmem, vmem],
        scratch_shapes=[pltpu.VMEM((entries * strip, width), jnp.float32)],
        compiler_params=pltpu.CompilerParams(vmem_limit_bytes=50 * MIB),
        cost_estimate=pl.CostEstimate(flops=6 * nodes * entries * strip * width**2, bytes_accessed=8 * MIB, transcendentals=0),
    )(holder, rank, whole, *arrived)


def per_device(rows, homes, sigma_anc, panel, diag_inv, structure):
    nodes, entries, strip, width = panel.shape
    own_rows, own_cols = sigma_anc.shape[0] // width, sigma_anc.shape[1] // width
    chips = homes // 2

    struct = lax.all_gather(structure, "col", axis=0, tiled=True)
    every_panel = lax.all_gather(panel, ("row", "col"), axis=0, tiled=False)
    every_panel = every_panel.reshape((rows, homes) + panel.shape)

    most = nodes * min(entries, own_rows)
    levels = sorted({min(slots, most) for slots in SLOTS + (most,)})
    holders = struct.reshape(homes, -1) // own_rows
    loads = jnp.sum(holders[:, :, None] == jnp.arange(rows, dtype=jnp.int32), axis=1)
    heaviest = jnp.max(loads)
    level = sum((heaviest > slots).astype(jnp.int32) for slots in levels[:-1])

    def pieces_of(slots):
        first = min(FIRST, slots - 2)
        last = (slots - first) // 2
        return first, slots - first - last, last

    my_row = lax.axis_index("row").astype(jnp.int32)
    my_col = lax.axis_index("col").astype(jnp.int32)
    chosen = jnp.asarray([(pieces_of(slots)[0], slots - pieces_of(slots)[0]) for slots in levels], jnp.int32)[level]
    spot = jnp.concatenate([jnp.stack([my_row, my_col]), chosen])
    plan = make_plan(spot, struct, most, nodes, own_rows, own_cols)

    holder = structure.reshape(-1) // own_rows
    pair = jnp.arange(nodes * entries, dtype=jnp.int32)
    earlier = (holder[:, None] == holder[None, :]) & (pair[None, :] < pair[:, None])
    rank = jnp.sum(earlier.astype(jnp.int32), axis=1)

    sibling = [(col, col ^ 1) for col in range(homes)]

    def to_rows(total):
        strips = total.reshape(-1, rows, strip, width).transpose(1, 0, 2, 3)
        landed = lax.all_to_all(strips, "row", split_axis=0, concat_axis=0, tiled=True)
        return landed.reshape(-1, strip, width)

    def between_cores(blocks):
        return [
            blocks[2 * away] + lax.ppermute(blocks[2 * away + 1], "col", sibling) for away in range(1, chips)
        ]

    def at_home(blocks):
        return blocks[0] + lax.ppermute(blocks[1], "col", sibling)

    def between_chips(sums):
        return [
            lax.ppermute(value, "col", [(col, (col + 2 * away) % homes) for col in range(homes)])
            for away, value in enumerate(sums, 1)
        ]

    def add(first, others):
        return functools.reduce(lambda left, right: left + right, others, first)

    def with_slots(slots, sigma_anc, every_panel, diag_inv, structure, spot, holder, rank, *plan):
        sizes = pieces_of(slots)
        inverse = lax.all_gather(diag_inv, "row", axis=1, tiled=True)

        early = local_product(plan, sigma_anc, every_panel, homes, 0, sizes[:1])
        sums = between_cores(early)
        sums, todo = lax.optimization_barrier((sums, plan[0]))
        crossed = between_chips(sums)
        late = local_product((todo,) + plan[1:], sigma_anc, every_panel, homes, 1, sizes[1:])
        late, crossed = lax.optimization_barrier((late, crossed))
        first = add(at_home(early), crossed)

        sums = between_cores(late[:homes])
        first, sums = lax.optimization_barrier((first, sums))
        landed, crossed, inverse = lax.optimization_barrier((to_rows(first), between_chips(sums), inverse))
        arrived = [landed]
        second = add(at_home(late[:homes]), crossed)

        sums = between_cores(late[homes:])
        second, sums = lax.optimization_barrier((second, sums))
        gram = corner(spot, structure, every_panel, (first, second), 0, sizes[:2], own_rows)
        landed, crossed, gram = lax.optimization_barrier((to_rows(second), between_chips(sums), gram))
        arrived.append(landed)
        third = add(at_home(late[homes:]), crossed)

        part = corner(
            spot, structure, every_panel, (third,), sum(sizes[:2]), sizes[2:], own_rows, gram, inverse, diag_inv
        )
        arrived.append(to_rows(jnp.concatenate([third, part], axis=0)))
        return tuple(finish(holder, rank, panel.shape, rows, inverse, arrived, sizes))

    branches = [functools.partial(with_slots, slots) for slots in levels]
    operands = (sigma_anc, every_panel, diag_inv, structure, spot, holder, rank) + tuple(plan)
    if len(branches) == 1:
        return branches[0](*operands)
    return lax.switch(level, branches, *operands)


def solution(mesh):
    placed = (
        P(("grp", "row"), "col"),
        P(("grp", "col"), None, "row", None),
        P(("grp", "col"), "row", None),
        P("col", None),
    )
    return jax.shard_map(
        functools.partial(per_device, mesh.shape["row"], mesh.shape["col"]),
        mesh=mesh,
        in_specs=placed,
        out_specs=(P(("grp", "col"), None, "row", None), P(("grp", "col"), "row", None)),
        check_vma=False,
    )
```

```python
import functools

import jax
import jax.numpy as jnp
from jax import lax
from jax.experimental import pallas as pl
from jax.experimental.pallas import tpu as pltpu
from jax.sharding import PartitionSpec as P

SLOTS = (9, 10, 11, 12, 13, 15)
BUFS = 12
FIELDS = 9
MIB = 1024 * 1024


def triple_dot(left, right):
    return jnp.dot(left, right, precision=lax.Precision.HIGH, preferred_element_type=jnp.float32)


def plan_kernel(nodes, own_rows, own_cols, spot, struct, todo, ends, empty, empties):
    entries = struct.shape[1]
    homes = struct.shape[0] // nodes
    chips = homes // 2
    my_row, my_col = spot[0], spot[1]

    def piece_list(first, size, state):
        def per_home(home, state):
            distance = lax.rem(home // 2 - my_col // 2 + chips, chips)
            group = distance * 2 + lax.rem(home + my_col, 2)

            def per_node(member, state):
                rank, count, blocks, none = state
                node = home * nodes + member
                low = high = rank
                for p in range(entries):
                    mine = (struct[node, p] // own_rows == my_row).astype(jnp.int32)
                    high += mine
                held = high - low
                start = jnp.maximum(low, first)
                stop = jnp.minimum(high, first + size)
                columns = jnp.int32(0)
                for q in range(entries):
                    columns += (struct[node, q] // own_cols == my_col).astype(jnp.int32)

                def enlist():
                    def per_column(q, state):
                        order, count, blocks = state
                        other = struct[node, q]

                        def per_row(p, state):
                            at_rank, count = state
                            block = struct[node, p]
                            mine = block // own_rows == my_row

                            @pl.when(mine & (at_rank >= start) & (at_rank < stop))
                            def _():
                                at = count * FIELDS
                                todo[at] = block - my_row * own_rows
                                todo[at + 1] = other - my_col * own_cols
                                todo[at + 2] = node
                                todo[at + 3] = q
                                todo[at + 4] = group * size + at_rank - first
                                todo[at + 5] = (order == 0).astype(jnp.int32)
                                todo[at + 6] = (order == columns - 1).astype(jnp.int32)
                                todo[at + 7] = (at_rank == start).astype(jnp.int32)
                                todo[at + 8] = blocks

                            taken = mine & (at_rank >= start) & (at_rank < stop)
                            return at_rank + mine.astype(jnp.int32), count + taken.astype(jnp.int32)

                        def column():
                            return lax.fori_loop(0, entries, per_row, (low, count))[1]

                        hit = other // own_cols == my_col
                        count = lax.cond(hit, column, lambda: count)
                        step = hit.astype(jnp.int32)
                        return order + step, count, blocks + step

                    def all_empty():
                        def one(at_rank, none):
                            empty[none] = group * size + at_rank - first
                            return none + 1

                        return lax.fori_loop(start, stop, one, none)

                    _, more, further = lax.fori_loop(0, entries, per_column, (jnp.int32(0), count, blocks))
                    return more, further, lax.cond(columns == 0, all_empty, lambda: none)

                count, blocks, none = lax.cond(start < stop, enlist, lambda: (count, blocks, none))
                return high, count, blocks, none

            return lax.fori_loop(0, nodes, per_node, (jnp.int32(0),) + state)[1:]

        return lax.fori_loop(0, homes, per_home, state)

    count = none = jnp.int32(0)
    for piece, (first, size) in enumerate(((0, spot[2]), (spot[2], spot[3]))):
        count, _, none = piece_list(first, size, (count, jnp.int32(0), none))
        ends[piece] = count
        empties[piece] = none


def make_plan(spot, struct, most, nodes, own_rows, own_cols):
    total = struct.shape[0] // nodes * most
    smem = pl.BlockSpec(memory_space=pltpu.SMEM)
    lengths = (total * struct.shape[1] * FIELDS, 2, total, 2)
    return pl.pallas_call(
        functools.partial(plan_kernel, nodes, own_rows, own_cols),
        out_shape=[jax.ShapeDtypeStruct((length,), jnp.int32) for length in lengths],
        in_specs=[smem, smem],
        out_specs=[smem] * 4,
    )(spot, struct)


def product_kernel(part, sizes, nodes, homes, todo, ends, empty, empties, sigma, panel, *refs):
    outs = refs[: homes * len(sizes)]
    sbuf, xbuf, obuf, ssem, xsem, osem = refs[homes * len(sizes) :]
    width = sbuf.shape[1]
    slots = sum(sizes)
    begin = ends[part - 1] if part else 0
    end = ends[part]
    none_begin = empties[part - 1] if part else 0
    none_end = empties[part]

    def put(slot):
        group = slot // slots
        inside = slot - group * slots
        first = 0
        for piece, size in enumerate(sizes):
            @pl.when((inside >= first) & (inside < first + size))
            def _(piece=piece, first=first):
                for other in range(homes):
                    @pl.when(group == other)
                    def _(out=outs[piece * homes + other]):
                        pltpu.make_async_copy(obuf.at[slot], out.at[inside - first], osem.at[slot]).start()

            first += size

    def settle(slot):
        pltpu.make_async_copy(obuf.at[slot], outs[0].at[0], osem.at[slot]).wait()

    def fetch(item, act):
        buf = lax.rem(item, BUFS)
        at = item * FIELDS
        top = pl.multiple_of(todo[at] * width, width)
        left = pl.multiple_of(todo[at + 1] * width, width)
        act(pltpu.make_async_copy(sigma.at[pl.ds(top, width), pl.ds(left, width)], sbuf.at[buf], ssem.at[buf]))

        @pl.when(todo[at + 7] == 1)
        def _():
            node, q = todo[at + 2], todo[at + 3]
            xslot = lax.rem(todo[at + 8], BUFS)
            source = panel.at[:, node // nodes, lax.rem(node, nodes), q]
            act(pltpu.make_async_copy(source, xbuf.at[xslot], xsem.at[xslot]))

    for ahead in range(BUFS - 2):
        @pl.when(begin + ahead < end)
        def _():
            fetch(begin + ahead, lambda copy: copy.start())

    def blank(item, carry):
        slot = empty[item]
        obuf[slot] = jnp.zeros(obuf.shape[1:], jnp.float32)
        put(slot)
        return carry

    lax.fori_loop(none_begin, none_end, blank, 0)

    def step(item, carry):
        @pl.when(item + BUFS - 2 < end)
        def _():
            fetch(item + BUFS - 2, lambda copy: copy.start())

        fetch(item, lambda copy: copy.wait())
        at = item * FIELDS
        slot = todo[at + 4]
        term = triple_dot(sbuf[lax.rem(item, BUFS)], xbuf[lax.rem(todo[at + 8], BUFS)].reshape(width, width))
        obuf[slot] = term + jnp.where(todo[at + 5] == 1, 0.0, obuf[slot])

        @pl.when(todo[at + 6] == 1)
        def _():
            put(slot)

        return carry

    lax.fori_loop(begin, end, step, 0)

    def drain(item, carry):
        @pl.when(todo[item * FIELDS + 6] == 1)
        def _():
            settle(todo[item * FIELDS + 4])

        return carry

    lax.fori_loop(begin, end, drain, 0)

    def drain_blank(item, carry):
        settle(empty[item])
        return carry

    lax.fori_loop(none_begin, none_end, drain_blank, 0)


def local_product(plan, sigma, panel, homes, part, sizes):
    rows, _, nodes, _, strip, width = panel.shape
    total = homes * sum(sizes)
    hbm = pl.BlockSpec(memory_space=pl.ANY)
    smem = pl.BlockSpec(memory_space=pltpu.SMEM)
    return pl.pallas_call(
        functools.partial(product_kernel, part, sizes, nodes, homes),
        out_shape=[jax.ShapeDtypeStruct((size, width, width), jnp.float32) for size in sizes for _ in range(homes)],
        in_specs=[smem] * 4 + [hbm, hbm],
        out_specs=[hbm] * (homes * len(sizes)),
        scratch_shapes=[
            pltpu.VMEM((BUFS, width, width), jnp.float32),
            pltpu.VMEM((BUFS, rows, strip, width), jnp.float32),
            pltpu.VMEM((total, width, width), jnp.float32),
            pltpu.SemaphoreType.DMA((BUFS,)),
            pltpu.SemaphoreType.DMA((BUFS,)),
            pltpu.SemaphoreType.DMA((total,)),
        ],
        compiler_params=pltpu.CompilerParams(vmem_limit_bytes=50 * MIB),
        cost_estimate=pl.CostEstimate(flops=width, bytes_accessed=width, transcendentals=0),
    )(*plan, sigma, panel)


def corner_kernel(base, sizes, own_rows, spot, own_struct, panel, *refs):
    totals, refs = refs[: len(sizes)], refs[len(sizes) :]
    if base:
        before, whole, own, out, gram, xbuf, xsem = refs
    else:
        gram, xbuf, xsem = refs
    nodes, entries = own_struct.shape
    width = gram.shape[1]
    my_row, my_col = spot[0], spot[1]
    slots = sum(sizes)

    def walk(act):
        def per_pair(pair, rank):
            node, p = pair // entries, lax.rem(pair, entries)
            mine = own_struct[node, p] // own_rows == my_row
            slot = rank - base

            @pl.when(mine & (slot >= 0) & (slot < slots))
            def _():
                act(node, slot, pltpu.make_async_copy(panel.at[:, my_col, node, p], xbuf.at[slot], xsem.at[slot]))

            return rank + mine.astype(jnp.int32)

        lax.fori_loop(0, nodes * entries, per_pair, jnp.int32(0))

    walk(lambda node, slot, copy: copy.start())
    gram[...] = before[...] if base else jnp.zeros(gram.shape, jnp.float32)

    def gather(node, slot, copy):
        copy.wait()
        left = xbuf[slot].reshape(width, width).T
        first = 0
        for total, size in zip(totals, sizes):
            @pl.when((slot >= first) & (slot < first + size))
            def _(total=total, first=first):
                gram[node] += triple_dot(left, total[slot - first])

            first += size

    walk(gather)
    if base:
        for node in range(nodes):
            inverse, mine = whole[node], own[node]
            out[node] = triple_dot(inverse.T, triple_dot(gram[node], inverse)) + triple_dot(mine.T, mine)


def corner(spot, own_struct, panel, totals, base, sizes, own_rows, *ending):
    rows, _, nodes, _, strip, width = panel.shape
    vmem = pl.BlockSpec(memory_space=pltpu.VMEM)
    smem = pl.BlockSpec(memory_space=pltpu.SMEM)
    blocks = (nodes, width, width)
    return pl.pallas_call(
        functools.partial(corner_kernel, base, sizes, own_rows),
        out_shape=jax.ShapeDtypeStruct(blocks, jnp.float32),
        in_specs=[smem, smem, pl.BlockSpec(memory_space=pl.ANY)] + [vmem] * (len(totals) + len(ending)),
        out_specs=vmem,
        scratch_shapes=([pltpu.VMEM(blocks, jnp.float32)] if base else [])
        + [
            pltpu.VMEM((sum(sizes), rows, strip, width), jnp.float32),
            pltpu.SemaphoreType.DMA((sum(sizes),)),
        ],
        compiler_params=pltpu.CompilerParams(vmem_limit_bytes=50 * MIB),
        cost_estimate=pl.CostEstimate(flops=6 * 8 * width**3, bytes_accessed=8 * MIB, transcendentals=0),
    )(spot, own_struct, panel, *totals, *ending)


def finish_kernel(sizes, shape, holder, rank, whole, *refs):
    nodes, entries, strip, width = shape
    arrived, (off, raw) = refs[: len(sizes)], refs[len(sizes) :]
    for node in range(nodes):
        def pick(entry, carry):
            at = node * entries + entry
            first = 0
            for blocks, size in zip(arrived, sizes):
                slot = rank[at] - first

                @pl.when((slot >= 0) & (slot < size))
                def _(blocks=blocks, size=size, slot=slot):
                    raw[pl.ds(pl.multiple_of(entry * strip, strip), strip), :] = blocks[holder[at] * size + slot]

                first += size
            return carry

        lax.fori_loop(0, entries, pick, 0)
        off[node] = -triple_dot(raw[...], whole[node]).reshape(entries, strip, width)


def finish(holder, rank, shape, whole, arrived, sizes):
    nodes, entries, strip, width = shape
    vmem = pl.BlockSpec(memory_space=pltpu.VMEM)
    smem = pl.BlockSpec(memory_space=pltpu.SMEM)
    return pl.pallas_call(
        functools.partial(finish_kernel, sizes, shape),
        out_shape=jax.ShapeDtypeStruct(shape, jnp.float32),
        in_specs=[smem] * 2 + [vmem] * (1 + len(arrived)),
        out_specs=vmem,
        scratch_shapes=[pltpu.VMEM((entries * strip, width), jnp.float32)],
        compiler_params=pltpu.CompilerParams(vmem_limit_bytes=50 * MIB),
        cost_estimate=pl.CostEstimate(flops=6 * nodes * entries * strip * width**2, bytes_accessed=8 * MIB, transcendentals=0),
    )(holder, rank, whole, *arrived)


def per_device(rows, homes, sigma_anc, panel, diag_inv, structure):
    nodes, entries, strip, width = panel.shape
    own_rows, own_cols = sigma_anc.shape[0] // width, sigma_anc.shape[1] // width
    chips = homes // 2

    struct = lax.all_gather(structure, "col", axis=0, tiled=True)
    every_panel = lax.all_gather(panel, ("row", "col"), axis=0, tiled=False)
    every_panel = every_panel.reshape((rows, homes) + panel.shape)

    most = nodes * min(entries, own_rows)
    levels = sorted({min(slots, most) for slots in SLOTS + (most,)})
    holders = struct.reshape(homes, -1) // own_rows
    loads = jnp.sum(holders[:, :, None] == jnp.arange(rows, dtype=jnp.int32), axis=1)
    heaviest = jnp.max(loads)
    level = sum((heaviest > slots).astype(jnp.int32) for slots in levels[:-1])

    def pieces_of(slots):
        return slots // 2, slots - slots // 2

    my_row = lax.axis_index("row").astype(jnp.int32)
    my_col = lax.axis_index("col").astype(jnp.int32)
    chosen = jnp.asarray([pieces_of(slots) for slots in levels], jnp.int32)[level]
    spot = jnp.concatenate([jnp.stack([my_row, my_col]), chosen])
    plan = make_plan(spot, struct, most, nodes, own_rows, own_cols)

    holder = structure.reshape(-1) // own_rows
    pair = jnp.arange(nodes * entries, dtype=jnp.int32)
    earlier = (holder[:, None] == holder[None, :]) & (pair[None, :] < pair[:, None])
    rank = jnp.sum(earlier.astype(jnp.int32), axis=1)

    sibling = [(col, col ^ 1) for col in range(homes)]

    def to_rows(total):
        strips = total.reshape(-1, rows, strip, width).transpose(1, 0, 2, 3)
        landed = lax.all_to_all(strips, "row", split_axis=0, concat_axis=0, tiled=True)
        return landed.reshape(-1, strip, width)

    def between_cores(blocks):
        return [
            blocks[2 * away] + lax.ppermute(blocks[2 * away + 1], "col", sibling) for away in range(1, chips)
        ]

    def at_home(blocks):
        return blocks[0] + lax.ppermute(blocks[1], "col", sibling)

    def between_chips(sums):
        return [
            lax.ppermute(value, "col", [(col, (col + 2 * away) % homes) for col in range(homes)])
            for away, value in enumerate(sums, 1)
        ]

    def add(first, others):
        return functools.reduce(lambda left, right: left + right, others, first)

    def with_slots(slots, sigma_anc, every_panel, diag_inv, structure, spot, holder, rank, *plan):
        sizes = pieces_of(slots)
        inverse = lax.all_gather(diag_inv, "row", axis=1, tiled=True)

        early = local_product(plan, sigma_anc, every_panel, homes, 0, sizes[:1])
        sums = between_cores(early)
        sums, todo = lax.optimization_barrier((sums, plan[0]))
        crossed = between_chips(sums)
        late = local_product((todo,) + plan[1:], sigma_anc, every_panel, homes, 1, sizes[1:])
        sums = between_cores(late)
        sums, crossed, inverse = lax.optimization_barrier((sums, crossed, inverse))

        first = add(at_home(early), crossed)
        gram = corner(spot, structure, every_panel, (first,), 0, sizes[:1], own_rows)
        second = add(at_home(late), between_chips(sums))
        landed = to_rows(first)
        second, gram = lax.optimization_barrier((second, gram))

        part = corner(spot, structure, every_panel, (second,), sizes[0], sizes[1:], own_rows, gram, inverse, diag_inv)
        off = finish(holder, rank, panel.shape, inverse, (landed, to_rows(second)), sizes)
        return off, lax.psum_scatter(part, "row", scatter_dimension=1, tiled=True)

    branches = [functools.partial(with_slots, slots) for slots in levels]
    operands = (sigma_anc, every_panel, diag_inv, structure, spot, holder, rank) + tuple(plan)
    if len(branches) == 1:
        return branches[0](*operands)
    return lax.switch(level, branches, *operands)


def solution(mesh):
    placed = (
        P(("grp", "row"), "col"),
        P(("grp", "col"), None, "row", None),
        P(("grp", "col"), "row", None),
        P("col", None),
    )
    return jax.shard_map(
        functools.partial(per_device, mesh.shape["row"], mesh.shape["col"]),
        mesh=mesh,
        in_specs=placed,
        out_specs=(P(("grp", "col"), None, "row", None), P(("grp", "col"), "row", None)),
        check_vma=False,
    )
```

```python
import functools

import jax
import jax.numpy as jnp
from jax import lax
from jax.experimental import pallas as pl
from jax.experimental.pallas import tpu as pltpu
from jax.sharding import PartitionSpec as P

SLOTS = (9, 10, 11, 12, 13, 15)
USUAL = 10.4
BUFS = 12
FIELDS = 9
MIB = 1024 * 1024


def split(value):
    high = value.astype(jnp.bfloat16)
    return high, (value - high.astype(jnp.float32)).astype(jnp.bfloat16)


def triple_dot(left, right):
    left_high, left_low = split(left)
    right_high, right_low = split(right)
    dot = functools.partial(jnp.dot, preferred_element_type=jnp.float32)
    return dot(left_high, right_high) + (dot(left_high, right_low) + dot(left_low, right_high))


def plan_kernel(nodes, own_rows, own_cols, spot, struct, todo, ends, empty, empties):
    entries = struct.shape[1]
    homes = struct.shape[0] // nodes
    chips = homes // 2
    my_row, my_col = spot[0], spot[1]

    def piece_list(first, size, state):
        def per_home(home, state):
            distance = lax.rem(home // 2 - my_col // 2 + chips, chips)
            group = distance * 2 + lax.rem(home + my_col, 2)

            def per_node(member, state):
                rank, count, blocks, none = state
                node = home * nodes + member
                low = high = rank
                for p in range(entries):
                    mine = (struct[node, p] // own_rows == my_row).astype(jnp.int32)
                    high += mine
                held = high - low
                start = jnp.maximum(low, first)
                stop = jnp.minimum(high, first + size)
                columns = jnp.int32(0)
                for q in range(entries):
                    columns += (struct[node, q] // own_cols == my_col).astype(jnp.int32)

                def enlist():
                    def per_column(q, state):
                        order, count, blocks = state
                        other = struct[node, q]

                        def per_row(p, state):
                            at_rank, count = state
                            block = struct[node, p]
                            mine = block // own_rows == my_row

                            @pl.when(mine & (at_rank >= start) & (at_rank < stop))
                            def _():
                                at = count * FIELDS
                                todo[at] = block - my_row * own_rows
                                todo[at + 1] = other - my_col * own_cols
                                todo[at + 2] = node
                                todo[at + 3] = q
                                todo[at + 4] = group * size + at_rank - first
                                todo[at + 5] = (order == 0).astype(jnp.int32)
                                todo[at + 6] = (order == columns - 1).astype(jnp.int32)
                                todo[at + 7] = (at_rank == start).astype(jnp.int32)
                                todo[at + 8] = blocks

                            taken = mine & (at_rank >= start) & (at_rank < stop)
                            return at_rank + mine.astype(jnp.int32), count + taken.astype(jnp.int32)

                        def column():
                            return lax.fori_loop(0, entries, per_row, (low, count))[1]

                        hit = other // own_cols == my_col
                        count = lax.cond(hit, column, lambda: count)
                        step = hit.astype(jnp.int32)
                        return order + step, count, blocks + step

                    def all_empty():
                        def one(at_rank, none):
                            empty[none] = group * size + at_rank - first
                            return none + 1

                        return lax.fori_loop(start, stop, one, none)

                    _, more, further = lax.fori_loop(0, entries, per_column, (jnp.int32(0), count, blocks))
                    return more, further, lax.cond(columns == 0, all_empty, lambda: none)

                count, blocks, none = lax.cond(start < stop, enlist, lambda: (count, blocks, none))
                return high, count, blocks, none

            return lax.fori_loop(0, nodes, per_node, (jnp.int32(0),) + state)[1:]

        return lax.fori_loop(0, homes, per_home, state)

    count = none = jnp.int32(0)
    for piece, (first, size) in enumerate(((0, spot[2]), (spot[2], spot[3]))):
        count, _, none = piece_list(first, size, (count, jnp.int32(0), none))
        ends[piece] = count
        empties[piece] = none


def make_plan(spot, struct, most, nodes, own_rows, own_cols):
    total = struct.shape[0] // nodes * most
    smem = pl.BlockSpec(memory_space=pltpu.SMEM)
    lengths = (total * struct.shape[1] * FIELDS, 2, total, 2)
    return pl.pallas_call(
        functools.partial(plan_kernel, nodes, own_rows, own_cols),
        out_shape=[jax.ShapeDtypeStruct((length,), jnp.int32) for length in lengths],
        in_specs=[smem, smem],
        out_specs=[smem] * 4,
    )(spot, struct)


def product_kernel(part, sizes, nodes, homes, todo, ends, empty, empties, sigma, panel, *refs):
    outs = refs[: homes * len(sizes)]
    sbuf, xbuf, deep, obuf, ssem, xsem, osem = refs[homes * len(sizes) :]
    width = sbuf.shape[1]
    slots = sum(sizes)
    begin = ends[part - 1] if part else 0
    end = ends[part]
    none_begin = empties[part - 1] if part else 0
    none_end = empties[part]

    def put(slot):
        group = slot // slots
        inside = slot - group * slots
        first = 0
        for piece, size in enumerate(sizes):
            @pl.when((inside >= first) & (inside < first + size))
            def _(piece=piece, first=first):
                for other in range(homes):
                    @pl.when(group == other)
                    def _(out=outs[piece * homes + other]):
                        pltpu.make_async_copy(obuf.at[slot], out.at[inside - first], osem.at[slot]).start()

            first += size

    def settle(slot):
        pltpu.make_async_copy(obuf.at[slot], outs[0].at[0], osem.at[slot]).wait()

    def fetch(item, act):
        buf = lax.rem(item, BUFS)
        at = item * FIELDS
        top = pl.multiple_of(todo[at] * width, width)
        left = pl.multiple_of(todo[at + 1] * width, width)
        act(pltpu.make_async_copy(sigma.at[pl.ds(top, width), pl.ds(left, width)], sbuf.at[buf], ssem.at[buf]))

        @pl.when(todo[at + 7] == 1)
        def _():
            node, q = todo[at + 2], todo[at + 3]
            xslot = lax.rem(todo[at + 8], BUFS)
            source = panel.at[:, node // nodes, lax.rem(node, nodes), q]
            act(pltpu.make_async_copy(source, xbuf.at[xslot], xsem.at[xslot]))

    for ahead in range(BUFS - 2):
        @pl.when(begin + ahead < end)
        def _():
            fetch(begin + ahead, lambda copy: copy.start())

    def blank(item, carry):
        slot = empty[item]
        obuf[slot] = jnp.zeros(obuf.shape[1:], jnp.float32)
        put(slot)
        return carry

    lax.fori_loop(none_begin, none_end, blank, 0)

    def step(item, carry):
        @pl.when(item + BUFS - 2 < end)
        def _():
            fetch(item + BUFS - 2, lambda copy: copy.start())

        fetch(item, lambda copy: copy.wait())
        at = item * FIELDS
        slot = todo[at + 4]

        @pl.when(todo[at + 7] == 1)
        def _():
            high, low = split(xbuf[lax.rem(todo[at + 8], BUFS)].reshape(width, width))
            deep[:width] = high
            deep[width : 2 * width] = low
            deep[2 * width :] = high

        high, low = split(sbuf[lax.rem(item, BUFS)])
        term = jnp.dot(
            jnp.concatenate([high, high, low], axis=1), deep[...], preferred_element_type=jnp.float32
        )
        obuf[slot] = term + jnp.where(todo[at + 5] == 1, 0.0, obuf[slot])

        @pl.when(todo[at + 6] == 1)
        def _():
            put(slot)

        return carry

    lax.fori_loop(begin, end, step, 0)

    def drain(item, carry):
        @pl.when(todo[item * FIELDS + 6] == 1)
        def _():
            settle(todo[item * FIELDS + 4])

        return carry

    lax.fori_loop(begin, end, drain, 0)

    def drain_blank(item, carry):
        settle(empty[item])
        return carry

    lax.fori_loop(none_begin, none_end, drain_blank, 0)


def local_product(plan, sigma, panel, homes, part, sizes):
    rows, _, nodes, _, strip, width = panel.shape
    total = homes * sum(sizes)
    hbm = pl.BlockSpec(memory_space=pl.ANY)
    smem = pl.BlockSpec(memory_space=pltpu.SMEM)
    return pl.pallas_call(
        functools.partial(product_kernel, part, sizes, nodes, homes),
        out_shape=[jax.ShapeDtypeStruct((size, width, width), jnp.float32) for size in sizes for _ in range(homes)],
        in_specs=[smem] * 4 + [hbm, hbm],
        out_specs=[hbm] * (homes * len(sizes)),
        scratch_shapes=[
            pltpu.VMEM((BUFS, width, width), jnp.float32),
            pltpu.VMEM((BUFS, rows, strip, width), jnp.float32),
            pltpu.VMEM((3 * width, width), jnp.bfloat16),
            pltpu.VMEM((total, width, width), jnp.float32),
            pltpu.SemaphoreType.DMA((BUFS,)),
            pltpu.SemaphoreType.DMA((BUFS,)),
            pltpu.SemaphoreType.DMA((total,)),
        ],
        compiler_params=pltpu.CompilerParams(vmem_limit_bytes=50 * MIB),
        cost_estimate=pl.CostEstimate(flops=width, bytes_accessed=width, transcendentals=0),
    )(*plan, sigma, panel)


def corner_kernel(base, sizes, own_rows, spot, own_struct, panel, *refs):
    totals, refs = refs[: len(sizes)], refs[len(sizes) :]
    if base:
        before, whole, own, out, gram, xbuf, xsem = refs
    else:
        gram, xbuf, xsem = refs
    nodes, entries = own_struct.shape
    width = gram.shape[1]
    my_row, my_col = spot[0], spot[1]
    slots = sum(sizes)

    def walk(act):
        def per_pair(pair, rank):
            node, p = pair // entries, lax.rem(pair, entries)
            mine = own_struct[node, p] // own_rows == my_row
            slot = rank - base

            @pl.when(mine & (slot >= 0) & (slot < slots))
            def _():
                act(node, slot, pltpu.make_async_copy(panel.at[:, my_col, node, p], xbuf.at[slot], xsem.at[slot]))

            return rank + mine.astype(jnp.int32)

        lax.fori_loop(0, nodes * entries, per_pair, jnp.int32(0))

    walk(lambda node, slot, copy: copy.start())
    gram[...] = before[...] if base else jnp.zeros(gram.shape, jnp.float32)

    def gather(node, slot, copy):
        copy.wait()
        left = xbuf[slot].reshape(width, width).T
        first = 0
        for total, size in zip(totals, sizes):
            @pl.when((slot >= first) & (slot < first + size))
            def _(total=total, first=first):
                gram[node] += triple_dot(left, total[slot - first])

            first += size

    walk(gather)
    if base:
        for node in range(nodes):
            inverse, mine = whole[node], own[node]
            out[node] = triple_dot(inverse.T, triple_dot(gram[node], inverse)) + triple_dot(mine.T, mine)


def corner(spot, own_struct, panel, totals, base, sizes, own_rows, *ending):
    rows, _, nodes, _, strip, width = panel.shape
    vmem = pl.BlockSpec(memory_space=pltpu.VMEM)
    smem = pl.BlockSpec(memory_space=pltpu.SMEM)
    blocks = (nodes, width, width)
    return pl.pallas_call(
        functools.partial(corner_kernel, base, sizes, own_rows),
        out_shape=jax.ShapeDtypeStruct(blocks, jnp.float32),
        in_specs=[smem, smem, pl.BlockSpec(memory_space=pl.ANY)] + [vmem] * (len(totals) + len(ending)),
        out_specs=vmem,
        scratch_shapes=([pltpu.VMEM(blocks, jnp.float32)] if base else [])
        + [
            pltpu.VMEM((sum(sizes), rows, strip, width), jnp.float32),
            pltpu.SemaphoreType.DMA((sum(sizes),)),
        ],
        compiler_params=pltpu.CompilerParams(vmem_limit_bytes=50 * MIB),
        cost_estimate=pl.CostEstimate(flops=6 * 8 * width**3, bytes_accessed=8 * MIB, transcendentals=0),
    )(spot, own_struct, panel, *totals, *ending)


def finish_kernel(sizes, shape, holder, rank, whole, *refs):
    nodes, entries, strip, width = shape
    arrived, (off, raw) = refs[: len(sizes)], refs[len(sizes) :]
    for node in range(nodes):
        def pick(entry, carry):
            at = node * entries + entry
            first = 0
            for blocks, size in zip(arrived, sizes):
                slot = rank[at] - first

                @pl.when((slot >= 0) & (slot < size))
                def _(blocks=blocks, size=size, slot=slot):
                    raw[pl.ds(pl.multiple_of(entry * strip, strip), strip), :] = blocks[holder[at] * size + slot]

                first += size
            return carry

        lax.fori_loop(0, entries, pick, 0)
        off[node] = -triple_dot(raw[...], whole[node]).reshape(entries, strip, width)


def finish(holder, rank, shape, whole, arrived, sizes):
    nodes, entries, strip, width = shape
    vmem = pl.BlockSpec(memory_space=pltpu.VMEM)
    smem = pl.BlockSpec(memory_space=pltpu.SMEM)
    return pl.pallas_call(
        functools.partial(finish_kernel, sizes, shape),
        out_shape=jax.ShapeDtypeStruct(shape, jnp.float32),
        in_specs=[smem] * 2 + [vmem] * (1 + len(arrived)),
        out_specs=vmem,
        scratch_shapes=[pltpu.VMEM((entries * strip, width), jnp.float32)],
        compiler_params=pltpu.CompilerParams(vmem_limit_bytes=50 * MIB),
        cost_estimate=pl.CostEstimate(flops=6 * nodes * entries * strip * width**2, bytes_accessed=8 * MIB, transcendentals=0),
    )(holder, rank, whole, *arrived)


def per_device(rows, homes, sigma_anc, panel, diag_inv, structure):
    nodes, entries, strip, width = panel.shape
    own_rows, own_cols = sigma_anc.shape[0] // width, sigma_anc.shape[1] // width
    chips = homes // 2

    struct = lax.all_gather(structure, "col", axis=0, tiled=True)
    every_panel = lax.all_gather(panel, ("row", "col"), axis=0, tiled=False)
    every_panel = every_panel.reshape((rows, homes) + panel.shape)

    most = nodes * min(entries, own_rows)
    levels = sorted({min(slots, most) for slots in SLOTS + (most,)})
    holders = struct.reshape(homes, -1) // own_rows
    loads = jnp.sum(holders[:, :, None] == jnp.arange(rows, dtype=jnp.int32), axis=1)
    heaviest = jnp.max(loads)
    level = sum((heaviest > slots).astype(jnp.int32) for slots in levels[:-1])

    def pieces_of(slots):
        return slots // 2, slots - slots // 2

    my_row = lax.axis_index("row").astype(jnp.int32)
    my_col = lax.axis_index("col").astype(jnp.int32)
    chosen = jnp.asarray([pieces_of(slots) for slots in levels], jnp.int32)[level]
    spot = jnp.concatenate([jnp.stack([my_row, my_col]), chosen])
    plan = make_plan(spot, struct, most, nodes, own_rows, own_cols)

    holder = structure.reshape(-1) // own_rows
    pair = jnp.arange(nodes * entries, dtype=jnp.int32)
    earlier = (holder[:, None] == holder[None, :]) & (pair[None, :] < pair[:, None])
    rank = jnp.sum(earlier.astype(jnp.int32), axis=1)

    sibling = [(col, col ^ 1) for col in range(homes)]

    def to_rows(total):
        strips = total.reshape(-1, rows, strip, width).transpose(1, 0, 2, 3)
        landed = lax.all_to_all(strips, "row", split_axis=0, concat_axis=0, tiled=True)
        return landed.reshape(-1, strip, width)

    def between_cores(blocks):
        return [
            blocks[2 * away] + lax.ppermute(blocks[2 * away + 1], "col", sibling) for away in range(1, chips)
        ]

    def at_home(blocks):
        return blocks[0] + lax.ppermute(blocks[1], "col", sibling)

    def between_chips(sums):
        return [
            lax.ppermute(value, "col", [(col, (col + 2 * away) % homes) for col in range(homes)])
            for away, value in enumerate(sums, 1)
        ]

    def add(first, others):
        return functools.reduce(lambda left, right: left + right, others, first)

    def with_slots(slots, sigma_anc, every_panel, diag_inv, structure, spot, holder, rank, *plan):
        sizes = pieces_of(slots)
        inverse = lax.all_gather(diag_inv, "row", axis=1, tiled=True)

        early = local_product(plan, sigma_anc, every_panel, homes, 0, sizes[:1])
        sums = between_cores(early)
        sums, todo = lax.optimization_barrier((sums, plan[0]))
        crossed = between_chips(sums)
        late = local_product((todo,) + plan[1:], sigma_anc, every_panel, homes, 1, sizes[1:])
        late, crossed, inverse = lax.optimization_barrier((late, crossed, inverse))

        sums = between_cores(late)
        second = add(at_home(late), between_chips(sums))
        first = add(at_home(early), crossed)
        gram = corner(spot, structure, every_panel, (first,), 0, sizes[:1], own_rows)
        first, gram, _ = lax.optimization_barrier((first, gram, sums))
        landed = to_rows(first)
        second, gram = lax.optimization_barrier((second, gram))

        part = corner(spot, structure, every_panel, (second,), sizes[0], sizes[1:], own_rows, gram, inverse, diag_inv)
        off = finish(holder, rank, panel.shape, inverse, (landed, to_rows(second)), sizes)
        return off, lax.psum_scatter(part, "row", scatter_dimension=1, tiled=True)

    order = sorted(levels, key=lambda slots: abs(slots - USUAL))
    branches = [functools.partial(with_slots, slots) for slots in order]
    operands = (sigma_anc, every_panel, diag_inv, structure, spot, holder, rank) + tuple(plan)
    if len(branches) == 1:
        return branches[0](*operands)
    branch = jnp.asarray([order.index(slots) for slots in levels], jnp.int32)[level]
    return lax.switch(branch, branches, *operands)


def solution(mesh):
    placed = (
        P(("grp", "row"), "col"),
        P(("grp", "col"), None, "row", None),
        P(("grp", "col"), "row", None),
        P("col", None),
    )
    return jax.shard_map(
        functools.partial(per_device, mesh.shape["row"], mesh.shape["col"]),
        mesh=mesh,
        in_specs=placed,
        out_specs=(P(("grp", "col"), None, "row", None), P(("grp", "col"), "row", None)),
        check_vma=False,
    )
```

```python
import functools

import jax
import jax.numpy as jnp
from jax import lax
from jax.experimental import pallas as pl
from jax.experimental.pallas import tpu as pltpu
from jax.sharding import PartitionSpec as P

SLOTS = (9, 10, 11, 12, 13, 15)
USUAL = 10.4
BUFS = 12
FIELDS = 9
MIB = 1024 * 1024


def split(value):
    high = value.astype(jnp.bfloat16)
    return high, (value - high.astype(jnp.float32)).astype(jnp.bfloat16)


def triple_dot(left, right):
    left_high, left_low = split(left)
    right_high, right_low = split(right)
    dot = functools.partial(jnp.dot, preferred_element_type=jnp.float32)
    return dot(left_high, right_high) + (dot(left_high, right_low) + dot(left_low, right_high))


def plan_kernel(nodes, own_rows, own_cols, spot, struct, todo, ends, empty, empties):
    entries = struct.shape[1]
    homes = struct.shape[0] // nodes
    chips = homes // 2
    my_row, my_col = spot[0], spot[1]

    def piece_list(first, size, state):
        def per_home(home, state):
            distance = lax.rem(home // 2 - my_col // 2 + chips, chips)
            group = distance * 2 + lax.rem(home + my_col, 2)

            def per_node(member, state):
                rank, count, blocks, none = state
                node = home * nodes + member
                low = high = rank
                for p in range(entries):
                    mine = (struct[node, p] // own_rows == my_row).astype(jnp.int32)
                    high += mine
                held = high - low
                start = jnp.maximum(low, first)
                stop = jnp.minimum(high, first + size)
                columns = jnp.int32(0)
                for q in range(entries):
                    columns += (struct[node, q] // own_cols == my_col).astype(jnp.int32)

                def enlist():
                    def per_column(q, state):
                        order, count, blocks = state
                        other = struct[node, q]

                        def per_row(p, state):
                            at_rank, count = state
                            block = struct[node, p]
                            mine = block // own_rows == my_row

                            @pl.when(mine & (at_rank >= start) & (at_rank < stop))
                            def _():
                                at = count * FIELDS
                                todo[at] = block - my_row * own_rows
                                todo[at + 1] = other - my_col * own_cols
                                todo[at + 2] = node
                                todo[at + 3] = q
                                todo[at + 4] = group * size + at_rank - first
                                todo[at + 5] = (order == 0).astype(jnp.int32)
                                todo[at + 6] = (order == columns - 1).astype(jnp.int32)
                                todo[at + 7] = (at_rank == start).astype(jnp.int32)
                                todo[at + 8] = blocks

                            taken = mine & (at_rank >= start) & (at_rank < stop)
                            return at_rank + mine.astype(jnp.int32), count + taken.astype(jnp.int32)

                        def column():
                            return lax.fori_loop(0, entries, per_row, (low, count))[1]

                        hit = other // own_cols == my_col
                        count = lax.cond(hit, column, lambda: count)
                        step = hit.astype(jnp.int32)
                        return order + step, count, blocks + step

                    def all_empty():
                        def one(at_rank, none):
                            empty[none] = group * size + at_rank - first
                            return none + 1

                        return lax.fori_loop(start, stop, one, none)

                    _, more, further = lax.fori_loop(0, entries, per_column, (jnp.int32(0), count, blocks))
                    return more, further, lax.cond(columns == 0, all_empty, lambda: none)

                count, blocks, none = lax.cond(start < stop, enlist, lambda: (count, blocks, none))
                return high, count, blocks, none

            return lax.fori_loop(0, nodes, per_node, (jnp.int32(0),) + state)[1:]

        return lax.fori_loop(0, homes, per_home, state)

    count = none = jnp.int32(0)
    for piece, (first, size) in enumerate(((0, spot[2]), (spot[2], spot[3]))):
        count, _, none = piece_list(first, size, (count, jnp.int32(0), none))
        ends[piece] = count
        empties[piece] = none


def make_plan(spot, struct, most, nodes, own_rows, own_cols):
    total = struct.shape[0] // nodes * most
    smem = pl.BlockSpec(memory_space=pltpu.SMEM)
    lengths = (total * struct.shape[1] * FIELDS, 2, total, 2)
    return pl.pallas_call(
        functools.partial(plan_kernel, nodes, own_rows, own_cols),
        out_shape=[jax.ShapeDtypeStruct((length,), jnp.int32) for length in lengths],
        in_specs=[smem, smem],
        out_specs=[smem] * 4,
    )(spot, struct)


def product_kernel(part, sizes, nodes, homes, todo, ends, empty, empties, sigma, panel, *refs):
    outs = refs[: homes * len(sizes)]
    sbuf, xbuf, deep, obuf, ssem, xsem, osem = refs[homes * len(sizes) :]
    width = sbuf.shape[1]
    slots = sum(sizes)
    begin = ends[part - 1] if part else 0
    end = ends[part]
    none_begin = empties[part - 1] if part else 0
    none_end = empties[part]

    def put(slot):
        group = slot // slots
        inside = slot - group * slots
        first = 0
        for piece, size in enumerate(sizes):
            @pl.when((inside >= first) & (inside < first + size))
            def _(piece=piece, first=first):
                for other in range(homes):
                    @pl.when(group == other)
                    def _(out=outs[piece * homes + other]):
                        pltpu.make_async_copy(obuf.at[slot], out.at[inside - first], osem.at[slot]).start()

            first += size

    def settle(slot):
        pltpu.make_async_copy(obuf.at[slot], outs[0].at[0], osem.at[slot]).wait()

    def fetch(item, act):
        buf = lax.rem(item, BUFS)
        at = item * FIELDS
        top = pl.multiple_of(todo[at] * width, width)
        left = pl.multiple_of(todo[at + 1] * width, width)
        act(pltpu.make_async_copy(sigma.at[pl.ds(top, width), pl.ds(left, width)], sbuf.at[buf], ssem.at[buf]))

        @pl.when(todo[at + 7] == 1)
        def _():
            node, q = todo[at + 2], todo[at + 3]
            xslot = lax.rem(todo[at + 8], BUFS)
            source = panel.at[:, node // nodes, lax.rem(node, nodes), q]
            act(pltpu.make_async_copy(source, xbuf.at[xslot], xsem.at[xslot]))

    for ahead in range(BUFS - 2):
        @pl.when(begin + ahead < end)
        def _():
            fetch(begin + ahead, lambda copy: copy.start())

    def blank(item, carry):
        slot = empty[item]
        obuf[slot] = jnp.zeros(obuf.shape[1:], jnp.float32)
        put(slot)
        return carry

    lax.fori_loop(none_begin, none_end, blank, 0)

    def step(item, carry):
        @pl.when(item + BUFS - 2 < end)
        def _():
            fetch(item + BUFS - 2, lambda copy: copy.start())

        fetch(item, lambda copy: copy.wait())
        at = item * FIELDS
        slot = todo[at + 4]

        @pl.when(todo[at + 7] == 1)
        def _():
            high, low = split(xbuf[lax.rem(todo[at + 8], BUFS)].reshape(width, width))
            deep[:width] = high
            deep[width : 2 * width] = low
            deep[2 * width :] = high

        high, low = split(sbuf[lax.rem(item, BUFS)])
        term = jnp.dot(
            jnp.concatenate([high, high, low], axis=1), deep[...], preferred_element_type=jnp.float32
        )
        obuf[slot] = term + jnp.where(todo[at + 5] == 1, 0.0, obuf[slot])

        @pl.when(todo[at + 6] == 1)
        def _():
            put(slot)

        return carry

    lax.fori_loop(begin, end, step, 0)

    def drain(item, carry):
        @pl.when(todo[item * FIELDS + 6] == 1)
        def _():
            settle(todo[item * FIELDS + 4])

        return carry

    lax.fori_loop(begin, end, drain, 0)

    def drain_blank(item, carry):
        settle(empty[item])
        return carry

    lax.fori_loop(none_begin, none_end, drain_blank, 0)


def local_product(plan, sigma, panel, homes, part, sizes):
    rows, _, nodes, _, strip, width = panel.shape
    total = homes * sum(sizes)
    hbm = pl.BlockSpec(memory_space=pl.ANY)
    smem = pl.BlockSpec(memory_space=pltpu.SMEM)
    return pl.pallas_call(
        functools.partial(product_kernel, part, sizes, nodes, homes),
        out_shape=[jax.ShapeDtypeStruct((size, width, width), jnp.float32) for size in sizes for _ in range(homes)],
        in_specs=[smem] * 4 + [hbm, hbm],
        out_specs=[hbm] * (homes * len(sizes)),
        scratch_shapes=[
            pltpu.VMEM((BUFS, width, width), jnp.float32),
            pltpu.VMEM((BUFS, rows, strip, width), jnp.float32),
            pltpu.VMEM((3 * width, width), jnp.bfloat16),
            pltpu.VMEM((total, width, width), jnp.float32),
            pltpu.SemaphoreType.DMA((BUFS,)),
            pltpu.SemaphoreType.DMA((BUFS,)),
            pltpu.SemaphoreType.DMA((total,)),
        ],
        compiler_params=pltpu.CompilerParams(vmem_limit_bytes=50 * MIB),
        cost_estimate=pl.CostEstimate(flops=width, bytes_accessed=width, transcendentals=0),
    )(*plan, sigma, panel)


def corner_kernel(base, sizes, own_rows, spot, own_struct, panel, *refs):
    totals, refs = refs[: len(sizes)], refs[len(sizes) :]
    if base:
        before, whole, own, out, gram, xbuf, xsem = refs
    else:
        gram, xbuf, xsem = refs
    nodes, entries = own_struct.shape
    width = gram.shape[1]
    my_row, my_col = spot[0], spot[1]
    slots = sum(sizes)

    def walk(act):
        def per_pair(pair, rank):
            node, p = pair // entries, lax.rem(pair, entries)
            mine = own_struct[node, p] // own_rows == my_row
            slot = rank - base

            @pl.when(mine & (slot >= 0) & (slot < slots))
            def _():
                act(node, slot, pltpu.make_async_copy(panel.at[:, my_col, node, p], xbuf.at[slot], xsem.at[slot]))

            return rank + mine.astype(jnp.int32)

        lax.fori_loop(0, nodes * entries, per_pair, jnp.int32(0))

    walk(lambda node, slot, copy: copy.start())
    gram[...] = before[...] if base else jnp.zeros(gram.shape, jnp.float32)

    def gather(node, slot, copy):
        copy.wait()
        left = xbuf[slot].reshape(width, width).T
        first = 0
        for total, size in zip(totals, sizes):
            @pl.when((slot >= first) & (slot < first + size))
            def _(total=total, first=first):
                gram[node] += triple_dot(left, total[slot - first])

            first += size

    walk(gather)
    if base:
        for node in range(nodes):
            inverse, mine = whole[node], own[node]
            out[node] = triple_dot(inverse.T, triple_dot(gram[node], inverse)) + triple_dot(mine.T, mine)


def corner(spot, own_struct, panel, totals, base, sizes, own_rows, *ending):
    rows, _, nodes, _, strip, width = panel.shape
    vmem = pl.BlockSpec(memory_space=pltpu.VMEM)
    smem = pl.BlockSpec(memory_space=pltpu.SMEM)
    blocks = (nodes, width, width)
    return pl.pallas_call(
        functools.partial(corner_kernel, base, sizes, own_rows),
        out_shape=jax.ShapeDtypeStruct(blocks, jnp.float32),
        in_specs=[smem, smem, pl.BlockSpec(memory_space=pl.ANY)] + [vmem] * (len(totals) + len(ending)),
        out_specs=vmem,
        scratch_shapes=([pltpu.VMEM(blocks, jnp.float32)] if base else [])
        + [
            pltpu.VMEM((sum(sizes), rows, strip, width), jnp.float32),
            pltpu.SemaphoreType.DMA((sum(sizes),)),
        ],
        compiler_params=pltpu.CompilerParams(vmem_limit_bytes=50 * MIB),
        cost_estimate=pl.CostEstimate(flops=6 * 8 * width**3, bytes_accessed=8 * MIB, transcendentals=0),
    )(spot, own_struct, panel, *totals, *ending)


def finish_kernel(sizes, shape, holder, rank, whole, *refs):
    nodes, entries, strip, width = shape
    arrived, (off, raw) = refs[: len(sizes)], refs[len(sizes) :]
    for node in range(nodes):
        def pick(entry, carry):
            at = node * entries + entry
            first = 0
            for blocks, size in zip(arrived, sizes):
                slot = rank[at] - first

                @pl.when((slot >= 0) & (slot < size))
                def _(blocks=blocks, size=size, slot=slot):
                    raw[pl.ds(pl.multiple_of(entry * strip, strip), strip), :] = blocks[holder[at] * size + slot]

                first += size
            return carry

        lax.fori_loop(0, entries, pick, 0)
        off[node] = -triple_dot(raw[...], whole[node]).reshape(entries, strip, width)


def finish(holder, rank, shape, whole, arrived, sizes):
    nodes, entries, strip, width = shape
    vmem = pl.BlockSpec(memory_space=pltpu.VMEM)
    smem = pl.BlockSpec(memory_space=pltpu.SMEM)
    return pl.pallas_call(
        functools.partial(finish_kernel, sizes, shape),
        out_shape=jax.ShapeDtypeStruct(shape, jnp.float32),
        in_specs=[smem] * 2 + [vmem] * (1 + len(arrived)),
        out_specs=vmem,
        scratch_shapes=[pltpu.VMEM((entries * strip, width), jnp.float32)],
        compiler_params=pltpu.CompilerParams(vmem_limit_bytes=50 * MIB),
        cost_estimate=pl.CostEstimate(flops=6 * nodes * entries * strip * width**2, bytes_accessed=8 * MIB, transcendentals=0),
    )(holder, rank, whole, *arrived)


def per_device(rows, homes, sigma_anc, panel, diag_inv, structure):
    nodes, entries, strip, width = panel.shape
    own_rows, own_cols = sigma_anc.shape[0] // width, sigma_anc.shape[1] // width
    chips = homes // 2

    struct = lax.all_gather(structure, "col", axis=0, tiled=True)
    every_panel = lax.all_gather(panel, ("row", "col"), axis=0, tiled=False)
    every_panel = every_panel.reshape((rows, homes) + panel.shape)

    most = nodes * min(entries, own_rows)
    levels = sorted({min(slots, most) for slots in SLOTS + (most,)})
    holders = struct.reshape(homes, -1) // own_rows
    loads = jnp.sum(holders[:, :, None] == jnp.arange(rows, dtype=jnp.int32), axis=1)
    heaviest = jnp.max(loads)
    level = sum((heaviest > slots).astype(jnp.int32) for slots in levels[:-1])

    def pieces_of(slots):
        first = max(1, slots * 2 // 5)
        last = (slots - first) // 2
        return first, slots - first - last, last

    my_row = lax.axis_index("row").astype(jnp.int32)
    my_col = lax.axis_index("col").astype(jnp.int32)
    halves = [(pieces_of(slots)[0], slots - pieces_of(slots)[0]) for slots in levels]
    chosen = jnp.asarray(halves, jnp.int32)[level]
    spot = jnp.concatenate([jnp.stack([my_row, my_col]), chosen])
    plan = make_plan(spot, struct, most, nodes, own_rows, own_cols)

    holder = structure.reshape(-1) // own_rows
    pair = jnp.arange(nodes * entries, dtype=jnp.int32)
    earlier = (holder[:, None] == holder[None, :]) & (pair[None, :] < pair[:, None])
    rank = jnp.sum(earlier.astype(jnp.int32), axis=1)

    sibling = [(col, col ^ 1) for col in range(homes)]

    def to_rows(total):
        strips = total.reshape(-1, rows, strip, width).transpose(1, 0, 2, 3)
        landed = lax.all_to_all(strips, "row", split_axis=0, concat_axis=0, tiled=True)
        return landed.reshape(-1, strip, width)

    def between_cores(blocks):
        return [
            blocks[2 * away] + lax.ppermute(blocks[2 * away + 1], "col", sibling) for away in range(1, chips)
        ]

    def at_home(blocks):
        return blocks[0] + lax.ppermute(blocks[1], "col", sibling)

    def between_chips(sums):
        return [
            lax.ppermute(value, "col", [(col, (col + 2 * away) % homes) for col in range(homes)])
            for away, value in enumerate(sums, 1)
        ]

    def add(first, others):
        return functools.reduce(lambda left, right: left + right, others, first)

    def with_slots(slots, sigma_anc, every_panel, diag_inv, structure, spot, holder, rank, *plan):
        sizes = pieces_of(slots)
        inverse = lax.all_gather(diag_inv, "row", axis=1, tiled=True)

        early = local_product(plan, sigma_anc, every_panel, homes, 0, sizes[:1])
        sums = between_cores(early)
        sums, todo = lax.optimization_barrier((sums, plan[0]))
        crossed = between_chips(sums)
        late = local_product((todo,) + plan[1:], sigma_anc, every_panel, homes, 1, sizes[1:])
        late, crossed, inverse = lax.optimization_barrier((late, crossed, inverse))

        sums = between_cores(late[:homes])
        first = add(at_home(early), crossed)
        first, _ = lax.optimization_barrier((first, sums))
        crossed = between_chips(sums)
        second = add(at_home(late[:homes]), crossed)
        sums = between_cores(late[homes:])
        sums, crossed = lax.optimization_barrier((sums, crossed))
        third = add(at_home(late[homes:]), between_chips(sums))

        arrived = [to_rows(first), to_rows(second)]
        gram = corner(spot, structure, every_panel, (first, second), 0, sizes[:2], own_rows)
        third, gram = lax.optimization_barrier((third, gram))
        arrived.append(to_rows(third))
        part = corner(
            spot, structure, every_panel, (third,), sum(sizes[:2]), sizes[2:], own_rows, gram, inverse, diag_inv
        )
        off = finish(holder, rank, panel.shape, inverse, arrived, sizes)
        return off, lax.psum_scatter(part, "row", scatter_dimension=1, tiled=True)

    order = sorted(levels, key=lambda slots: abs(slots - USUAL))
    branches = [functools.partial(with_slots, slots) for slots in order]
    operands = (sigma_anc, every_panel, diag_inv, structure, spot, holder, rank) + tuple(plan)
    if len(branches) == 1:
        return branches[0](*operands)
    branch = jnp.asarray([order.index(slots) for slots in levels], jnp.int32)[level]
    return lax.switch(branch, branches, *operands)


def solution(mesh):
    placed = (
        P(("grp", "row"), "col"),
        P(("grp", "col"), None, "row", None),
        P(("grp", "col"), "row", None),
        P("col", None),
    )
    return jax.shard_map(
        functools.partial(per_device, mesh.shape["row"], mesh.shape["col"]),
        mesh=mesh,
        in_specs=placed,
        out_specs=(P(("grp", "col"), None, "row", None), P(("grp", "col"), "row", None)),
        check_vma=False,
    )
```

```python
import functools

import jax
import jax.numpy as jnp
from jax import lax
from jax.experimental import pallas as pl
from jax.experimental.pallas import tpu as pltpu
from jax.sharding import PartitionSpec as P

SLOTS = (10, 11, 12, 13, 15)
FIRST = 3
USUAL = 10.4
BUFS = 12
FIELDS = 9
MIB = 1024 * 1024


def split(value):
    high = value.astype(jnp.bfloat16)
    return high, (value - high.astype(jnp.float32)).astype(jnp.bfloat16)


def triple_dot(left, right):
    left_high, left_low = split(left)
    right_high, right_low = split(right)
    dot = functools.partial(jnp.dot, preferred_element_type=jnp.float32)
    return dot(left_high, right_high) + (dot(left_high, right_low) + dot(left_low, right_high))


def plan_kernel(nodes, own_rows, own_cols, spot, struct, todo, ends, empty, empties):
    entries = struct.shape[1]
    homes = struct.shape[0] // nodes
    chips = homes // 2
    my_row, my_col = spot[0], spot[1]

    def piece_list(first, size, state):
        def per_home(home, state):
            distance = lax.rem(home // 2 - my_col // 2 + chips, chips)
            group = distance * 2 + lax.rem(home + my_col, 2)

            def per_node(member, state):
                rank, count, blocks, none = state
                node = home * nodes + member
                low = high = rank
                for p in range(entries):
                    mine = (struct[node, p] // own_rows == my_row).astype(jnp.int32)
                    high += mine
                held = high - low
                start = jnp.maximum(low, first)
                stop = jnp.minimum(high, first + size)
                columns = jnp.int32(0)
                for q in range(entries):
                    columns += (struct[node, q] // own_cols == my_col).astype(jnp.int32)

                def enlist():
                    def per_column(q, state):
                        order, count, blocks = state
                        other = struct[node, q]

                        def per_row(p, state):
                            at_rank, count = state
                            block = struct[node, p]
                            mine = block // own_rows == my_row

                            @pl.when(mine & (at_rank >= start) & (at_rank < stop))
                            def _():
                                at = count * FIELDS
                                todo[at] = block - my_row * own_rows
                                todo[at + 1] = other - my_col * own_cols
                                todo[at + 2] = node
                                todo[at + 3] = q
                                todo[at + 4] = group * size + at_rank - first
                                todo[at + 5] = (order == 0).astype(jnp.int32)
                                todo[at + 6] = (order == columns - 1).astype(jnp.int32)
                                todo[at + 7] = (at_rank == start).astype(jnp.int32)
                                todo[at + 8] = blocks

                            taken = mine & (at_rank >= start) & (at_rank < stop)
                            return at_rank + mine.astype(jnp.int32), count + taken.astype(jnp.int32)

                        def column():
                            return lax.fori_loop(0, entries, per_row, (low, count))[1]

                        hit = other // own_cols == my_col
                        count = lax.cond(hit, column, lambda: count)
                        step = hit.astype(jnp.int32)
                        return order + step, count, blocks + step

                    def all_empty():
                        def one(at_rank, none):
                            empty[none] = group * size + at_rank - first
                            return none + 1

                        return lax.fori_loop(start, stop, one, none)

                    _, more, further = lax.fori_loop(0, entries, per_column, (jnp.int32(0), count, blocks))
                    return more, further, lax.cond(columns == 0, all_empty, lambda: none)

                count, blocks, none = lax.cond(start < stop, enlist, lambda: (count, blocks, none))
                return high, count, blocks, none

            return lax.fori_loop(0, nodes, per_node, (jnp.int32(0),) + state)[1:]

        return lax.fori_loop(0, homes, per_home, state)

    count = none = jnp.int32(0)
    for piece, (first, size) in enumerate(((0, spot[2]), (spot[2], spot[3]))):
        count, _, none = piece_list(first, size, (count, jnp.int32(0), none))
        ends[piece] = count
        empties[piece] = none


def make_plan(spot, struct, most, nodes, own_rows, own_cols):
    total = struct.shape[0] // nodes * most
    smem = pl.BlockSpec(memory_space=pltpu.SMEM)
    lengths = (total * struct.shape[1] * FIELDS, 2, total, 2)
    return pl.pallas_call(
        functools.partial(plan_kernel, nodes, own_rows, own_cols),
        out_shape=[jax.ShapeDtypeStruct((length,), jnp.int32) for length in lengths],
        in_specs=[smem, smem],
        out_specs=[smem] * 4,
    )(spot, struct)


def product_kernel(part, sizes, nodes, homes, todo, ends, empty, empties, sigma, panel, *refs):
    outs = refs[: homes * len(sizes)]
    sbuf, xbuf, deep, obuf, ssem, xsem, osem = refs[homes * len(sizes) :]
    width = sbuf.shape[1]
    slots = sum(sizes)
    begin = ends[part - 1] if part else 0
    end = ends[part]
    none_begin = empties[part - 1] if part else 0
    none_end = empties[part]

    def put(slot):
        group = slot // slots
        inside = slot - group * slots
        first = 0
        for piece, size in enumerate(sizes):
            @pl.when((inside >= first) & (inside < first + size))
            def _(piece=piece, first=first):
                for other in range(homes):
                    @pl.when(group == other)
                    def _(out=outs[piece * homes + other]):
                        pltpu.make_async_copy(obuf.at[slot], out.at[inside - first], osem.at[slot]).start()

            first += size

    def settle(slot):
        pltpu.make_async_copy(obuf.at[slot], outs[0].at[0], osem.at[slot]).wait()

    def fetch(item, act):
        buf = lax.rem(item, BUFS)
        at = item * FIELDS
        top = pl.multiple_of(todo[at] * width, width)
        left = pl.multiple_of(todo[at + 1] * width, width)
        act(pltpu.make_async_copy(sigma.at[pl.ds(top, width), pl.ds(left, width)], sbuf.at[buf], ssem.at[buf]))

        @pl.when(todo[at + 7] == 1)
        def _():
            node, q = todo[at + 2], todo[at + 3]
            xslot = lax.rem(todo[at + 8], BUFS)
            source = panel.at[:, node // nodes, lax.rem(node, nodes), q]
            act(pltpu.make_async_copy(source, xbuf.at[xslot], xsem.at[xslot]))

    for ahead in range(BUFS - 2):
        @pl.when(begin + ahead < end)
        def _():
            fetch(begin + ahead, lambda copy: copy.start())

    def blank(item, carry):
        slot = empty[item]
        obuf[slot] = jnp.zeros(obuf.shape[1:], jnp.float32)
        put(slot)
        return carry

    lax.fori_loop(none_begin, none_end, blank, 0)

    def step(item, carry):
        @pl.when(item + BUFS - 2 < end)
        def _():
            fetch(item + BUFS - 2, lambda copy: copy.start())

        fetch(item, lambda copy: copy.wait())
        at = item * FIELDS
        slot = todo[at + 4]

        @pl.when(todo[at + 7] == 1)
        def _():
            high, low = split(xbuf[lax.rem(todo[at + 8], BUFS)].reshape(width, width))
            deep[:width] = high
            deep[width : 2 * width] = low
            deep[2 * width :] = high

        high, low = split(sbuf[lax.rem(item, BUFS)])
        term = jnp.dot(
            jnp.concatenate([high, high, low], axis=1), deep[...], preferred_element_type=jnp.float32
        )
        obuf[slot] = term + jnp.where(todo[at + 5] == 1, 0.0, obuf[slot])

        @pl.when(todo[at + 6] == 1)
        def _():
            put(slot)

        return carry

    lax.fori_loop(begin, end, step, 0)

    def drain(item, carry):
        @pl.when(todo[item * FIELDS + 6] == 1)
        def _():
            settle(todo[item * FIELDS + 4])

        return carry

    lax.fori_loop(begin, end, drain, 0)

    def drain_blank(item, carry):
        settle(empty[item])
        return carry

    lax.fori_loop(none_begin, none_end, drain_blank, 0)


def local_product(plan, sigma, panel, homes, part, sizes):
    rows, _, nodes, _, strip, width = panel.shape
    total = homes * sum(sizes)
    hbm = pl.BlockSpec(memory_space=pl.ANY)
    smem = pl.BlockSpec(memory_space=pltpu.SMEM)
    return pl.pallas_call(
        functools.partial(product_kernel, part, sizes, nodes, homes),
        out_shape=[jax.ShapeDtypeStruct((size, width, width), jnp.float32) for size in sizes for _ in range(homes)],
        in_specs=[smem] * 4 + [hbm, hbm],
        out_specs=[hbm] * (homes * len(sizes)),
        scratch_shapes=[
            pltpu.VMEM((BUFS, width, width), jnp.float32),
            pltpu.VMEM((BUFS, rows, strip, width), jnp.float32),
            pltpu.VMEM((3 * width, width), jnp.bfloat16),
            pltpu.VMEM((total, width, width), jnp.float32),
            pltpu.SemaphoreType.DMA((BUFS,)),
            pltpu.SemaphoreType.DMA((BUFS,)),
            pltpu.SemaphoreType.DMA((total,)),
        ],
        compiler_params=pltpu.CompilerParams(vmem_limit_bytes=50 * MIB),
        cost_estimate=pl.CostEstimate(flops=width, bytes_accessed=width, transcendentals=0),
    )(*plan, sigma, panel)


def corner_kernel(base, sizes, own_rows, spot, own_struct, panel, *refs):
    totals, refs = refs[: len(sizes)], refs[len(sizes) :]
    if base:
        before, whole, own, out, gram, xbuf, xsem = refs
    else:
        gram, xbuf, xsem = refs
    nodes, entries = own_struct.shape
    width = gram.shape[1]
    my_row, my_col = spot[0], spot[1]
    slots = sum(sizes)

    def walk(act):
        def per_pair(pair, rank):
            node, p = pair // entries, lax.rem(pair, entries)
            mine = own_struct[node, p] // own_rows == my_row
            slot = rank - base

            @pl.when(mine & (slot >= 0) & (slot < slots))
            def _():
                act(node, slot, pltpu.make_async_copy(panel.at[:, my_col, node, p], xbuf.at[slot], xsem.at[slot]))

            return rank + mine.astype(jnp.int32)

        lax.fori_loop(0, nodes * entries, per_pair, jnp.int32(0))

    walk(lambda node, slot, copy: copy.start())
    gram[...] = before[...] if base else jnp.zeros(gram.shape, jnp.float32)

    def gather(node, slot, copy):
        copy.wait()
        left = xbuf[slot].reshape(width, width).T
        first = 0
        for total, size in zip(totals, sizes):
            @pl.when((slot >= first) & (slot < first + size))
            def _(total=total, first=first):
                gram[node] += triple_dot(left, total[slot - first])

            first += size

    walk(gather)
    if base:
        for node in range(nodes):
            inverse, mine = whole[node], own[node]
            out[node] = triple_dot(inverse.T, triple_dot(gram[node], inverse)) + triple_dot(mine.T, mine)


def corner(spot, own_struct, panel, totals, base, sizes, own_rows, *ending):
    rows, _, nodes, _, strip, width = panel.shape
    vmem = pl.BlockSpec(memory_space=pltpu.VMEM)
    smem = pl.BlockSpec(memory_space=pltpu.SMEM)
    blocks = (nodes, width, width)
    return pl.pallas_call(
        functools.partial(corner_kernel, base, sizes, own_rows),
        out_shape=jax.ShapeDtypeStruct(blocks, jnp.float32),
        in_specs=[smem, smem, pl.BlockSpec(memory_space=pl.ANY)] + [vmem] * (len(totals) + len(ending)),
        out_specs=vmem,
        scratch_shapes=([pltpu.VMEM(blocks, jnp.float32)] if base else [])
        + [
            pltpu.VMEM((sum(sizes), rows, strip, width), jnp.float32),
            pltpu.SemaphoreType.DMA((sum(sizes),)),
        ],
        compiler_params=pltpu.CompilerParams(vmem_limit_bytes=50 * MIB),
        cost_estimate=pl.CostEstimate(flops=6 * 8 * width**3, bytes_accessed=8 * MIB, transcendentals=0),
    )(spot, own_struct, panel, *totals, *ending)


def finish_kernel(sizes, shape, holder, rank, whole, *refs):
    nodes, entries, strip, width = shape
    arrived, (off, raw) = refs[: len(sizes)], refs[len(sizes) :]
    for node in range(nodes):
        def pick(entry, carry):
            at = node * entries + entry
            first = 0
            for blocks, size in zip(arrived, sizes):
                slot = rank[at] - first

                @pl.when((slot >= 0) & (slot < size))
                def _(blocks=blocks, size=size, slot=slot):
                    raw[pl.ds(pl.multiple_of(entry * strip, strip), strip), :] = blocks[holder[at] * size + slot]

                first += size
            return carry

        lax.fori_loop(0, entries, pick, 0)
        off[node] = -triple_dot(raw[...], whole[node]).reshape(entries, strip, width)


def finish(holder, rank, shape, whole, arrived, sizes):
    nodes, entries, strip, width = shape
    vmem = pl.BlockSpec(memory_space=pltpu.VMEM)
    smem = pl.BlockSpec(memory_space=pltpu.SMEM)
    return pl.pallas_call(
        functools.partial(finish_kernel, sizes, shape),
        out_shape=jax.ShapeDtypeStruct(shape, jnp.float32),
        in_specs=[smem] * 2 + [vmem] * (1 + len(arrived)),
        out_specs=vmem,
        scratch_shapes=[pltpu.VMEM((entries * strip, width), jnp.float32)],
        compiler_params=pltpu.CompilerParams(vmem_limit_bytes=50 * MIB),
        cost_estimate=pl.CostEstimate(flops=6 * nodes * entries * strip * width**2, bytes_accessed=8 * MIB, transcendentals=0),
    )(holder, rank, whole, *arrived)


def per_device(rows, homes, sigma_anc, panel, diag_inv, structure):
    nodes, entries, strip, width = panel.shape
    own_rows, own_cols = sigma_anc.shape[0] // width, sigma_anc.shape[1] // width
    chips = homes // 2

    struct = lax.all_gather(structure, "col", axis=0, tiled=True)
    every_panel = lax.all_gather(panel, ("row", "col"), axis=0, tiled=False)
    every_panel = every_panel.reshape((rows, homes) + panel.shape)

    most = nodes * min(entries, own_rows)
    levels = sorted({min(slots, most) for slots in SLOTS + (most,)})
    holders = struct.reshape(homes, -1) // own_rows
    loads = jnp.sum(holders[:, :, None] == jnp.arange(rows, dtype=jnp.int32), axis=1)
    heaviest = jnp.max(loads)
    level = sum((heaviest > slots).astype(jnp.int32) for slots in levels[:-1])

    def pieces_of(slots):
        first = max(1, min(FIRST, slots - 2))
        last = (slots - first) // 2
        return first, slots - first - last, last

    my_row = lax.axis_index("row").astype(jnp.int32)
    my_col = lax.axis_index("col").astype(jnp.int32)
    halves = [(pieces_of(slots)[0], slots - pieces_of(slots)[0]) for slots in levels]
    chosen = jnp.asarray(halves, jnp.int32)[level]
    spot = jnp.concatenate([jnp.stack([my_row, my_col]), chosen])
    plan = make_plan(spot, struct, most, nodes, own_rows, own_cols)

    holder = structure.reshape(-1) // own_rows
    pair = jnp.arange(nodes * entries, dtype=jnp.int32)
    earlier = (holder[:, None] == holder[None, :]) & (pair[None, :] < pair[:, None])
    rank = jnp.sum(earlier.astype(jnp.int32), axis=1)

    sibling = [(col, col ^ 1) for col in range(homes)]

    def to_rows(total):
        strips = total.reshape(-1, rows, strip, width).transpose(1, 0, 2, 3)
        landed = lax.all_to_all(strips, "row", split_axis=0, concat_axis=0, tiled=True)
        return landed.reshape(-1, strip, width)

    def between_cores(blocks):
        return [
            blocks[2 * away] + lax.ppermute(blocks[2 * away + 1], "col", sibling) for away in range(1, chips)
        ]

    def at_home(blocks):
        return blocks[0] + lax.ppermute(blocks[1], "col", sibling)

    def between_chips(sums):
        return [
            lax.ppermute(value, "col", [(col, (col + 2 * away) % homes) for col in range(homes)])
            for away, value in enumerate(sums, 1)
        ]

    def add(first, others):
        return functools.reduce(lambda left, right: left + right, others, first)

    def with_slots(slots, sigma_anc, every_panel, diag_inv, structure, spot, holder, rank, *plan):
        sizes = pieces_of(slots)
        inverse = lax.all_gather(diag_inv, "row", axis=1, tiled=True)

        early = local_product(plan, sigma_anc, every_panel, homes, 0, sizes[:1])
        sums = between_cores(early)
        sums, todo = lax.optimization_barrier((sums, plan[0]))
        crossed = between_chips(sums)
        late = local_product((todo,) + plan[1:], sigma_anc, every_panel, homes, 1, sizes[1:])
        late, crossed = lax.optimization_barrier((late, crossed))

        sums = between_cores(late[:homes])
        first = add(at_home(early), crossed)
        first, inverse, _ = lax.optimization_barrier((first, inverse, sums))
        crossed = between_chips(sums)
        second = add(at_home(late[:homes]), crossed)
        sums = between_cores(late[homes:])
        sums, crossed = lax.optimization_barrier((sums, crossed))
        third = add(at_home(late[homes:]), between_chips(sums))

        arrived = [to_rows(first), to_rows(second)]
        gram = corner(spot, structure, every_panel, (first, second), 0, sizes[:2], own_rows)
        third, gram = lax.optimization_barrier((third, gram))
        arrived.append(to_rows(third))
        part = corner(
            spot, structure, every_panel, (third,), sum(sizes[:2]), sizes[2:], own_rows, gram, inverse, diag_inv
        )
        off = finish(holder, rank, panel.shape, inverse, arrived, sizes)
        return off, lax.psum_scatter(part, "row", scatter_dimension=1, tiled=True)

    order = sorted(levels, key=lambda slots: abs(slots - USUAL))
    branches = [functools.partial(with_slots, slots) for slots in order]
    operands = (sigma_anc, every_panel, diag_inv, structure, spot, holder, rank) + tuple(plan)
    if len(branches) == 1:
        return branches[0](*operands)
    branch = jnp.asarray([order.index(slots) for slots in levels], jnp.int32)[level]
    return lax.switch(branch, branches, *operands)


def solution(mesh):
    placed = (
        P(("grp", "row"), "col"),
        P(("grp", "col"), None, "row", None),
        P(("grp", "col"), "row", None),
        P("col", None),
    )
    return jax.shard_map(
        functools.partial(per_device, mesh.shape["row"], mesh.shape["col"]),
        mesh=mesh,
        in_specs=placed,
        out_specs=(P(("grp", "col"), None, "row", None), P(("grp", "col"), "row", None)),
        check_vma=False,
    )
```

```python
import functools

import jax
import jax.numpy as jnp
from jax import lax
from jax.experimental import pallas as pl
from jax.experimental.pallas import tpu as pltpu
from jax.sharding import PartitionSpec as P

SLOTS = (10, 11, 12, 14)
FIRST, SECOND = 3, 4
USUAL = 10.4
BUFS = 12
FIELDS = 9
MIB = 1024 * 1024


def split(value):
    high = value.astype(jnp.bfloat16)
    return high, (value - high.astype(jnp.float32)).astype(jnp.bfloat16)


def triple_dot(left, right):
    left_high, left_low = split(left)
    right_high, right_low = split(right)
    dot = functools.partial(jnp.dot, preferred_element_type=jnp.float32)
    return dot(left_high, right_high) + (dot(left_high, right_low) + dot(left_low, right_high))


def plan_kernel(spans, nodes, own_rows, own_cols, spot, struct, todo, ends, empty, empties):
    entries = struct.shape[1]
    homes = struct.shape[0] // nodes
    chips = homes // 2
    my_row, my_col = spot[0], spot[1]

    def piece_list(first, size, state):
        def per_home(home, state):
            distance = lax.rem(home // 2 - my_col // 2 + chips, chips)
            group = distance * 2 + lax.rem(home + my_col, 2)

            def per_node(member, state):
                rank, count, blocks, none = state
                node = home * nodes + member
                low = high = rank
                for p in range(entries):
                    mine = (struct[node, p] // own_rows == my_row).astype(jnp.int32)
                    high += mine
                held = high - low
                start = jnp.maximum(low, first)
                stop = jnp.minimum(high, first + size)
                columns = jnp.int32(0)
                for q in range(entries):
                    columns += (struct[node, q] // own_cols == my_col).astype(jnp.int32)

                def enlist():
                    def per_column(q, state):
                        order, count, blocks = state
                        other = struct[node, q]

                        def per_row(p, state):
                            at_rank, count = state
                            block = struct[node, p]
                            mine = block // own_rows == my_row

                            @pl.when(mine & (at_rank >= start) & (at_rank < stop))
                            def _():
                                at = count * FIELDS
                                todo[at] = block - my_row * own_rows
                                todo[at + 1] = other - my_col * own_cols
                                todo[at + 2] = node
                                todo[at + 3] = q
                                todo[at + 4] = group * size + at_rank - first
                                todo[at + 5] = (order == 0).astype(jnp.int32)
                                todo[at + 6] = (order == columns - 1).astype(jnp.int32)
                                todo[at + 7] = (at_rank == start).astype(jnp.int32)
                                todo[at + 8] = blocks

                            taken = mine & (at_rank >= start) & (at_rank < stop)
                            return at_rank + mine.astype(jnp.int32), count + taken.astype(jnp.int32)

                        def column():
                            return lax.fori_loop(0, entries, per_row, (low, count))[1]

                        hit = other // own_cols == my_col
                        count = lax.cond(hit, column, lambda: count)
                        step = hit.astype(jnp.int32)
                        return order + step, count, blocks + step

                    def all_empty():
                        def one(at_rank, none):
                            empty[none] = group * size + at_rank - first
                            return none + 1

                        return lax.fori_loop(start, stop, one, none)

                    _, more, further = lax.fori_loop(0, entries, per_column, (jnp.int32(0), count, blocks))
                    return more, further, lax.cond(columns == 0, all_empty, lambda: none)

                count, blocks, none = lax.cond(start < stop, enlist, lambda: (count, blocks, none))
                return high, count, blocks, none

            return lax.fori_loop(0, nodes, per_node, (jnp.int32(0),) + state)[1:]

        return lax.fori_loop(0, homes, per_home, state)

    count = none = jnp.int32(0)
    for piece, (first, size) in enumerate(spans):
        count, _, none = piece_list(first, size, (count, jnp.int32(0), none))
        ends[piece] = count
        empties[piece] = none


def make_plan(spot, struct, spans, nodes, own_rows, own_cols):
    total = struct.shape[0] // nodes * sum(size for _, size in spans)
    smem = pl.BlockSpec(memory_space=pltpu.SMEM)
    lengths = (total * struct.shape[1] * FIELDS, 2, total, 2)
    return pl.pallas_call(
        functools.partial(plan_kernel, spans, nodes, own_rows, own_cols),
        out_shape=[jax.ShapeDtypeStruct((length,), jnp.int32) for length in lengths],
        in_specs=[smem, smem],
        out_specs=[smem] * 4,
    )(spot, struct)


def product_kernel(part, sizes, nodes, homes, todo, ends, empty, empties, sigma, panel, *refs):
    outs = refs[: homes * len(sizes)]
    sbuf, xbuf, deep, obuf, ssem, xsem, osem = refs[homes * len(sizes) :]
    width = sbuf.shape[1]
    slots = sum(sizes)
    begin = ends[part - 1] if part else 0
    end = ends[part]
    none_begin = empties[part - 1] if part else 0
    none_end = empties[part]

    def put(slot):
        group = slot // slots
        inside = slot - group * slots
        first = 0
        for piece, size in enumerate(sizes):
            @pl.when((inside >= first) & (inside < first + size))
            def _(piece=piece, first=first):
                for other in range(homes):
                    @pl.when(group == other)
                    def _(out=outs[piece * homes + other]):
                        pltpu.make_async_copy(obuf.at[slot], out.at[inside - first], osem.at[slot]).start()

            first += size

    def settle(slot):
        pltpu.make_async_copy(obuf.at[slot], outs[0].at[0], osem.at[slot]).wait()

    def fetch(item, act):
        buf = lax.rem(item, BUFS)
        at = item * FIELDS
        top = pl.multiple_of(todo[at] * width, width)
        left = pl.multiple_of(todo[at + 1] * width, width)
        act(pltpu.make_async_copy(sigma.at[pl.ds(top, width), pl.ds(left, width)], sbuf.at[buf], ssem.at[buf]))

        @pl.when(todo[at + 7] == 1)
        def _():
            node, q = todo[at + 2], todo[at + 3]
            xslot = lax.rem(todo[at + 8], BUFS)
            source = panel.at[:, node // nodes, lax.rem(node, nodes), q]
            act(pltpu.make_async_copy(source, xbuf.at[xslot], xsem.at[xslot]))

    for ahead in range(BUFS - 2):
        @pl.when(begin + ahead < end)
        def _():
            fetch(begin + ahead, lambda copy: copy.start())

    def blank(item, carry):
        slot = empty[item]
        obuf[slot] = jnp.zeros(obuf.shape[1:], jnp.float32)
        put(slot)
        return carry

    lax.fori_loop(none_begin, none_end, blank, 0)

    def step(item, carry):
        @pl.when(item + BUFS - 2 < end)
        def _():
            fetch(item + BUFS - 2, lambda copy: copy.start())

        fetch(item, lambda copy: copy.wait())
        at = item * FIELDS
        slot = todo[at + 4]

        @pl.when(todo[at + 7] == 1)
        def _():
            high, low = split(xbuf[lax.rem(todo[at + 8], BUFS)].reshape(width, width))
            deep[:width] = high
            deep[width : 2 * width] = low
            deep[2 * width :] = high

        high, low = split(sbuf[lax.rem(item, BUFS)])
        term = jnp.dot(
            jnp.concatenate([high, high, low], axis=1), deep[...], preferred_element_type=jnp.float32
        )
        obuf[slot] = term + jnp.where(todo[at + 5] == 1, 0.0, obuf[slot])

        @pl.when(todo[at + 6] == 1)
        def _():
            put(slot)

        return carry

    lax.fori_loop(begin, end, step, 0)

    def drain(item, carry):
        @pl.when(todo[item * FIELDS + 6] == 1)
        def _():
            settle(todo[item * FIELDS + 4])

        return carry

    lax.fori_loop(begin, end, drain, 0)

    def drain_blank(item, carry):
        settle(empty[item])
        return carry

    lax.fori_loop(none_begin, none_end, drain_blank, 0)


def local_product(plan, sigma, panel, homes, part, sizes):
    rows, _, nodes, _, strip, width = panel.shape
    total = homes * sum(sizes)
    hbm = pl.BlockSpec(memory_space=pl.ANY)
    smem = pl.BlockSpec(memory_space=pltpu.SMEM)
    return pl.pallas_call(
        functools.partial(product_kernel, part, sizes, nodes, homes),
        out_shape=[jax.ShapeDtypeStruct((size, width, width), jnp.float32) for size in sizes for _ in range(homes)],
        in_specs=[smem] * 4 + [hbm, hbm],
        out_specs=[hbm] * (homes * len(sizes)),
        scratch_shapes=[
            pltpu.VMEM((BUFS, width, width), jnp.float32),
            pltpu.VMEM((BUFS, rows, strip, width), jnp.float32),
            pltpu.VMEM((3 * width, width), jnp.bfloat16),
            pltpu.VMEM((total, width, width), jnp.float32),
            pltpu.SemaphoreType.DMA((BUFS,)),
            pltpu.SemaphoreType.DMA((BUFS,)),
            pltpu.SemaphoreType.DMA((total,)),
        ],
        compiler_params=pltpu.CompilerParams(vmem_limit_bytes=50 * MIB),
        cost_estimate=pl.CostEstimate(flops=width, bytes_accessed=width, transcendentals=0),
    )(*plan, sigma, panel)


def corner_kernel(base, sizes, own_rows, spot, own_struct, panel, *refs):
    totals, refs = refs[: len(sizes)], refs[len(sizes) :]
    if base:
        before, whole, own, out, gram, right, xbuf, xsem = refs
    else:
        gram, right, xbuf, xsem = refs
    nodes, entries = own_struct.shape
    width = gram.shape[1]
    my_row, my_col = spot[0], spot[1]
    slots = sum(sizes)

    def walk(act):
        def per_pair(pair, rank):
            node, p = pair // entries, lax.rem(pair, entries)
            mine = own_struct[node, p] // own_rows == my_row
            slot = rank - base

            @pl.when(mine & (slot >= 0) & (slot < slots))
            def _():
                act(node, slot, pltpu.make_async_copy(panel.at[:, my_col, node, p], xbuf.at[slot], xsem.at[slot]))

            return rank + mine.astype(jnp.int32)

        lax.fori_loop(0, nodes * entries, per_pair, jnp.int32(0))

    walk(lambda node, slot, copy: copy.start())
    gram[...] = before[...] if base else jnp.zeros(gram.shape, jnp.float32)

    def gather(node, slot, copy):
        copy.wait()
        left = xbuf[slot].reshape(width, width).T
        first = 0
        for total, size in zip(totals, sizes):
            @pl.when((slot >= first) & (slot < first + size))
            def _(total=total, first=first):
                right[...] = total[slot - first]

            first += size
        gram[node] += triple_dot(left, right[...])

    walk(gather)
    if base:
        def close(node, carry):
            inverse, mine = whole[node], own[node]
            out[node] = triple_dot(inverse.T, triple_dot(gram[node], inverse)) + triple_dot(mine.T, mine)
            return carry

        lax.fori_loop(0, nodes, close, 0)


def corner(spot, own_struct, panel, totals, base, sizes, own_rows, *ending):
    rows, _, nodes, _, strip, width = panel.shape
    vmem = pl.BlockSpec(memory_space=pltpu.VMEM)
    smem = pl.BlockSpec(memory_space=pltpu.SMEM)
    blocks = (nodes, width, width)
    return pl.pallas_call(
        functools.partial(corner_kernel, base, sizes, own_rows),
        out_shape=jax.ShapeDtypeStruct(blocks, jnp.float32),
        in_specs=[smem, smem, pl.BlockSpec(memory_space=pl.ANY)] + [vmem] * (len(totals) + len(ending)),
        out_specs=vmem,
        scratch_shapes=([pltpu.VMEM(blocks, jnp.float32)] if base else [])
        + [
            pltpu.VMEM((width, width), jnp.float32),
            pltpu.VMEM((sum(sizes), rows, strip, width), jnp.float32),
            pltpu.SemaphoreType.DMA((sum(sizes),)),
        ],
        compiler_params=pltpu.CompilerParams(vmem_limit_bytes=50 * MIB),
        cost_estimate=pl.CostEstimate(flops=6 * 8 * width**3, bytes_accessed=8 * MIB, transcendentals=0),
    )(spot, own_struct, panel, *totals, *ending)


def finish_kernel(sizes, shape, holder, rank, whole, *refs):
    nodes, entries, strip, width = shape
    arrived, (off, raw) = refs[: len(sizes)], refs[len(sizes) :]

    def per_node(node, carry):
        def pick(entry, carry):
            at = node * entries + entry
            first = 0
            for blocks, size in zip(arrived, sizes):
                slot = rank[at] - first

                @pl.when((slot >= 0) & (slot < size))
                def _(blocks=blocks, size=size, slot=slot):
                    raw[pl.ds(pl.multiple_of(entry * strip, strip), strip), :] = blocks[holder[at] * size + slot]

                first += size
            return carry

        lax.fori_loop(0, entries, pick, 0)
        off[node] = -triple_dot(raw[...], whole[node]).reshape(entries, strip, width)
        return carry

    lax.fori_loop(0, nodes, per_node, 0)


def finish(holder, rank, shape, whole, arrived, sizes):
    nodes, entries, strip, width = shape
    vmem = pl.BlockSpec(memory_space=pltpu.VMEM)
    smem = pl.BlockSpec(memory_space=pltpu.SMEM)
    return pl.pallas_call(
        functools.partial(finish_kernel, sizes, shape),
        out_shape=jax.ShapeDtypeStruct(shape, jnp.float32),
        in_specs=[smem] * 2 + [vmem] * (1 + len(arrived)),
        out_specs=vmem,
        scratch_shapes=[pltpu.VMEM((entries * strip, width), jnp.float32)],
        compiler_params=pltpu.CompilerParams(vmem_limit_bytes=50 * MIB),
        cost_estimate=pl.CostEstimate(flops=6 * nodes * entries * strip * width**2, bytes_accessed=8 * MIB, transcendentals=0),
    )(holder, rank, whole, *arrived)


def per_device(rows, homes, sigma_anc, panel, diag_inv, structure):
    nodes, entries, strip, width = panel.shape
    own_rows, own_cols = sigma_anc.shape[0] // width, sigma_anc.shape[1] // width
    chips = homes // 2

    struct = lax.all_gather(structure, "col", axis=0, tiled=True)
    every_panel = lax.all_gather(panel, ("row", "col"), axis=0, tiled=False)
    own_inverse, every_panel = lax.optimization_barrier((diag_inv, every_panel))
    inverse = lax.all_gather(own_inverse, "row", axis=1, tiled=True)
    every_panel = every_panel.reshape((rows, homes) + panel.shape)

    most = nodes * min(entries, own_rows)
    first_size = max(1, min(FIRST, most - 2))
    second_size = max(1, min(SECOND, most - first_size - 1))
    levels = sorted({min(slots, most) for slots in SLOTS + (most,)})
    holders = struct.reshape(homes, -1) // own_rows
    loads = jnp.sum(holders[:, :, None] == jnp.arange(rows, dtype=jnp.int32), axis=1)
    heaviest = jnp.max(loads)
    level = sum((heaviest > slots).astype(jnp.int32) for slots in levels[:-1])

    my_row = lax.axis_index("row").astype(jnp.int32)
    my_col = lax.axis_index("col").astype(jnp.int32)
    spot = jnp.stack([my_row, my_col])
    spans = ((0, first_size), (first_size, most - first_size))
    plan = make_plan(spot, struct, spans, nodes, own_rows, own_cols)

    holder = structure.reshape(-1) // own_rows
    pair = jnp.arange(nodes * entries, dtype=jnp.int32)
    earlier = (holder[:, None] == holder[None, :]) & (pair[None, :] < pair[:, None])
    rank = jnp.sum(earlier.astype(jnp.int32), axis=1)

    order = sorted(levels, key=lambda slots: abs(slots - USUAL))
    branch = jnp.asarray([order.index(slots) for slots in levels], jnp.int32)[level]
    plan, branch, holder, rank = lax.optimization_barrier((plan, branch, holder, rank))

    sibling = [(col, col ^ 1) for col in range(homes)]

    def to_rows(total):
        strips = total.reshape(-1, rows, strip, width).transpose(1, 0, 2, 3)
        landed = lax.all_to_all(strips, "row", split_axis=0, concat_axis=0, tiled=True)
        return landed.reshape(-1, strip, width)

    def between_cores(blocks):
        return [
            blocks[2 * away] + lax.ppermute(blocks[2 * away + 1], "col", sibling) for away in range(1, chips)
        ]

    def at_home(blocks):
        return blocks[0] + lax.ppermute(blocks[1], "col", sibling)

    def between_chips(sums):
        return [
            lax.ppermute(value, "col", [(col, (col + 2 * away) % homes) for col in range(homes)])
            for away, value in enumerate(sums, 1)
        ]

    def add(first, others):
        return functools.reduce(lambda left, right: left + right, others, first)

    early = local_product(plan, sigma_anc, every_panel, homes, 0, (first_size,))
    sums = between_cores(early)
    sums, todo = lax.optimization_barrier((sums, plan[0]))
    crossed = between_chips(sums)
    late_sizes = (second_size, most - first_size - second_size)
    late = local_product([todo] + list(plan[1:]), sigma_anc, every_panel, homes, 1, late_sizes)
    home = at_home(early)

    def with_slots(slots, every_panel, diag_inv, inverse, structure, spot, holder, rank, home, crossed, late):
        last_size = slots - first_size - second_size
        sizes = (first_size, second_size, last_size)
        middle, last = late[:homes], [blocks[:last_size] for blocks in late[homes:]]

        sums = between_cores(middle)
        first = add(home, crossed)
        first, _ = lax.optimization_barrier((first, sums))
        crossed = between_chips(sums)
        second = add(at_home(middle), crossed)
        sums = between_cores(last)
        sums, crossed = lax.optimization_barrier((sums, crossed))
        third = add(at_home(last), between_chips(sums))

        arrived = [to_rows(first), to_rows(second)]
        gram = corner(spot, structure, every_panel, (first, second), 0, sizes[:2], own_rows)
        third, gram = lax.optimization_barrier((third, gram))
        arrived.append(to_rows(third))
        part = corner(
            spot, structure, every_panel, (third,), sum(sizes[:2]), sizes[2:], own_rows, gram, inverse, diag_inv
        )
        off = finish(holder, rank, panel.shape, inverse, arrived, sizes)
        return off, lax.psum_scatter(part, "row", scatter_dimension=1, tiled=True)

    branches = [functools.partial(with_slots, slots) for slots in order]
    operands = (every_panel, diag_inv, inverse, structure, spot, holder, rank, home, crossed, list(late))
    if len(branches) == 1:
        return branches[0](*operands)
    return lax.switch(branch, branches, *operands)


def solution(mesh):
    placed = (
        P(("grp", "row"), "col"),
        P(("grp", "col"), None, "row", None),
        P(("grp", "col"), "row", None),
        P("col", None),
    )
    return jax.shard_map(
        functools.partial(per_device, mesh.shape["row"], mesh.shape["col"]),
        mesh=mesh,
        in_specs=placed,
        out_specs=(P(("grp", "col"), None, "row", None), P(("grp", "col"), "row", None)),
        check_vma=False,
    )
```

```python
import functools

import jax
import jax.numpy as jnp
from jax import lax
from jax.experimental import pallas as pl
from jax.experimental.pallas import tpu as pltpu
from jax.sharding import PartitionSpec as P

SLOTS = (10, 11, 12, 14)
FIRST, SECOND, THIRD = 4, 3, 3
USUAL = 10.4
BUFS = 12
FIELDS = 9
MIB = 1024 * 1024


def split(value):
    high = value.astype(jnp.bfloat16)
    return high, (value - high.astype(jnp.float32)).astype(jnp.bfloat16)


def triple_dot(left, right):
    left_high, left_low = split(left)
    right_high, right_low = split(right)
    dot = functools.partial(jnp.dot, preferred_element_type=jnp.float32)
    return dot(left_high, right_high) + (dot(left_high, right_low) + dot(left_low, right_high))


def plan_kernel(spans, nodes, own_rows, own_cols, spot, struct, todo, ends, empty, empties):
    entries = struct.shape[1]
    homes = struct.shape[0] // nodes
    chips = homes // 2
    my_row, my_col = spot[0], spot[1]

    def piece_list(first, size, state):
        def per_home(home, state):
            distance = lax.rem(home // 2 - my_col // 2 + chips, chips)
            group = distance * 2 + lax.rem(home + my_col, 2)

            def per_node(member, state):
                rank, count, blocks, none = state
                node = home * nodes + member
                low = high = rank
                for p in range(entries):
                    mine = (struct[node, p] // own_rows == my_row).astype(jnp.int32)
                    high += mine
                held = high - low
                start = jnp.maximum(low, first)
                stop = jnp.minimum(high, first + size)
                columns = jnp.int32(0)
                for q in range(entries):
                    columns += (struct[node, q] // own_cols == my_col).astype(jnp.int32)

                def enlist():
                    def per_column(q, state):
                        order, count, blocks = state
                        other = struct[node, q]

                        def per_row(p, state):
                            at_rank, count = state
                            block = struct[node, p]
                            mine = block // own_rows == my_row

                            @pl.when(mine & (at_rank >= start) & (at_rank < stop))
                            def _():
                                at = count * FIELDS
                                todo[at] = block - my_row * own_rows
                                todo[at + 1] = other - my_col * own_cols
                                todo[at + 2] = node
                                todo[at + 3] = q
                                todo[at + 4] = group * size + at_rank - first
                                todo[at + 5] = (order == 0).astype(jnp.int32)
                                todo[at + 6] = (order == columns - 1).astype(jnp.int32)
                                todo[at + 7] = (at_rank == start).astype(jnp.int32)
                                todo[at + 8] = blocks

                            taken = mine & (at_rank >= start) & (at_rank < stop)
                            return at_rank + mine.astype(jnp.int32), count + taken.astype(jnp.int32)

                        def column():
                            return lax.fori_loop(0, entries, per_row, (low, count))[1]

                        hit = other // own_cols == my_col
                        count = lax.cond(hit, column, lambda: count)
                        step = hit.astype(jnp.int32)
                        return order + step, count, blocks + step

                    def all_empty():
                        def one(at_rank, none):
                            empty[none] = group * size + at_rank - first
                            return none + 1

                        return lax.fori_loop(start, stop, one, none)

                    _, more, further = lax.fori_loop(0, entries, per_column, (jnp.int32(0), count, blocks))
                    return more, further, lax.cond(columns == 0, all_empty, lambda: none)

                count, blocks, none = lax.cond(start < stop, enlist, lambda: (count, blocks, none))
                return high, count, blocks, none

            return lax.fori_loop(0, nodes, per_node, (jnp.int32(0),) + state)[1:]

        return lax.fori_loop(0, homes, per_home, state)

    count = none = jnp.int32(0)
    for piece, (first, size) in enumerate(spans):
        count, _, none = piece_list(first, size, (count, jnp.int32(0), none))
        ends[piece] = count
        empties[piece] = none


def make_plan(spot, struct, spans, nodes, own_rows, own_cols):
    total = struct.shape[0] // nodes * sum(size for _, size in spans)
    smem = pl.BlockSpec(memory_space=pltpu.SMEM)
    lengths = (total * struct.shape[1] * FIELDS, 2, total, 2)
    return pl.pallas_call(
        functools.partial(plan_kernel, spans, nodes, own_rows, own_cols),
        out_shape=[jax.ShapeDtypeStruct((length,), jnp.int32) for length in lengths],
        in_specs=[smem, smem],
        out_specs=[smem] * 4,
    )(spot, struct)


def product_kernel(part, sizes, nodes, homes, todo, ends, empty, empties, sigma, panel, *refs):
    outs = refs[: homes * len(sizes)]
    sbuf, xbuf, deep, obuf, ssem, xsem, osem = refs[homes * len(sizes) :]
    width = sbuf.shape[1]
    slots = sum(sizes)
    begin = ends[part - 1] if part else 0
    end = ends[part]
    none_begin = empties[part - 1] if part else 0
    none_end = empties[part]

    def put(slot):
        group = slot // slots
        inside = slot - group * slots
        first = 0
        for piece, size in enumerate(sizes):
            @pl.when((inside >= first) & (inside < first + size))
            def _(piece=piece, first=first):
                for other in range(homes):
                    @pl.when(group == other)
                    def _(out=outs[piece * homes + other]):
                        pltpu.make_async_copy(obuf.at[slot], out.at[inside - first], osem.at[slot]).start()

            first += size

    def settle(slot):
        pltpu.make_async_copy(obuf.at[slot], outs[0].at[0], osem.at[slot]).wait()

    def fetch(item, act):
        buf = lax.rem(item, BUFS)
        at = item * FIELDS
        top = pl.multiple_of(todo[at] * width, width)
        left = pl.multiple_of(todo[at + 1] * width, width)
        act(pltpu.make_async_copy(sigma.at[pl.ds(top, width), pl.ds(left, width)], sbuf.at[buf], ssem.at[buf]))

        @pl.when(todo[at + 7] == 1)
        def _():
            node, q = todo[at + 2], todo[at + 3]
            xslot = lax.rem(todo[at + 8], BUFS)
            source = panel.at[:, node // nodes, lax.rem(node, nodes), q]
            act(pltpu.make_async_copy(source, xbuf.at[xslot], xsem.at[xslot]))

    for ahead in range(BUFS - 2):
        @pl.when(begin + ahead < end)
        def _():
            fetch(begin + ahead, lambda copy: copy.start())

    def blank(item, carry):
        slot = empty[item]
        obuf[slot] = jnp.zeros(obuf.shape[1:], jnp.float32)
        put(slot)
        return carry

    lax.fori_loop(none_begin, none_end, blank, 0)

    def step(item, carry):
        @pl.when(item + BUFS - 2 < end)
        def _():
            fetch(item + BUFS - 2, lambda copy: copy.start())

        fetch(item, lambda copy: copy.wait())
        at = item * FIELDS
        slot = todo[at + 4]

        @pl.when(todo[at + 7] == 1)
        def _():
            high, low = split(xbuf[lax.rem(todo[at + 8], BUFS)].reshape(width, width))
            deep[:width] = high
            deep[width : 2 * width] = low
            deep[2 * width :] = high

        high, low = split(sbuf[lax.rem(item, BUFS)])
        term = jnp.dot(
            jnp.concatenate([high, high, low], axis=1), deep[...], preferred_element_type=jnp.float32
        )
        obuf[slot] = term + jnp.where(todo[at + 5] == 1, 0.0, obuf[slot])

        @pl.when(todo[at + 6] == 1)
        def _():
            put(slot)

        return carry

    lax.fori_loop(begin, end, step, 0)

    def drain(item, carry):
        @pl.when(todo[item * FIELDS + 6] == 1)
        def _():
            settle(todo[item * FIELDS + 4])

        return carry

    lax.fori_loop(begin, end, drain, 0)

    def drain_blank(item, carry):
        settle(empty[item])
        return carry

    lax.fori_loop(none_begin, none_end, drain_blank, 0)


def local_product(plan, sigma, panel, homes, part, sizes):
    rows, _, nodes, _, strip, width = panel.shape
    total = homes * sum(sizes)
    hbm = pl.BlockSpec(memory_space=pl.ANY)
    smem = pl.BlockSpec(memory_space=pltpu.SMEM)
    return pl.pallas_call(
        functools.partial(product_kernel, part, sizes, nodes, homes),
        out_shape=[jax.ShapeDtypeStruct((size, width, width), jnp.float32) for size in sizes for _ in range(homes)],
        in_specs=[smem] * 4 + [hbm, hbm],
        out_specs=[hbm] * (homes * len(sizes)),
        scratch_shapes=[
            pltpu.VMEM((BUFS, width, width), jnp.float32),
            pltpu.VMEM((BUFS, rows, strip, width), jnp.float32),
            pltpu.VMEM((3 * width, width), jnp.bfloat16),
            pltpu.VMEM((total, width, width), jnp.float32),
            pltpu.SemaphoreType.DMA((BUFS,)),
            pltpu.SemaphoreType.DMA((BUFS,)),
            pltpu.SemaphoreType.DMA((total,)),
        ],
        compiler_params=pltpu.CompilerParams(vmem_limit_bytes=50 * MIB),
        cost_estimate=pl.CostEstimate(flops=width, bytes_accessed=width, transcendentals=0),
    )(*plan, sigma, panel)


def corner_kernel(base, sizes, own_rows, spot, own_struct, panel, *refs):
    totals, refs = refs[: len(sizes)], refs[len(sizes) :]
    if base:
        before, whole, own, out, gram, right, xbuf, xsem = refs
    else:
        gram, right, xbuf, xsem = refs
    nodes, entries = own_struct.shape
    width = gram.shape[1]
    my_row, my_col = spot[0], spot[1]
    slots = sum(sizes)

    def walk(act):
        def per_pair(pair, rank):
            node, p = pair // entries, lax.rem(pair, entries)
            mine = own_struct[node, p] // own_rows == my_row
            slot = rank - base

            @pl.when(mine & (slot >= 0) & (slot < slots))
            def _():
                act(node, slot, pltpu.make_async_copy(panel.at[:, my_col, node, p], xbuf.at[slot], xsem.at[slot]))

            return rank + mine.astype(jnp.int32)

        lax.fori_loop(0, nodes * entries, per_pair, jnp.int32(0))

    walk(lambda node, slot, copy: copy.start())
    gram[...] = before[...] if base else jnp.zeros(gram.shape, jnp.float32)

    def gather(node, slot, copy):
        copy.wait()
        left = xbuf[slot].reshape(width, width).T
        first = 0
        for total, size in zip(totals, sizes):
            @pl.when((slot >= first) & (slot < first + size))
            def _(total=total, first=first):
                right[...] = total[slot - first]

            first += size
        gram[node] += triple_dot(left, right[...])

    walk(gather)
    if base:
        def close(node, carry):
            inverse, mine = whole[node], own[node]
            out[node] = triple_dot(inverse.T, triple_dot(gram[node], inverse)) + triple_dot(mine.T, mine)
            return carry

        lax.fori_loop(0, nodes, close, 0)


def corner(spot, own_struct, panel, totals, base, sizes, own_rows, *ending):
    rows, _, nodes, _, strip, width = panel.shape
    vmem = pl.BlockSpec(memory_space=pltpu.VMEM)
    smem = pl.BlockSpec(memory_space=pltpu.SMEM)
    blocks = (nodes, width, width)
    return pl.pallas_call(
        functools.partial(corner_kernel, base, sizes, own_rows),
        out_shape=jax.ShapeDtypeStruct(blocks, jnp.float32),
        in_specs=[smem, smem, pl.BlockSpec(memory_space=pl.ANY)] + [vmem] * (len(totals) + len(ending)),
        out_specs=vmem,
        scratch_shapes=([pltpu.VMEM(blocks, jnp.float32)] if base else [])
        + [
            pltpu.VMEM((width, width), jnp.float32),
            pltpu.VMEM((sum(sizes), rows, strip, width), jnp.float32),
            pltpu.SemaphoreType.DMA((sum(sizes),)),
        ],
        compiler_params=pltpu.CompilerParams(vmem_limit_bytes=50 * MIB),
        cost_estimate=pl.CostEstimate(flops=6 * 8 * width**3, bytes_accessed=8 * MIB, transcendentals=0),
    )(spot, own_struct, panel, *totals, *ending)


def finish_kernel(sizes, shape, holder, rank, whole, *refs):
    nodes, entries, strip, width = shape
    arrived, (off, raw) = refs[: len(sizes)], refs[len(sizes) :]

    def per_node(node, carry):
        def pick(entry, carry):
            at = node * entries + entry
            first = 0
            for blocks, size in zip(arrived, sizes):
                slot = rank[at] - first

                @pl.when((slot >= 0) & (slot < size))
                def _(blocks=blocks, size=size, slot=slot):
                    raw[pl.ds(pl.multiple_of(entry * strip, strip), strip), :] = blocks[holder[at] * size + slot]

                first += size
            return carry

        lax.fori_loop(0, entries, pick, 0)
        off[node] = -triple_dot(raw[...], whole[node]).reshape(entries, strip, width)
        return carry

    lax.fori_loop(0, nodes, per_node, 0)


def finish(holder, rank, shape, whole, arrived, sizes):
    nodes, entries, strip, width = shape
    vmem = pl.BlockSpec(memory_space=pltpu.VMEM)
    smem = pl.BlockSpec(memory_space=pltpu.SMEM)
    return pl.pallas_call(
        functools.partial(finish_kernel, sizes, shape),
        out_shape=jax.ShapeDtypeStruct(shape, jnp.float32),
        in_specs=[smem] * 2 + [vmem] * (1 + len(arrived)),
        out_specs=vmem,
        scratch_shapes=[pltpu.VMEM((entries * strip, width), jnp.float32)],
        compiler_params=pltpu.CompilerParams(vmem_limit_bytes=50 * MIB),
        cost_estimate=pl.CostEstimate(flops=6 * nodes * entries * strip * width**2, bytes_accessed=8 * MIB, transcendentals=0),
    )(holder, rank, whole, *arrived)


def per_device(rows, homes, sigma_anc, panel, diag_inv, structure):
    nodes, entries, strip, width = panel.shape
    own_rows, own_cols = sigma_anc.shape[0] // width, sigma_anc.shape[1] // width
    chips = homes // 2

    struct = lax.all_gather(structure, "col", axis=0, tiled=True)
    every_panel = lax.all_gather(panel, ("row", "col"), axis=0, tiled=False)
    own_inverse, every_panel = lax.optimization_barrier((diag_inv, every_panel))
    inverse = lax.all_gather(own_inverse, "row", axis=1, tiled=True)
    every_panel = every_panel.reshape((rows, homes) + panel.shape)

    most = nodes * min(entries, own_rows)
    first_size = max(1, min(FIRST, most - 2))
    second_size = max(1, min(SECOND, most - first_size - 1))
    levels = sorted({min(slots, most) for slots in SLOTS + (most,)})
    holders = struct.reshape(homes, -1) // own_rows
    loads = jnp.sum(holders[:, :, None] == jnp.arange(rows, dtype=jnp.int32), axis=1)
    heaviest = jnp.max(loads)
    level = sum((heaviest > slots).astype(jnp.int32) for slots in levels[:-1])

    my_row = lax.axis_index("row").astype(jnp.int32)
    my_col = lax.axis_index("col").astype(jnp.int32)
    holder = structure.reshape(-1) // own_rows
    pair = jnp.arange(nodes * entries, dtype=jnp.int32)
    earlier = (holder[:, None] == holder[None, :]) & (pair[None, :] < pair[:, None])
    rank = jnp.sum(earlier.astype(jnp.int32), axis=1)

    order = sorted(levels, key=lambda slots: abs(slots - USUAL))
    branch = jnp.asarray([order.index(slots) for slots in levels], jnp.int32)[level]
    spot = jnp.stack([my_row, my_col])
    spot, branch, holder, rank = lax.optimization_barrier((spot, branch, holder, rank))
    spans = ((0, first_size), (first_size, most - first_size))
    plan = make_plan(spot, struct, spans, nodes, own_rows, own_cols)

    sibling = [(col, col ^ 1) for col in range(homes)]

    def to_rows(total):
        strips = total.reshape(-1, rows, strip, width).transpose(1, 0, 2, 3)
        landed = lax.all_to_all(strips, "row", split_axis=0, concat_axis=0, tiled=True)
        return landed.reshape(-1, strip, width)

    def between_cores(blocks):
        return [
            blocks[2 * away] + lax.ppermute(blocks[2 * away + 1], "col", sibling) for away in range(1, chips)
        ]

    def at_home(blocks):
        return blocks[0] + lax.ppermute(blocks[1], "col", sibling)

    def between_chips(sums):
        return [
            lax.ppermute(value, "col", [(col, (col + 2 * away) % homes) for col in range(homes)])
            for away, value in enumerate(sums, 1)
        ]

    def add(first, others):
        return functools.reduce(lambda left, right: left + right, others, first)

    early = local_product(plan, sigma_anc, every_panel, homes, 0, (first_size,))
    sums = between_cores(early)
    sums, todo = lax.optimization_barrier((sums, plan[0]))
    crossed = between_chips(sums)
    third_size = min(THIRD, most - first_size - second_size)
    late_sizes = tuple(size for size in (second_size, third_size, most - first_size - second_size - third_size) if size)
    late = local_product([todo] + list(plan[1:]), sigma_anc, every_panel, homes, 1, late_sizes)
    home = at_home(early)

    def with_slots(slots, every_panel, diag_inv, inverse, structure, spot, holder, rank, home, crossed, late):
        last_size = slots - first_size - second_size
        sizes = (first_size, second_size, last_size)
        middle, last = late[:homes], late[homes : 2 * homes]
        if last_size > third_size:
            rest = late[2 * homes :]
            last = [
                jnp.concatenate([blocks, more[: last_size - third_size]], axis=0) for blocks, more in zip(last, rest)
            ]

        sums = between_cores(middle)
        first = add(home, crossed)
        first, _ = lax.optimization_barrier((first, sums))
        crossed = between_chips(sums)
        second = add(at_home(middle), crossed)
        sums = between_cores(last)
        sums, crossed = lax.optimization_barrier((sums, crossed))
        third = add(at_home(last), between_chips(sums))

        arrived = [to_rows(first), to_rows(second)]
        gram = corner(spot, structure, every_panel, (first, second), 0, sizes[:2], own_rows)
        third, gram = lax.optimization_barrier((third, gram))
        arrived.append(to_rows(third))
        part = corner(
            spot, structure, every_panel, (third,), sum(sizes[:2]), sizes[2:], own_rows, gram, inverse, diag_inv
        )
        off = finish(holder, rank, panel.shape, inverse, arrived, sizes)
        return off, lax.psum_scatter(part, "row", scatter_dimension=1, tiled=True)

    branches = [functools.partial(with_slots, slots) for slots in order]
    operands = (every_panel, diag_inv, inverse, structure, spot, holder, rank, home, crossed, list(late))
    if len(branches) == 1:
        return branches[0](*operands)
    return lax.switch(branch, branches, *operands)


def solution(mesh):
    placed = (
        P(("grp", "row"), "col"),
        P(("grp", "col"), None, "row", None),
        P(("grp", "col"), "row", None),
        P("col", None),
    )
    return jax.shard_map(
        functools.partial(per_device, mesh.shape["row"], mesh.shape["col"]),
        mesh=mesh,
        in_specs=placed,
        out_specs=(P(("grp", "col"), None, "row", None), P(("grp", "col"), "row", None)),
        check_vma=False,
    )
```

```python
import functools

import jax
import jax.numpy as jnp
from jax import lax
from jax.experimental import pallas as pl
from jax.experimental.pallas import tpu as pltpu
from jax.sharding import PartitionSpec as P

SLOTS = (9, 10, 11, 12, 13, 15)
FIRST, SECOND = 3, 3
USUAL = 10.4
BUFS = 12
FIELDS = 9
MIB = 1024 * 1024


def split(value):
    high = value.astype(jnp.bfloat16)
    return high, (value - high.astype(jnp.float32)).astype(jnp.bfloat16)


def triple_dot(left, right):
    left_high, left_low = split(left)
    right_high, right_low = split(right)
    dot = functools.partial(jnp.dot, preferred_element_type=jnp.float32)
    return dot(left_high, right_high) + (dot(left_high, right_low) + dot(left_low, right_high))


class Part:
    def __init__(self, numbers, start):
        self.numbers, self.start = numbers, start

    def __getitem__(self, index):
        return self.numbers[self.start + index]

    def __setitem__(self, index, value):
        self.numbers[self.start + index] = value


def parts_of(lists, total, entries, spans):
    starts = [0, total * entries * FIELDS]
    starts.append(starts[-1] + spans)
    starts.append(starts[-1] + total)
    return [Part(lists, start) for start in starts], starts[-1] + spans


def plan_kernel(spans, total, nodes, own_rows, own_cols, spot, struct, lists):
    entries = struct.shape[1]
    (todo, ends, empty, empties), _ = parts_of(lists, total, entries, len(spans))
    homes = struct.shape[0] // nodes
    chips = homes // 2
    my_row, my_col = spot[0], spot[1]

    def piece_list(first, size, state):
        def per_home(home, state):
            distance = lax.rem(home // 2 - my_col // 2 + chips, chips)
            group = distance * 2 + lax.rem(home + my_col, 2)

            def per_node(member, state):
                rank, count, blocks, none = state
                node = home * nodes + member
                low = high = rank
                for p in range(entries):
                    mine = (struct[node, p] // own_rows == my_row).astype(jnp.int32)
                    high += mine
                held = high - low
                start = jnp.maximum(low, first)
                stop = jnp.minimum(high, first + size)
                columns = jnp.int32(0)
                for q in range(entries):
                    columns += (struct[node, q] // own_cols == my_col).astype(jnp.int32)

                def enlist():
                    def per_column(q, state):
                        order, count, blocks = state
                        other = struct[node, q]

                        def per_row(p, state):
                            at_rank, count = state
                            block = struct[node, p]
                            mine = block // own_rows == my_row

                            @pl.when(mine & (at_rank >= start) & (at_rank < stop))
                            def _():
                                at = count * FIELDS
                                todo[at] = block - my_row * own_rows
                                todo[at + 1] = other - my_col * own_cols
                                todo[at + 2] = node
                                todo[at + 3] = q
                                todo[at + 4] = group * size + at_rank - first
                                todo[at + 5] = (order == 0).astype(jnp.int32)
                                todo[at + 6] = (order == columns - 1).astype(jnp.int32)
                                todo[at + 7] = (at_rank == start).astype(jnp.int32)
                                todo[at + 8] = blocks

                            taken = mine & (at_rank >= start) & (at_rank < stop)
                            return at_rank + mine.astype(jnp.int32), count + taken.astype(jnp.int32)

                        def column():
                            return lax.fori_loop(0, entries, per_row, (low, count))[1]

                        hit = other // own_cols == my_col
                        count = lax.cond(hit, column, lambda: count)
                        step = hit.astype(jnp.int32)
                        return order + step, count, blocks + step

                    def all_empty():
                        def one(at_rank, none):
                            empty[none] = group * size + at_rank - first
                            return none + 1

                        return lax.fori_loop(start, stop, one, none)

                    _, more, further = lax.fori_loop(0, entries, per_column, (jnp.int32(0), count, blocks))
                    return more, further, lax.cond(columns == 0, all_empty, lambda: none)

                count, blocks, none = lax.cond(start < stop, enlist, lambda: (count, blocks, none))
                return high, count, blocks, none

            return lax.fori_loop(0, nodes, per_node, (jnp.int32(0),) + state)[1:]

        return lax.fori_loop(0, homes, per_home, state)

    count = none = jnp.int32(0)
    for piece, (first, size) in enumerate(spans):
        count, _, none = piece_list(first, size, (count, jnp.int32(0), none))
        ends[piece] = count
        empties[piece] = none


def make_plan(spot, struct, spans, nodes, own_rows, own_cols):
    total = struct.shape[0] // nodes * sum(size for _, size in spans)
    smem = pl.BlockSpec(memory_space=pltpu.SMEM)
    length = parts_of(None, total, struct.shape[1], len(spans))[1]
    return pl.pallas_call(
        functools.partial(plan_kernel, spans, total, nodes, own_rows, own_cols),
        out_shape=jax.ShapeDtypeStruct((length,), jnp.int32),
        in_specs=[smem, smem],
        out_specs=smem,
    )(spot, struct)


def product_kernel(part, planned, sizes, nodes, homes, lists, sigma, panel, *refs):
    (todo, ends, empty, empties), _ = parts_of(lists, *planned)
    outs = refs[: homes * len(sizes)]
    sbuf, xbuf, deep, obuf, ssem, xsem, osem = refs[homes * len(sizes) :]
    width = sbuf.shape[1]
    slots = sum(sizes)
    begin = ends[part - 1] if part else 0
    end = ends[part]
    none_begin = empties[part - 1] if part else 0
    none_end = empties[part]

    def put(slot):
        group = slot // slots
        inside = slot - group * slots
        first = 0
        for piece, size in enumerate(sizes):
            @pl.when((inside >= first) & (inside < first + size))
            def _(piece=piece, first=first):
                for other in range(homes):
                    @pl.when(group == other)
                    def _(out=outs[piece * homes + other]):
                        pltpu.make_async_copy(obuf.at[slot], out.at[inside - first], osem.at[slot]).start()

            first += size

    def settle(slot):
        pltpu.make_async_copy(obuf.at[slot], outs[0].at[0], osem.at[slot]).wait()

    def fetch(item, act):
        buf = lax.rem(item, BUFS)
        at = item * FIELDS
        top = pl.multiple_of(todo[at] * width, width)
        left = pl.multiple_of(todo[at + 1] * width, width)
        act(pltpu.make_async_copy(sigma.at[pl.ds(top, width), pl.ds(left, width)], sbuf.at[buf], ssem.at[buf]))

        @pl.when(todo[at + 7] == 1)
        def _():
            node, q = todo[at + 2], todo[at + 3]
            xslot = lax.rem(todo[at + 8], BUFS)
            source = panel.at[:, node // nodes, lax.rem(node, nodes), q]
            act(pltpu.make_async_copy(source, xbuf.at[xslot], xsem.at[xslot]))

    for ahead in range(BUFS - 2):
        @pl.when(begin + ahead < end)
        def _():
            fetch(begin + ahead, lambda copy: copy.start())

    def blank(item, carry):
        slot = empty[item]
        obuf[slot] = jnp.zeros(obuf.shape[1:], jnp.float32)
        put(slot)
        return carry

    lax.fori_loop(none_begin, none_end, blank, 0)

    def step(item, carry):
        @pl.when(item + BUFS - 2 < end)
        def _():
            fetch(item + BUFS - 2, lambda copy: copy.start())

        fetch(item, lambda copy: copy.wait())
        at = item * FIELDS
        slot = todo[at + 4]

        @pl.when(todo[at + 7] == 1)
        def _():
            high, low = split(xbuf[lax.rem(todo[at + 8], BUFS)].reshape(width, width))
            deep[:width] = high
            deep[width : 2 * width] = low
            deep[2 * width :] = high

        high, low = split(sbuf[lax.rem(item, BUFS)])
        term = jnp.dot(
            jnp.concatenate([high, high, low], axis=1), deep[...], preferred_element_type=jnp.float32
        )
        obuf[slot] = term + jnp.where(todo[at + 5] == 1, 0.0, obuf[slot])

        @pl.when(todo[at + 6] == 1)
        def _():
            put(slot)

        return carry

    lax.fori_loop(begin, end, step, 0)

    def drain(item, carry):
        @pl.when(todo[item * FIELDS + 6] == 1)
        def _():
            settle(todo[item * FIELDS + 4])

        return carry

    lax.fori_loop(begin, end, drain, 0)

    def drain_blank(item, carry):
        settle(empty[item])
        return carry

    lax.fori_loop(none_begin, none_end, drain_blank, 0)


def local_product(plan, sigma, panel, homes, part, planned, sizes):
    rows, _, nodes, _, strip, width = panel.shape
    total = homes * sum(sizes)
    hbm = pl.BlockSpec(memory_space=pl.ANY)
    smem = pl.BlockSpec(memory_space=pltpu.SMEM)
    return pl.pallas_call(
        functools.partial(product_kernel, part, planned, sizes, nodes, homes),
        out_shape=[jax.ShapeDtypeStruct((size, width, width), jnp.float32) for size in sizes for _ in range(homes)],
        in_specs=[smem, hbm, hbm],
        out_specs=[hbm] * (homes * len(sizes)),
        scratch_shapes=[
            pltpu.VMEM((BUFS, width, width), jnp.float32),
            pltpu.VMEM((BUFS, rows, strip, width), jnp.float32),
            pltpu.VMEM((3 * width, width), jnp.bfloat16),
            pltpu.VMEM((total, width, width), jnp.float32),
            pltpu.SemaphoreType.DMA((BUFS,)),
            pltpu.SemaphoreType.DMA((BUFS,)),
            pltpu.SemaphoreType.DMA((total,)),
        ],
        compiler_params=pltpu.CompilerParams(vmem_limit_bytes=50 * MIB),
        cost_estimate=pl.CostEstimate(flops=width, bytes_accessed=width, transcendentals=0),
    )(plan, sigma, panel)


def corner_kernel(base, sizes, own_rows, spot, own_struct, panel, *refs):
    totals, refs = refs[: len(sizes)], refs[len(sizes) :]
    if base:
        before, whole, own, out, gram, right, xbuf, xsem = refs
    else:
        gram, right, xbuf, xsem = refs
    nodes, entries = own_struct.shape
    width = gram.shape[1]
    my_row, my_col = spot[0], spot[1]
    slots = sum(sizes)

    def walk(act):
        def per_pair(pair, rank):
            node, p = pair // entries, lax.rem(pair, entries)
            mine = own_struct[node, p] // own_rows == my_row
            slot = rank - base

            @pl.when(mine & (slot >= 0) & (slot < slots))
            def _():
                act(node, slot, pltpu.make_async_copy(panel.at[:, my_col, node, p], xbuf.at[slot], xsem.at[slot]))

            return rank + mine.astype(jnp.int32)

        lax.fori_loop(0, nodes * entries, per_pair, jnp.int32(0))

    walk(lambda node, slot, copy: copy.start())
    gram[...] = before[...] if base else jnp.zeros(gram.shape, jnp.float32)

    def gather(node, slot, copy):
        copy.wait()
        left = xbuf[slot].reshape(width, width).T
        first = 0
        for total, size in zip(totals, sizes):
            @pl.when((slot >= first) & (slot < first + size))
            def _(total=total, first=first):
                right[...] = total[slot - first]

            first += size
        gram[node] += triple_dot(left, right[...])

    walk(gather)
    if base:
        def close(node, carry):
            inverse, mine = whole[node], own[node]
            out[node] = triple_dot(inverse.T, triple_dot(gram[node], inverse)) + triple_dot(mine.T, mine)
            return carry

        lax.fori_loop(0, nodes, close, 0)


def corner(spot, own_struct, panel, totals, base, sizes, own_rows, *ending):
    rows, _, nodes, _, strip, width = panel.shape
    vmem = pl.BlockSpec(memory_space=pltpu.VMEM)
    smem = pl.BlockSpec(memory_space=pltpu.SMEM)
    blocks = (nodes, width, width)
    return pl.pallas_call(
        functools.partial(corner_kernel, base, sizes, own_rows),
        out_shape=jax.ShapeDtypeStruct(blocks, jnp.float32),
        in_specs=[smem, smem, pl.BlockSpec(memory_space=pl.ANY)] + [vmem] * (len(totals) + len(ending)),
        out_specs=vmem,
        scratch_shapes=([pltpu.VMEM(blocks, jnp.float32)] if base else [])
        + [
            pltpu.VMEM((width, width), jnp.float32),
            pltpu.VMEM((sum(sizes), rows, strip, width), jnp.float32),
            pltpu.SemaphoreType.DMA((sum(sizes),)),
        ],
        compiler_params=pltpu.CompilerParams(vmem_limit_bytes=50 * MIB),
        cost_estimate=pl.CostEstimate(flops=6 * 8 * width**3, bytes_accessed=8 * MIB, transcendentals=0),
    )(spot, own_struct, panel, *totals, *ending)


def finish_kernel(sizes, shape, holder, rank, whole, *refs):
    nodes, entries, strip, width = shape
    arrived, (off, raw) = refs[: len(sizes)], refs[len(sizes) :]

    def per_node(node, carry):
        def pick(entry, carry):
            at = node * entries + entry
            first = 0
            for blocks, size in zip(arrived, sizes):
                slot = rank[at] - first

                @pl.when((slot >= 0) & (slot < size))
                def _(blocks=blocks, size=size, slot=slot):
                    raw[pl.ds(pl.multiple_of(entry * strip, strip), strip), :] = blocks[holder[at] * size + slot]

                first += size
            return carry

        lax.fori_loop(0, entries, pick, 0)
        off[node] = -triple_dot(raw[...], whole[node]).reshape(entries, strip, width)
        return carry

    lax.fori_loop(0, nodes, per_node, 0)


def finish(holder, rank, shape, whole, arrived, sizes):
    nodes, entries, strip, width = shape
    vmem = pl.BlockSpec(memory_space=pltpu.VMEM)
    smem = pl.BlockSpec(memory_space=pltpu.SMEM)
    return pl.pallas_call(
        functools.partial(finish_kernel, sizes, shape),
        out_shape=jax.ShapeDtypeStruct(shape, jnp.float32),
        in_specs=[smem] * 2 + [vmem] * (1 + len(arrived)),
        out_specs=vmem,
        scratch_shapes=[pltpu.VMEM((entries * strip, width), jnp.float32)],
        compiler_params=pltpu.CompilerParams(vmem_limit_bytes=50 * MIB),
        cost_estimate=pl.CostEstimate(flops=6 * nodes * entries * strip * width**2, bytes_accessed=8 * MIB, transcendentals=0),
    )(holder, rank, whole, *arrived)


def per_device(rows, homes, sigma_anc, panel, diag_inv, structure):
    nodes, entries, strip, width = panel.shape
    own_rows, own_cols = sigma_anc.shape[0] // width, sigma_anc.shape[1] // width
    chips = homes // 2

    struct = lax.all_gather(structure, "col", axis=0, tiled=True)
    every_panel = lax.all_gather(panel, ("row", "col"), axis=0, tiled=False)
    own_inverse, every_panel = lax.optimization_barrier((diag_inv, every_panel))
    inverse = lax.all_gather(own_inverse, "row", axis=1, tiled=True)
    every_panel = every_panel.reshape((rows, homes) + panel.shape)

    most = nodes * min(entries, own_rows)
    first_size = max(1, min(FIRST, most - 2))
    second_size = max(1, min(SECOND, most - first_size - 1))
    levels = sorted({min(slots, most) for slots in SLOTS + (most,)})
    holders = struct.reshape(homes, -1) // own_rows
    loads = jnp.sum(holders[:, :, None] == jnp.arange(rows, dtype=jnp.int32), axis=1)
    heaviest = jnp.max(loads)
    level = sum((heaviest > slots).astype(jnp.int32) for slots in levels[:-1])

    my_row = lax.axis_index("row").astype(jnp.int32)
    my_col = lax.axis_index("col").astype(jnp.int32)
    spot = jnp.stack([my_row, my_col])
    spans = ((0, first_size), (first_size, most - first_size))
    plan = make_plan(spot, struct, spans, nodes, own_rows, own_cols)

    holder = structure.reshape(-1) // own_rows
    pair = jnp.arange(nodes * entries, dtype=jnp.int32)
    earlier = (holder[:, None] == holder[None, :]) & (pair[None, :] < pair[:, None])
    rank = jnp.sum(earlier.astype(jnp.int32), axis=1)

    order = sorted(levels, key=lambda slots: abs(slots - USUAL))
    branch = jnp.asarray([order.index(slots) for slots in levels], jnp.int32)[level]
    plan, branch, holder, rank = lax.optimization_barrier((plan, branch, holder, rank))

    sibling = [(col, col ^ 1) for col in range(homes)]

    def to_rows(total):
        strips = total.reshape(-1, rows, strip, width).transpose(1, 0, 2, 3)
        landed = lax.all_to_all(strips, "row", split_axis=0, concat_axis=0, tiled=True)
        return landed.reshape(-1, strip, width)

    def between_cores(blocks):
        return [
            blocks[2 * away] + lax.ppermute(blocks[2 * away + 1], "col", sibling) for away in range(1, chips)
        ]

    def at_home(blocks):
        return blocks[0] + lax.ppermute(blocks[1], "col", sibling)

    def between_chips(sums):
        return [
            lax.ppermute(value, "col", [(col, (col + 2 * away) % homes) for col in range(homes)])
            for away, value in enumerate(sums, 1)
        ]

    def add(first, others):
        return functools.reduce(lambda left, right: left + right, others, first)

    planned = (homes * most, entries, len(spans))
    early = local_product(plan, sigma_anc, every_panel, homes, 0, planned, (first_size,))
    sums = between_cores(early)
    sums, plan = lax.optimization_barrier((sums, plan))
    crossed = between_chips(sums)
    late_sizes = (second_size, most - first_size - second_size)
    late = local_product(plan, sigma_anc, every_panel, homes, 1, planned, late_sizes)
    home = at_home(early)

    def with_slots(slots, every_panel, diag_inv, inverse, structure, spot, holder, rank, home, crossed, late):
        last_size = slots - first_size - second_size
        sizes = (first_size, second_size, last_size)
        middle, last = late[:homes], [blocks[:last_size] for blocks in late[homes:]]

        sums = between_cores(middle)
        first = add(home, crossed)
        first, _ = lax.optimization_barrier((first, sums))
        crossed = between_chips(sums)
        second = add(at_home(middle), crossed)
        sums = between_cores(last)
        sums, crossed = lax.optimization_barrier((sums, crossed))
        third = add(at_home(last), between_chips(sums))

        arrived = [to_rows(first), to_rows(second)]
        gram = corner(spot, structure, every_panel, (first, second), 0, sizes[:2], own_rows)
        third, gram = lax.optimization_barrier((third, gram))
        arrived.append(to_rows(third))
        part = corner(
            spot, structure, every_panel, (third,), sum(sizes[:2]), sizes[2:], own_rows, gram, inverse, diag_inv
        )
        off = finish(holder, rank, panel.shape, inverse, arrived, sizes)
        return off, lax.psum_scatter(part, "row", scatter_dimension=1, tiled=True)

    branches = [functools.partial(with_slots, slots) for slots in order]
    operands = (every_panel, diag_inv, inverse, structure, spot, holder, rank, home, crossed, list(late))
    if len(branches) == 1:
        return branches[0](*operands)
    return lax.switch(branch, branches, *operands)


def solution(mesh):
    placed = (
        P(("grp", "row"), "col"),
        P(("grp", "col"), None, "row", None),
        P(("grp", "col"), "row", None),
        P("col", None),
    )
    return jax.shard_map(
        functools.partial(per_device, mesh.shape["row"], mesh.shape["col"]),
        mesh=mesh,
        in_specs=placed,
        out_specs=(P(("grp", "col"), None, "row", None), P(("grp", "col"), "row", None)),
        check_vma=False,
    )
```

```python
import functools

import jax
import jax.numpy as jnp
from jax import lax
from jax.experimental import pallas as pl
from jax.experimental.pallas import tpu as pltpu
from jax.sharding import PartitionSpec as P

SLOTS = (9, 10, 11, 12, 13, 15, 18)
FIRST, SECOND = 3, 4
LARGEST = 6
USUAL = 10.4
BUFS = 12
FIELDS = 9
MIB = 1024 * 1024


def split(value):
    high = value.astype(jnp.bfloat16)
    return high, (value - high.astype(jnp.float32)).astype(jnp.bfloat16)


def triple_dot(left, right):
    left_high, left_low = split(left)
    right_high, right_low = split(right)
    dot = functools.partial(jnp.dot, preferred_element_type=jnp.float32)
    return dot(left_high, right_high) + (dot(left_high, right_low) + dot(left_low, right_high))


class Part:
    def __init__(self, numbers, start):
        self.numbers, self.start = numbers, start

    def __getitem__(self, index):
        return self.numbers[self.start + index]

    def __setitem__(self, index, value):
        self.numbers[self.start + index] = value


def parts_of(lists, total, entries, spans):
    starts = [0, total * entries * FIELDS]
    starts.append(starts[-1] + spans)
    starts.append(starts[-1] + total)
    return [Part(lists, start) for start in starts], starts[-1] + spans


def plan_kernel(spans, total, nodes, own_rows, own_cols, spot, struct, lists):
    entries = struct.shape[1]
    (todo, ends, empty, empties), _ = parts_of(lists, total, entries, len(spans))
    homes = struct.shape[0] // nodes
    chips = homes // 2
    my_row, my_col = spot[0], spot[1]

    def piece_list(first, size, state):
        def per_home(home, state):
            distance = lax.rem(home // 2 - my_col // 2 + chips, chips)
            group = distance * 2 + lax.rem(home + my_col, 2)

            def per_node(member, state):
                rank, count, blocks, none = state
                node = home * nodes + member
                low = high = rank
                for p in range(entries):
                    mine = (struct[node, p] // own_rows == my_row).astype(jnp.int32)
                    high += mine
                held = high - low
                start = jnp.maximum(low, first)
                stop = jnp.minimum(high, first + size)
                columns = jnp.int32(0)
                for q in range(entries):
                    columns += (struct[node, q] // own_cols == my_col).astype(jnp.int32)

                def enlist():
                    def per_column(q, state):
                        order, count, blocks = state
                        other = struct[node, q]

                        def per_row(p, state):
                            at_rank, count = state
                            block = struct[node, p]
                            mine = block // own_rows == my_row

                            @pl.when(mine & (at_rank >= start) & (at_rank < stop))
                            def _():
                                at = count * FIELDS
                                todo[at] = block - my_row * own_rows
                                todo[at + 1] = other - my_col * own_cols
                                todo[at + 2] = node
                                todo[at + 3] = q
                                todo[at + 4] = group * size + at_rank - first
                                todo[at + 5] = (order == 0).astype(jnp.int32)
                                todo[at + 6] = (order == columns - 1).astype(jnp.int32)
                                todo[at + 7] = (at_rank == start).astype(jnp.int32)
                                todo[at + 8] = blocks

                            taken = mine & (at_rank >= start) & (at_rank < stop)
                            return at_rank + mine.astype(jnp.int32), count + taken.astype(jnp.int32)

                        def column():
                            return lax.fori_loop(0, entries, per_row, (low, count))[1]

                        hit = other // own_cols == my_col
                        count = lax.cond(hit, column, lambda: count)
                        step = hit.astype(jnp.int32)
                        return order + step, count, blocks + step

                    def all_empty():
                        def one(at_rank, none):
                            empty[none] = group * size + at_rank - first
                            return none + 1

                        return lax.fori_loop(start, stop, one, none)

                    _, more, further = lax.fori_loop(0, entries, per_column, (jnp.int32(0), count, blocks))
                    return more, further, lax.cond(columns == 0, all_empty, lambda: none)

                count, blocks, none = lax.cond(start < stop, enlist, lambda: (count, blocks, none))
                return high, count, blocks, none

            return lax.fori_loop(0, nodes, per_node, (jnp.int32(0),) + state)[1:]

        return lax.fori_loop(0, homes, per_home, state)

    count = none = jnp.int32(0)
    for piece, (first, size) in enumerate(spans):
        count, _, none = piece_list(first, size, (count, jnp.int32(0), none))
        ends[piece] = count
        empties[piece] = none


def make_plan(spot, struct, spans, nodes, own_rows, own_cols):
    total = struct.shape[0] // nodes * sum(size for _, size in spans)
    smem = pl.BlockSpec(memory_space=pltpu.SMEM)
    length = parts_of(None, total, struct.shape[1], len(spans))[1]
    return pl.pallas_call(
        functools.partial(plan_kernel, spans, total, nodes, own_rows, own_cols),
        out_shape=jax.ShapeDtypeStruct((length,), jnp.int32),
        in_specs=[smem, smem],
        out_specs=smem,
    )(spot, struct)


def product_kernel(part, planned, sizes, nodes, homes, lists, sigma, panel, *refs):
    (todo, ends, empty, empties), _ = parts_of(lists, *planned)
    outs = refs[: homes * len(sizes)]
    sbuf, xbuf, deep, obuf, ssem, xsem, osem = refs[homes * len(sizes) :]
    width = sbuf.shape[1]
    slots = sum(sizes)
    begin = ends[part - 1] if part else 0
    end = ends[part]
    none_begin = empties[part - 1] if part else 0
    none_end = empties[part]

    def put(slot):
        group = slot // slots
        inside = slot - group * slots
        first = 0
        for piece, size in enumerate(sizes):
            @pl.when((inside >= first) & (inside < first + size))
            def _(piece=piece, first=first):
                for other in range(homes):
                    @pl.when(group == other)
                    def _(out=outs[piece * homes + other]):
                        pltpu.make_async_copy(obuf.at[slot], out.at[inside - first], osem.at[slot]).start()

            first += size

    def settle(slot):
        pltpu.make_async_copy(obuf.at[slot], outs[0].at[0], osem.at[slot]).wait()

    def fetch(item, act):
        buf = lax.rem(item, BUFS)
        at = item * FIELDS
        top = pl.multiple_of(todo[at] * width, width)
        left = pl.multiple_of(todo[at + 1] * width, width)
        act(pltpu.make_async_copy(sigma.at[pl.ds(top, width), pl.ds(left, width)], sbuf.at[buf], ssem.at[buf]))

        @pl.when(todo[at + 7] == 1)
        def _():
            node, q = todo[at + 2], todo[at + 3]
            xslot = lax.rem(todo[at + 8], BUFS)
            source = panel.at[:, node // nodes, lax.rem(node, nodes), q]
            act(pltpu.make_async_copy(source, xbuf.at[xslot], xsem.at[xslot]))

    for ahead in range(BUFS - 2):
        @pl.when(begin + ahead < end)
        def _():
            fetch(begin + ahead, lambda copy: copy.start())

    def blank(item, carry):
        slot = empty[item]
        obuf[slot] = jnp.zeros(obuf.shape[1:], jnp.float32)
        put(slot)
        return carry

    lax.fori_loop(none_begin, none_end, blank, 0)

    def step(item, carry):
        @pl.when(item + BUFS - 2 < end)
        def _():
            fetch(item + BUFS - 2, lambda copy: copy.start())

        fetch(item, lambda copy: copy.wait())
        at = item * FIELDS
        slot = todo[at + 4]

        @pl.when(todo[at + 7] == 1)
        def _():
            high, low = split(xbuf[lax.rem(todo[at + 8], BUFS)].reshape(width, width))
            deep[:width] = high
            deep[width : 2 * width] = low
            deep[2 * width :] = high

        high, low = split(sbuf[lax.rem(item, BUFS)])
        term = jnp.dot(
            jnp.concatenate([high, high, low], axis=1), deep[...], preferred_element_type=jnp.float32
        )
        obuf[slot] = term + jnp.where(todo[at + 5] == 1, 0.0, obuf[slot])

        @pl.when(todo[at + 6] == 1)
        def _():
            put(slot)

        return carry

    lax.fori_loop(begin, end, step, 0)

    def drain(item, carry):
        @pl.when(todo[item * FIELDS + 6] == 1)
        def _():
            settle(todo[item * FIELDS + 4])

        return carry

    lax.fori_loop(begin, end, drain, 0)

    def drain_blank(item, carry):
        settle(empty[item])
        return carry

    lax.fori_loop(none_begin, none_end, drain_blank, 0)


def local_product(plan, sigma, panel, homes, part, planned, sizes):
    rows, _, nodes, _, strip, width = panel.shape
    total = homes * sum(sizes)
    hbm = pl.BlockSpec(memory_space=pl.ANY)
    smem = pl.BlockSpec(memory_space=pltpu.SMEM)
    return pl.pallas_call(
        functools.partial(product_kernel, part, planned, sizes, nodes, homes),
        out_shape=[jax.ShapeDtypeStruct((size, width, width), jnp.float32) for size in sizes for _ in range(homes)],
        in_specs=[smem, hbm, hbm],
        out_specs=[hbm] * (homes * len(sizes)),
        scratch_shapes=[
            pltpu.VMEM((BUFS, width, width), jnp.float32),
            pltpu.VMEM((BUFS, rows, strip, width), jnp.float32),
            pltpu.VMEM((3 * width, width), jnp.bfloat16),
            pltpu.VMEM((total, width, width), jnp.float32),
            pltpu.SemaphoreType.DMA((BUFS,)),
            pltpu.SemaphoreType.DMA((BUFS,)),
            pltpu.SemaphoreType.DMA((total,)),
        ],
        compiler_params=pltpu.CompilerParams(vmem_limit_bytes=50 * MIB),
        cost_estimate=pl.CostEstimate(flops=width, bytes_accessed=width, transcendentals=0),
    )(plan, sigma, panel)


def corner_kernel(base, sizes, own_rows, spot, own_struct, panel, *refs):
    totals, refs = refs[: len(sizes)], refs[len(sizes) :]
    if base:
        before, whole, own, out, gram, right, xbuf, xsem = refs
    else:
        gram, right, xbuf, xsem = refs
    nodes, entries = own_struct.shape
    width = gram.shape[1]
    my_row, my_col = spot[0], spot[1]
    slots = sum(sizes)

    def walk(act):
        def per_pair(pair, rank):
            node, p = pair // entries, lax.rem(pair, entries)
            mine = own_struct[node, p] // own_rows == my_row
            slot = rank - base

            @pl.when(mine & (slot >= 0) & (slot < slots))
            def _():
                act(node, slot, pltpu.make_async_copy(panel.at[:, my_col, node, p], xbuf.at[slot], xsem.at[slot]))

            return rank + mine.astype(jnp.int32)

        lax.fori_loop(0, nodes * entries, per_pair, jnp.int32(0))

    walk(lambda node, slot, copy: copy.start())
    gram[...] = before[...] if base else jnp.zeros(gram.shape, jnp.float32)

    def gather(node, slot, copy):
        copy.wait()
        left = xbuf[slot].reshape(width, width).T
        first = 0
        for total, size in zip(totals, sizes):
            @pl.when((slot >= first) & (slot < first + size))
            def _(total=total, first=first):
                right[...] = total[slot - first]

            first += size
        gram[node] += triple_dot(left, right[...])

    walk(gather)
    if base:
        def close(node, carry):
            inverse, mine = whole[node], own[node]
            out[node] = triple_dot(inverse.T, triple_dot(gram[node], inverse)) + triple_dot(mine.T, mine)
            return carry

        lax.fori_loop(0, nodes, close, 0)


def corner(spot, own_struct, panel, totals, base, sizes, own_rows, *ending):
    rows, _, nodes, _, strip, width = panel.shape
    vmem = pl.BlockSpec(memory_space=pltpu.VMEM)
    smem = pl.BlockSpec(memory_space=pltpu.SMEM)
    blocks = (nodes, width, width)
    return pl.pallas_call(
        functools.partial(corner_kernel, base, sizes, own_rows),
        out_shape=jax.ShapeDtypeStruct(blocks, jnp.float32),
        in_specs=[smem, smem, pl.BlockSpec(memory_space=pl.ANY)] + [vmem] * (len(totals) + len(ending)),
        out_specs=vmem,
        scratch_shapes=([pltpu.VMEM(blocks, jnp.float32)] if base else [])
        + [
            pltpu.VMEM((width, width), jnp.float32),
            pltpu.VMEM((sum(sizes), rows, strip, width), jnp.float32),
            pltpu.SemaphoreType.DMA((sum(sizes),)),
        ],
        compiler_params=pltpu.CompilerParams(vmem_limit_bytes=50 * MIB),
        cost_estimate=pl.CostEstimate(flops=6 * 8 * width**3, bytes_accessed=8 * MIB, transcendentals=0),
    )(spot, own_struct, panel, *totals, *ending)


def finish_kernel(sizes, shape, holder, rank, whole, *refs):
    nodes, entries, strip, width = shape
    arrived, (off, raw) = refs[: len(sizes)], refs[len(sizes) :]

    def per_node(node, carry):
        def pick(entry, carry):
            at = node * entries + entry
            first = 0
            for blocks, size in zip(arrived, sizes):
                slot = rank[at] - first

                @pl.when((slot >= 0) & (slot < size))
                def _(blocks=blocks, size=size, slot=slot):
                    raw[pl.ds(pl.multiple_of(entry * strip, strip), strip), :] = blocks[holder[at] * size + slot]

                first += size
            return carry

        lax.fori_loop(0, entries, pick, 0)
        off[node] = -triple_dot(raw[...], whole[node]).reshape(entries, strip, width)
        return carry

    lax.fori_loop(0, nodes, per_node, 0)


def finish(holder, rank, shape, whole, arrived, sizes):
    nodes, entries, strip, width = shape
    vmem = pl.BlockSpec(memory_space=pltpu.VMEM)
    smem = pl.BlockSpec(memory_space=pltpu.SMEM)
    return pl.pallas_call(
        functools.partial(finish_kernel, sizes, shape),
        out_shape=jax.ShapeDtypeStruct(shape, jnp.float32),
        in_specs=[smem] * 2 + [vmem] * (1 + len(arrived)),
        out_specs=vmem,
        scratch_shapes=[pltpu.VMEM((entries * strip, width), jnp.float32)],
        compiler_params=pltpu.CompilerParams(vmem_limit_bytes=50 * MIB),
        cost_estimate=pl.CostEstimate(flops=6 * nodes * entries * strip * width**2, bytes_accessed=8 * MIB, transcendentals=0),
    )(holder, rank, whole, *arrived)


def per_device(rows, homes, sigma_anc, panel, diag_inv, structure):
    nodes, entries, strip, width = panel.shape
    own_rows, own_cols = sigma_anc.shape[0] // width, sigma_anc.shape[1] // width
    chips = homes // 2

    struct = lax.all_gather(structure, "col", axis=0, tiled=True)
    every_panel = lax.all_gather(panel, ("row", "col"), axis=0, tiled=False)
    own_inverse, every_panel = lax.optimization_barrier((diag_inv, every_panel))
    inverse = lax.all_gather(own_inverse, "row", axis=1, tiled=True)
    every_panel = every_panel.reshape((rows, homes) + panel.shape)

    most = nodes * min(entries, own_rows)
    first_size = max(1, min(FIRST, most - 2))
    second_size = max(1, min(SECOND, most - first_size - 1))
    levels = sorted({min(slots, most) for slots in SLOTS + (most,)})
    holders = struct.reshape(homes, -1) // own_rows
    loads = jnp.sum(holders[:, :, None] == jnp.arange(rows, dtype=jnp.int32), axis=1)
    heaviest = jnp.max(loads)
    level = sum((heaviest > slots).astype(jnp.int32) for slots in levels[:-1])

    my_row = lax.axis_index("row").astype(jnp.int32)
    my_col = lax.axis_index("col").astype(jnp.int32)
    spot = jnp.stack([my_row, my_col])
    spans = ((0, first_size), (first_size, most - first_size))
    plan = make_plan(spot, struct, spans, nodes, own_rows, own_cols)

    holder = structure.reshape(-1) // own_rows
    pair = jnp.arange(nodes * entries, dtype=jnp.int32)
    earlier = (holder[:, None] == holder[None, :]) & (pair[None, :] < pair[:, None])
    rank = jnp.sum(earlier.astype(jnp.int32), axis=1)

    order = sorted(levels, key=lambda slots: abs(slots - USUAL))
    branch = jnp.asarray([order.index(slots) for slots in levels], jnp.int32)[level]
    plan, branch, holder, rank = lax.optimization_barrier((plan, branch, holder, rank))

    sibling = [(col, col ^ 1) for col in range(homes)]

    def to_rows(total):
        strips = total.reshape(-1, rows, strip, width).transpose(1, 0, 2, 3)
        landed = lax.all_to_all(strips, "row", split_axis=0, concat_axis=0, tiled=True)
        return landed.reshape(-1, strip, width)

    def between_cores(blocks):
        return [
            blocks[2 * away] + lax.ppermute(blocks[2 * away + 1], "col", sibling) for away in range(1, chips)
        ]

    def at_home(blocks):
        return blocks[0] + lax.ppermute(blocks[1], "col", sibling)

    def between_chips(sums):
        return [
            lax.ppermute(value, "col", [(col, (col + 2 * away) % homes) for col in range(homes)])
            for away, value in enumerate(sums, 1)
        ]

    def add(first, others):
        return functools.reduce(lambda left, right: left + right, others, first)

    planned = (homes * most, entries, len(spans))
    early = local_product(plan, sigma_anc, every_panel, homes, 0, planned, (first_size,))
    sums = between_cores(early)
    sums, plan = lax.optimization_barrier((sums, plan))
    crossed = between_chips(sums)
    late_sizes = (second_size, most - first_size - second_size)
    late = local_product(plan, sigma_anc, every_panel, homes, 1, planned, late_sizes)
    home = at_home(early)

    def with_slots(slots, every_panel, diag_inv, inverse, structure, spot, holder, rank, home, crossed, late):
        rest = slots - first_size - second_size
        count = -(-rest // LARGEST)
        sizes = [first_size, second_size] + [(rest + index) // count for index in reversed(range(count))]

        totals, start = [add(home, crossed)], 0
        for turn, size in enumerate(sizes[1:]):
            blocks = late[:homes] if turn == 0 else [more[start : start + size] for more in late[homes:]]
            start += size if turn else 0
            sums = between_cores(blocks)
            if turn:
                sums, crossed = lax.optimization_barrier((sums, crossed))
            else:
                totals[0], _ = lax.optimization_barrier((totals[0], sums))
            crossed = between_chips(sums)
            totals.append(add(at_home(blocks), crossed))

        arrived = [to_rows(total) for total in totals[:-1]]
        gram = corner(spot, structure, every_panel, totals[:-1], 0, sizes[:-1], own_rows)
        third, gram = lax.optimization_barrier((totals[-1], gram))
        arrived.append(to_rows(third))
        part = corner(
            spot, structure, every_panel, (third,), slots - sizes[-1], sizes[-1:], own_rows, gram, inverse, diag_inv
        )
        off = finish(holder, rank, panel.shape, inverse, arrived, sizes)
        return off, lax.psum_scatter(part, "row", scatter_dimension=1, tiled=True)

    branches = [functools.partial(with_slots, slots) for slots in order]
    operands = (every_panel, diag_inv, inverse, structure, spot, holder, rank, home, crossed, list(late))
    if len(branches) == 1:
        return branches[0](*operands)
    return lax.switch(branch, branches, *operands)


def solution(mesh):
    placed = (
        P(("grp", "row"), "col"),
        P(("grp", "col"), None, "row", None),
        P(("grp", "col"), "row", None),
        P("col", None),
    )
    return jax.shard_map(
        functools.partial(per_device, mesh.shape["row"], mesh.shape["col"]),
        mesh=mesh,
        in_specs=placed,
        out_specs=(P(("grp", "col"), None, "row", None), P(("grp", "col"), "row", None)),
        check_vma=False,
    )
```

```python
import functools

import jax
import jax.numpy as jnp
from jax import lax
from jax.experimental import pallas as pl
from jax.experimental.pallas import tpu as pltpu
from jax.sharding import PartitionSpec as P

SLOTS = (9, 10, 11, 12, 13, 15, 18)
FIRST, SECOND = 3, 5
LARGEST = 6
USUAL = 10.4
BUFS = 12
FIELDS = 9
MIB = 1024 * 1024


def split(value):
    high = value.astype(jnp.bfloat16)
    return high, (value - high.astype(jnp.float32)).astype(jnp.bfloat16)


def triple_dot(left, right):
    left_high, left_low = split(left)
    right_high, right_low = split(right)
    dot = functools.partial(jnp.dot, preferred_element_type=jnp.float32)
    return dot(left_high, right_high) + (dot(left_high, right_low) + dot(left_low, right_high))


class Part:
    def __init__(self, numbers, start):
        self.numbers, self.start = numbers, start

    def __getitem__(self, index):
        return self.numbers[self.start + index]

    def __setitem__(self, index, value):
        self.numbers[self.start + index] = value


def parts_of(lists, total, entries, spans):
    starts = [0, total * entries * FIELDS]
    starts.append(starts[-1] + spans)
    starts.append(starts[-1] + total)
    return [Part(lists, start) for start in starts], starts[-1] + spans


def plan_kernel(spans, total, nodes, own_rows, own_cols, spot, struct, lists):
    entries = struct.shape[1]
    (todo, ends, empty, empties), _ = parts_of(lists, total, entries, len(spans))
    homes = struct.shape[0] // nodes
    chips = homes // 2
    my_row, my_col = spot[0], spot[1]

    def piece_list(first, size, state):
        def per_home(home, state):
            distance = lax.rem(home // 2 - my_col // 2 + chips, chips)
            group = distance * 2 + lax.rem(home + my_col, 2)

            def per_node(member, state):
                rank, count, blocks, none = state
                node = home * nodes + member
                low = high = rank
                for p in range(entries):
                    mine = (struct[node, p] // own_rows == my_row).astype(jnp.int32)
                    high += mine
                held = high - low
                start = jnp.maximum(low, first)
                stop = jnp.minimum(high, first + size)
                columns = jnp.int32(0)
                for q in range(entries):
                    columns += (struct[node, q] // own_cols == my_col).astype(jnp.int32)

                def enlist():
                    def per_column(q, state):
                        order, count, blocks = state
                        other = struct[node, q]

                        def per_row(p, state):
                            at_rank, count = state
                            block = struct[node, p]
                            mine = block // own_rows == my_row

                            @pl.when(mine & (at_rank >= start) & (at_rank < stop))
                            def _():
                                at = count * FIELDS
                                todo[at] = block - my_row * own_rows
                                todo[at + 1] = other - my_col * own_cols
                                todo[at + 2] = node
                                todo[at + 3] = q
                                todo[at + 4] = group * size + at_rank - first
                                todo[at + 5] = (order == 0).astype(jnp.int32)
                                todo[at + 6] = (order == columns - 1).astype(jnp.int32)
                                todo[at + 7] = (at_rank == start).astype(jnp.int32)
                                todo[at + 8] = blocks

                            taken = mine & (at_rank >= start) & (at_rank < stop)
                            return at_rank + mine.astype(jnp.int32), count + taken.astype(jnp.int32)

                        def column():
                            return lax.fori_loop(0, entries, per_row, (low, count))[1]

                        hit = other // own_cols == my_col
                        count = lax.cond(hit, column, lambda: count)
                        step = hit.astype(jnp.int32)
                        return order + step, count, blocks + step

                    def all_empty():
                        def one(at_rank, none):
                            empty[none] = group * size + at_rank - first
                            return none + 1

                        return lax.fori_loop(start, stop, one, none)

                    _, more, further = lax.fori_loop(0, entries, per_column, (jnp.int32(0), count, blocks))
                    return more, further, lax.cond(columns == 0, all_empty, lambda: none)

                count, blocks, none = lax.cond(start < stop, enlist, lambda: (count, blocks, none))
                return high, count, blocks, none

            return lax.fori_loop(0, nodes, per_node, (jnp.int32(0),) + state)[1:]

        return lax.fori_loop(0, homes, per_home, state)

    count = none = jnp.int32(0)
    for piece, (first, size) in enumerate(spans):
        count, _, none = piece_list(first, size, (count, jnp.int32(0), none))
        ends[piece] = count
        empties[piece] = none


def make_plan(spot, struct, spans, nodes, own_rows, own_cols):
    total = struct.shape[0] // nodes * sum(size for _, size in spans)
    smem = pl.BlockSpec(memory_space=pltpu.SMEM)
    length = parts_of(None, total, struct.shape[1], len(spans))[1]
    return pl.pallas_call(
        functools.partial(plan_kernel, spans, total, nodes, own_rows, own_cols),
        out_shape=jax.ShapeDtypeStruct((length,), jnp.int32),
        in_specs=[smem, smem],
        out_specs=smem,
    )(spot, struct)


def product_kernel(part, planned, sizes, nodes, homes, lists, sigma, panel, *refs):
    (todo, ends, empty, empties), _ = parts_of(lists, *planned)
    outs = refs[: homes * len(sizes)]
    sbuf, xbuf, deep, obuf, ssem, xsem, osem = refs[homes * len(sizes) :]
    width = sbuf.shape[1]
    slots = sum(sizes)
    begin = ends[part - 1] if part else 0
    end = ends[part]
    none_begin = empties[part - 1] if part else 0
    none_end = empties[part]

    def put(slot):
        group = slot // slots
        inside = slot - group * slots
        first = 0
        for piece, size in enumerate(sizes):
            @pl.when((inside >= first) & (inside < first + size))
            def _(piece=piece, first=first):
                for other in range(homes):
                    @pl.when(group == other)
                    def _(out=outs[piece * homes + other]):
                        pltpu.make_async_copy(obuf.at[slot], out.at[inside - first], osem.at[slot]).start()

            first += size

    def settle(slot):
        pltpu.make_async_copy(obuf.at[slot], outs[0].at[0], osem.at[slot]).wait()

    def fetch(item, act):
        buf = lax.rem(item, BUFS)
        at = item * FIELDS
        top = pl.multiple_of(todo[at] * width, width)
        left = pl.multiple_of(todo[at + 1] * width, width)
        act(pltpu.make_async_copy(sigma.at[pl.ds(top, width), pl.ds(left, width)], sbuf.at[buf], ssem.at[buf]))

        @pl.when(todo[at + 7] == 1)
        def _():
            node, q = todo[at + 2], todo[at + 3]
            xslot = lax.rem(todo[at + 8], BUFS)
            source = panel.at[:, node // nodes, lax.rem(node, nodes), q]
            act(pltpu.make_async_copy(source, xbuf.at[xslot], xsem.at[xslot]))

    for ahead in range(BUFS - 2):
        @pl.when(begin + ahead < end)
        def _():
            fetch(begin + ahead, lambda copy: copy.start())

    def blank(item, carry):
        slot = empty[item]
        obuf[slot] = jnp.zeros(obuf.shape[1:], jnp.float32)
        put(slot)
        return carry

    lax.fori_loop(none_begin, none_end, blank, 0)

    def step(item, carry):
        @pl.when(item + BUFS - 2 < end)
        def _():
            fetch(item + BUFS - 2, lambda copy: copy.start())

        fetch(item, lambda copy: copy.wait())
        at = item * FIELDS
        slot = todo[at + 4]

        @pl.when(todo[at + 7] == 1)
        def _():
            high, low = split(xbuf[lax.rem(todo[at + 8], BUFS)].reshape(width, width))
            deep[:width] = high
            deep[width : 2 * width] = low
            deep[2 * width :] = high

        high, low = split(sbuf[lax.rem(item, BUFS)])
        term = jnp.dot(
            jnp.concatenate([high, high, low], axis=1), deep[...], preferred_element_type=jnp.float32
        )
        obuf[slot] = term + jnp.where(todo[at + 5] == 1, 0.0, obuf[slot])

        @pl.when(todo[at + 6] == 1)
        def _():
            put(slot)

        return carry

    lax.fori_loop(begin, end, step, 0)

    def drain(item, carry):
        @pl.when(todo[item * FIELDS + 6] == 1)
        def _():
            settle(todo[item * FIELDS + 4])

        return carry

    lax.fori_loop(begin, end, drain, 0)

    def drain_blank(item, carry):
        settle(empty[item])
        return carry

    lax.fori_loop(none_begin, none_end, drain_blank, 0)


def local_product(plan, sigma, panel, homes, part, planned, sizes):
    rows, _, nodes, _, strip, width = panel.shape
    total = homes * sum(sizes)
    hbm = pl.BlockSpec(memory_space=pl.ANY)
    smem = pl.BlockSpec(memory_space=pltpu.SMEM)
    return pl.pallas_call(
        functools.partial(product_kernel, part, planned, sizes, nodes, homes),
        out_shape=[jax.ShapeDtypeStruct((size, width, width), jnp.float32) for size in sizes for _ in range(homes)],
        in_specs=[smem, hbm, hbm],
        out_specs=[hbm] * (homes * len(sizes)),
        scratch_shapes=[
            pltpu.VMEM((BUFS, width, width), jnp.float32),
            pltpu.VMEM((BUFS, rows, strip, width), jnp.float32),
            pltpu.VMEM((3 * width, width), jnp.bfloat16),
            pltpu.VMEM((total, width, width), jnp.float32),
            pltpu.SemaphoreType.DMA((BUFS,)),
            pltpu.SemaphoreType.DMA((BUFS,)),
            pltpu.SemaphoreType.DMA((total,)),
        ],
        compiler_params=pltpu.CompilerParams(vmem_limit_bytes=50 * MIB),
        cost_estimate=pl.CostEstimate(flops=width, bytes_accessed=width, transcendentals=0),
    )(plan, sigma, panel)


def corner_kernel(base, sizes, own_rows, spot, own_struct, panel, *refs):
    totals, refs = refs[: len(sizes)], refs[len(sizes) :]
    if base:
        before, whole, own, out, gram, right, xbuf, xsem = refs
    else:
        gram, right, xbuf, xsem = refs
    nodes, entries = own_struct.shape
    width = gram.shape[1]
    my_row, my_col = spot[0], spot[1]
    slots = sum(sizes)

    def walk(act):
        def per_pair(pair, rank):
            node, p = pair // entries, lax.rem(pair, entries)
            mine = own_struct[node, p] // own_rows == my_row
            slot = rank - base

            @pl.when(mine & (slot >= 0) & (slot < slots))
            def _():
                act(node, slot, pltpu.make_async_copy(panel.at[:, my_col, node, p], xbuf.at[slot], xsem.at[slot]))

            return rank + mine.astype(jnp.int32)

        lax.fori_loop(0, nodes * entries, per_pair, jnp.int32(0))

    walk(lambda node, slot, copy: copy.start())
    gram[...] = before[...] if base else jnp.zeros(gram.shape, jnp.float32)

    def gather(node, slot, copy):
        copy.wait()
        left = xbuf[slot].reshape(width, width).T
        first = 0
        for total, size in zip(totals, sizes):
            @pl.when((slot >= first) & (slot < first + size))
            def _(total=total, first=first):
                right[...] = total[slot - first]

            first += size
        gram[node] += triple_dot(left, right[...])

    walk(gather)
    if base:
        def close(node, carry):
            inverse, mine = whole[node], own[node]
            out[node] = triple_dot(inverse.T, triple_dot(gram[node], inverse)) + triple_dot(mine.T, mine)
            return carry

        lax.fori_loop(0, nodes, close, 0)


def corner(spot, own_struct, panel, totals, base, sizes, own_rows, *ending):
    rows, _, nodes, _, strip, width = panel.shape
    vmem = pl.BlockSpec(memory_space=pltpu.VMEM)
    smem = pl.BlockSpec(memory_space=pltpu.SMEM)
    blocks = (nodes, width, width)
    return pl.pallas_call(
        functools.partial(corner_kernel, base, sizes, own_rows),
        out_shape=jax.ShapeDtypeStruct(blocks, jnp.float32),
        in_specs=[smem, smem, pl.BlockSpec(memory_space=pl.ANY)] + [vmem] * (len(totals) + len(ending)),
        out_specs=vmem,
        scratch_shapes=([pltpu.VMEM(blocks, jnp.float32)] if base else [])
        + [
            pltpu.VMEM((width, width), jnp.float32),
            pltpu.VMEM((sum(sizes), rows, strip, width), jnp.float32),
            pltpu.SemaphoreType.DMA((sum(sizes),)),
        ],
        compiler_params=pltpu.CompilerParams(vmem_limit_bytes=50 * MIB),
        cost_estimate=pl.CostEstimate(flops=6 * 8 * width**3, bytes_accessed=8 * MIB, transcendentals=0),
    )(spot, own_struct, panel, *totals, *ending)


def finish_kernel(sizes, shape, holder, rank, whole, *refs):
    nodes, entries, strip, width = shape
    arrived, (off, raw) = refs[: len(sizes)], refs[len(sizes) :]

    def per_node(node, carry):
        def pick(entry, carry):
            at = node * entries + entry
            first = 0
            for blocks, size in zip(arrived, sizes):
                slot = rank[at] - first

                @pl.when((slot >= 0) & (slot < size))
                def _(blocks=blocks, size=size, slot=slot):
                    raw[pl.ds(pl.multiple_of(entry * strip, strip), strip), :] = blocks[holder[at] * size + slot]

                first += size
            return carry

        lax.fori_loop(0, entries, pick, 0)
        off[node] = -triple_dot(raw[...], whole[node]).reshape(entries, strip, width)
        return carry

    lax.fori_loop(0, nodes, per_node, 0)


def finish(holder, rank, shape, whole, arrived, sizes):
    nodes, entries, strip, width = shape
    vmem = pl.BlockSpec(memory_space=pltpu.VMEM)
    smem = pl.BlockSpec(memory_space=pltpu.SMEM)
    return pl.pallas_call(
        functools.partial(finish_kernel, sizes, shape),
        out_shape=jax.ShapeDtypeStruct(shape, jnp.float32),
        in_specs=[smem] * 2 + [vmem] * (1 + len(arrived)),
        out_specs=vmem,
        scratch_shapes=[pltpu.VMEM((entries * strip, width), jnp.float32)],
        compiler_params=pltpu.CompilerParams(vmem_limit_bytes=50 * MIB),
        cost_estimate=pl.CostEstimate(flops=6 * nodes * entries * strip * width**2, bytes_accessed=8 * MIB, transcendentals=0),
    )(holder, rank, whole, *arrived)


def per_device(rows, homes, sigma_anc, panel, diag_inv, structure):
    nodes, entries, strip, width = panel.shape
    own_rows, own_cols = sigma_anc.shape[0] // width, sigma_anc.shape[1] // width
    chips = homes // 2

    struct = lax.all_gather(structure, "col", axis=0, tiled=True)
    every_panel = lax.all_gather(panel, ("row", "col"), axis=0, tiled=False)
    own_inverse, every_panel = lax.optimization_barrier((diag_inv, every_panel))
    inverse = lax.all_gather(own_inverse, "row", axis=1, tiled=True)
    every_panel = every_panel.reshape((rows, homes) + panel.shape)

    most = nodes * min(entries, own_rows)
    first_size = max(1, min(FIRST, most - 2))
    second_size = max(1, min(SECOND, most - first_size - 1))
    levels = sorted({min(slots, most) for slots in SLOTS + (most,)})
    holders = struct.reshape(homes, -1) // own_rows
    loads = jnp.sum(holders[:, :, None] == jnp.arange(rows, dtype=jnp.int32), axis=1)
    heaviest = jnp.max(loads)
    level = sum((heaviest > slots).astype(jnp.int32) for slots in levels[:-1])

    my_row = lax.axis_index("row").astype(jnp.int32)
    my_col = lax.axis_index("col").astype(jnp.int32)
    spot = jnp.stack([my_row, my_col])
    spans = ((0, first_size), (first_size, most - first_size))
    plan = make_plan(spot, struct, spans, nodes, own_rows, own_cols)

    holder = structure.reshape(-1) // own_rows
    pair = jnp.arange(nodes * entries, dtype=jnp.int32)
    earlier = (holder[:, None] == holder[None, :]) & (pair[None, :] < pair[:, None])
    rank = jnp.sum(earlier.astype(jnp.int32), axis=1)

    order = sorted(levels, key=lambda slots: abs(slots - USUAL))
    branch = jnp.asarray([order.index(slots) for slots in levels], jnp.int32)[level]
    plan, branch, holder, rank = lax.optimization_barrier((plan, branch, holder, rank))

    sibling = [(col, col ^ 1) for col in range(homes)]

    def to_rows(total):
        strips = total.reshape(-1, rows, strip, width).transpose(1, 0, 2, 3)
        landed = lax.all_to_all(strips, "row", split_axis=0, concat_axis=0, tiled=True)
        return landed.reshape(-1, strip, width)

    def between_cores(blocks):
        return [
            blocks[2 * away] + lax.ppermute(blocks[2 * away + 1], "col", sibling) for away in range(1, chips)
        ]

    def at_home(blocks):
        return blocks[0] + lax.ppermute(blocks[1], "col", sibling)

    def between_chips(sums):
        return [
            lax.ppermute(value, "col", [(col, (col + 2 * away) % homes) for col in range(homes)])
            for away, value in enumerate(sums, 1)
        ]

    def add(first, others):
        return functools.reduce(lambda left, right: left + right, others, first)

    planned = (homes * most, entries, len(spans))
    early = local_product(plan, sigma_anc, every_panel, homes, 0, planned, (first_size,))
    sums = between_cores(early)
    sums, plan = lax.optimization_barrier((sums, plan))
    crossed = between_chips(sums)
    late_sizes = (second_size, most - first_size - second_size)
    late = local_product(plan, sigma_anc, every_panel, homes, 1, planned, late_sizes)
    home = at_home(early)

    def with_slots(slots, every_panel, diag_inv, inverse, structure, spot, holder, rank, home, crossed, late):
        rest = slots - first_size - second_size
        count = -(-rest // LARGEST)
        sizes = [first_size, second_size] + [(rest + index) // count for index in reversed(range(count))]

        totals, start = [add(home, crossed)], 0
        for turn, size in enumerate(sizes[1:]):
            blocks = late[:homes] if turn == 0 else [more[start : start + size] for more in late[homes:]]
            start += size if turn else 0
            sums = between_cores(blocks)
            if turn:
                sums, crossed = lax.optimization_barrier((sums, crossed))
            else:
                totals[0], _ = lax.optimization_barrier((totals[0], sums))
            crossed = between_chips(sums)
            totals.append(add(at_home(blocks), crossed))

        arrived = [to_rows(total) for total in totals[:-1]]
        gram = corner(spot, structure, every_panel, totals[:-1], 0, sizes[:-1], own_rows)
        third, gram = lax.optimization_barrier((totals[-1], gram))
        arrived.append(to_rows(third))
        part = corner(
            spot, structure, every_panel, (third,), slots - sizes[-1], sizes[-1:], own_rows, gram, inverse, diag_inv
        )
        off = finish(holder, rank, panel.shape, inverse, arrived, sizes)
        return off, lax.psum_scatter(part, "row", scatter_dimension=1, tiled=True)

    branches = [functools.partial(with_slots, slots) for slots in order]
    operands = (every_panel, diag_inv, inverse, structure, spot, holder, rank, home, crossed, list(late))
    if len(branches) == 1:
        return branches[0](*operands)
    return lax.switch(branch, branches, *operands)


def solution(mesh):
    placed = (
        P(("grp", "row"), "col"),
        P(("grp", "col"), None, "row", None),
        P(("grp", "col"), "row", None),
        P("col", None),
    )
    return jax.shard_map(
        functools.partial(per_device, mesh.shape["row"], mesh.shape["col"]),
        mesh=mesh,
        in_specs=placed,
        out_specs=(P(("grp", "col"), None, "row", None), P(("grp", "col"), "row", None)),
        check_vma=False,
    )
```

```python
import functools

import jax
import jax.numpy as jnp
from jax import lax
from jax.experimental import pallas as pl
from jax.experimental.pallas import tpu as pltpu
from jax.sharding import PartitionSpec as P

SLOTS = (9, 10, 11, 12, 13, 15, 18)
FIRST, SECOND = 3, 5
LARGEST = 6
USUAL = 10.4
BUFS = 12
FIELDS = 9
MIB = 1024 * 1024


def split(value):
    high = value.astype(jnp.bfloat16)
    return high, (value - high.astype(jnp.float32)).astype(jnp.bfloat16)


def triple_dot(left, right):
    left_high, left_low = split(left)
    right_high, right_low = split(right)
    dot = functools.partial(jnp.dot, preferred_element_type=jnp.float32)
    return dot(left_high, right_high) + (dot(left_high, right_low) + dot(left_low, right_high))


class Part:
    def __init__(self, numbers, start):
        self.numbers, self.start = numbers, start

    def __getitem__(self, index):
        return self.numbers[self.start + index]

    def __setitem__(self, index, value):
        self.numbers[self.start + index] = value


def parts_of(lists, total, entries, spans):
    starts = [0, total * entries * FIELDS]
    starts.append(starts[-1] + spans)
    starts.append(starts[-1] + total)
    return [Part(lists, start) for start in starts], starts[-1] + spans


def plan_kernel(spans, total, nodes, own_rows, own_cols, spot, struct, lists):
    entries = struct.shape[1]
    (todo, ends, empty, empties), _ = parts_of(lists, total, entries, len(spans))
    homes = struct.shape[0] // nodes
    chips = homes // 2
    my_row, my_col = spot[0], spot[1]

    def piece_list(first, size, state):
        def per_home(home, state):
            distance = lax.rem(home // 2 - my_col // 2 + chips, chips)
            group = distance * 2 + lax.rem(home + my_col, 2)

            def per_node(member, state):
                rank, count, blocks, none = state
                node = home * nodes + member
                low = high = rank
                for p in range(entries):
                    mine = (struct[node, p] // own_rows == my_row).astype(jnp.int32)
                    high += mine
                held = high - low
                start = jnp.maximum(low, first)
                stop = jnp.minimum(high, first + size)
                columns = jnp.int32(0)
                for q in range(entries):
                    columns += (struct[node, q] // own_cols == my_col).astype(jnp.int32)

                def enlist():
                    def per_column(q, state):
                        order, count, blocks = state
                        other = struct[node, q]

                        def per_row(p, state):
                            at_rank, count = state
                            block = struct[node, p]
                            mine = block // own_rows == my_row

                            @pl.when(mine & (at_rank >= start) & (at_rank < stop))
                            def _():
                                at = count * FIELDS
                                todo[at] = block - my_row * own_rows
                                todo[at + 1] = other - my_col * own_cols
                                todo[at + 2] = node
                                todo[at + 3] = q
                                todo[at + 4] = group * size + at_rank - first
                                todo[at + 5] = (order == 0).astype(jnp.int32)
                                todo[at + 6] = (order == columns - 1).astype(jnp.int32)
                                todo[at + 7] = (at_rank == start).astype(jnp.int32)
                                todo[at + 8] = blocks

                            taken = mine & (at_rank >= start) & (at_rank < stop)
                            return at_rank + mine.astype(jnp.int32), count + taken.astype(jnp.int32)

                        def column():
                            return lax.fori_loop(0, entries, per_row, (low, count))[1]

                        hit = other // own_cols == my_col
                        count = lax.cond(hit, column, lambda: count)
                        step = hit.astype(jnp.int32)
                        return order + step, count, blocks + step

                    def all_empty():
                        def one(at_rank, none):
                            empty[none] = group * size + at_rank - first
                            return none + 1

                        return lax.fori_loop(start, stop, one, none)

                    _, more, further = lax.fori_loop(0, entries, per_column, (jnp.int32(0), count, blocks))
                    return more, further, lax.cond(columns == 0, all_empty, lambda: none)

                count, blocks, none = lax.cond(start < stop, enlist, lambda: (count, blocks, none))
                return high, count, blocks, none

            return lax.fori_loop(0, nodes, per_node, (jnp.int32(0),) + state)[1:]

        return lax.fori_loop(0, homes, per_home, state)

    count = none = jnp.int32(0)
    for piece, (first, size) in enumerate(spans):
        count, _, none = piece_list(first, size, (count, jnp.int32(0), none))
        ends[piece] = count
        empties[piece] = none


def make_plan(spot, struct, spans, nodes, own_rows, own_cols):
    total = struct.shape[0] // nodes * sum(size for _, size in spans)
    smem = pl.BlockSpec(memory_space=pltpu.SMEM)
    length = parts_of(None, total, struct.shape[1], len(spans))[1]
    return pl.pallas_call(
        functools.partial(plan_kernel, spans, total, nodes, own_rows, own_cols),
        out_shape=jax.ShapeDtypeStruct((length,), jnp.int32),
        in_specs=[smem, smem],
        out_specs=smem,
    )(spot, struct)


def product_kernel(part, planned, sizes, nodes, homes, lists, sigma, panel, *refs):
    (todo, ends, empty, empties), _ = parts_of(lists, *planned)
    outs = refs[: homes * len(sizes)]
    sbuf, xbuf, deep, obuf, ssem, xsem, osem = refs[homes * len(sizes) :]
    width = sbuf.shape[1]
    slots = sum(sizes)
    begin = ends[part - 1] if part else 0
    end = ends[part]
    none_begin = empties[part - 1] if part else 0
    none_end = empties[part]

    def put(slot):
        group = slot // slots
        inside = slot - group * slots
        first = 0
        for piece, size in enumerate(sizes):
            @pl.when((inside >= first) & (inside < first + size))
            def _(piece=piece, first=first):
                for other in range(homes):
                    @pl.when(group == other)
                    def _(out=outs[piece * homes + other]):
                        pltpu.make_async_copy(obuf.at[slot], out.at[inside - first], osem.at[slot]).start()

            first += size

    def settle(slot):
        pltpu.make_async_copy(obuf.at[slot], outs[0].at[0], osem.at[slot]).wait()

    def fetch(item, act):
        buf = lax.rem(item, BUFS)
        at = item * FIELDS
        top = pl.multiple_of(todo[at] * width, width)
        left = pl.multiple_of(todo[at + 1] * width, width)
        act(pltpu.make_async_copy(sigma.at[pl.ds(top, width), pl.ds(left, width)], sbuf.at[buf], ssem.at[buf]))

        @pl.when(todo[at + 7] == 1)
        def _():
            node, q = todo[at + 2], todo[at + 3]
            xslot = lax.rem(todo[at + 8], BUFS)
            source = panel.at[:, node // nodes, lax.rem(node, nodes), q]
            act(pltpu.make_async_copy(source, xbuf.at[xslot], xsem.at[xslot]))

    for ahead in range(BUFS - 2):
        @pl.when(begin + ahead < end)
        def _():
            fetch(begin + ahead, lambda copy: copy.start())

    def blank(item, carry):
        slot = empty[item]
        obuf[slot] = jnp.zeros(obuf.shape[1:], jnp.float32)
        put(slot)
        return carry

    lax.fori_loop(none_begin, none_end, blank, 0)

    def step(item, carry):
        @pl.when(item + BUFS - 2 < end)
        def _():
            fetch(item + BUFS - 2, lambda copy: copy.start())

        fetch(item, lambda copy: copy.wait())
        at = item * FIELDS
        slot = todo[at + 4]

        @pl.when(todo[at + 7] == 1)
        def _():
            high, low = split(xbuf[lax.rem(todo[at + 8], BUFS)].reshape(width, width))
            deep[:width] = high
            deep[width : 2 * width] = low
            deep[2 * width :] = high

        high, low = split(sbuf[lax.rem(item, BUFS)])
        term = jnp.dot(
            jnp.concatenate([high, high, low], axis=1), deep[...], preferred_element_type=jnp.float32
        )
        obuf[slot] = term + jnp.where(todo[at + 5] == 1, 0.0, obuf[slot])

        @pl.when(todo[at + 6] == 1)
        def _():
            put(slot)

        return carry

    lax.fori_loop(begin, end, step, 0)

    def drain(item, carry):
        @pl.when(todo[item * FIELDS + 6] == 1)
        def _():
            settle(todo[item * FIELDS + 4])

        return carry

    lax.fori_loop(begin, end, drain, 0)

    def drain_blank(item, carry):
        settle(empty[item])
        return carry

    lax.fori_loop(none_begin, none_end, drain_blank, 0)


def local_product(plan, sigma, panel, homes, part, planned, sizes):
    rows, _, nodes, _, strip, width = panel.shape
    total = homes * sum(sizes)
    hbm = pl.BlockSpec(memory_space=pl.ANY)
    smem = pl.BlockSpec(memory_space=pltpu.SMEM)
    return pl.pallas_call(
        functools.partial(product_kernel, part, planned, sizes, nodes, homes),
        out_shape=[jax.ShapeDtypeStruct((size, width, width), jnp.float32) for size in sizes for _ in range(homes)],
        in_specs=[smem, hbm, hbm],
        out_specs=[hbm] * (homes * len(sizes)),
        scratch_shapes=[
            pltpu.VMEM((BUFS, width, width), jnp.float32),
            pltpu.VMEM((BUFS, rows, strip, width), jnp.float32),
            pltpu.VMEM((3 * width, width), jnp.bfloat16),
            pltpu.VMEM((total, width, width), jnp.float32),
            pltpu.SemaphoreType.DMA((BUFS,)),
            pltpu.SemaphoreType.DMA((BUFS,)),
            pltpu.SemaphoreType.DMA((total,)),
        ],
        compiler_params=pltpu.CompilerParams(vmem_limit_bytes=50 * MIB),
        cost_estimate=pl.CostEstimate(flops=width, bytes_accessed=width, transcendentals=0),
    )(plan, sigma, panel)


def corner_kernel(base, sizes, own_rows, spot, own_struct, panel, *refs):
    totals, refs = refs[: len(sizes)], refs[len(sizes) :]
    if base:
        before, whole, own, out, gram, right, xbuf, xsem = refs
    else:
        gram, right, xbuf, xsem = refs
    nodes, entries = own_struct.shape
    width = gram.shape[1]
    my_row, my_col = spot[0], spot[1]
    slots = sum(sizes)

    def walk(act):
        def per_pair(pair, rank):
            node, p = pair // entries, lax.rem(pair, entries)
            mine = own_struct[node, p] // own_rows == my_row
            slot = rank - base

            @pl.when(mine & (slot >= 0) & (slot < slots))
            def _():
                act(node, slot, pltpu.make_async_copy(panel.at[:, my_col, node, p], xbuf.at[slot], xsem.at[slot]))

            return rank + mine.astype(jnp.int32)

        lax.fori_loop(0, nodes * entries, per_pair, jnp.int32(0))

    walk(lambda node, slot, copy: copy.start())
    gram[...] = before[...] if base else jnp.zeros(gram.shape, jnp.float32)

    def gather(node, slot, copy):
        copy.wait()
        left = xbuf[slot].reshape(width, width).T
        first = 0
        for total, size in zip(totals, sizes):
            @pl.when((slot >= first) & (slot < first + size))
            def _(total=total, first=first):
                right[...] = total[slot - first]

            first += size
        gram[node] += triple_dot(left, right[...])

    walk(gather)
    if base:
        def close(node, carry):
            inverse, mine = whole[node], own[node]
            out[node] = triple_dot(inverse.T, triple_dot(gram[node], inverse)) + triple_dot(mine.T, mine)
            return carry

        lax.fori_loop(0, nodes, close, 0)


def corner(spot, own_struct, panel, totals, base, sizes, own_rows, *ending):
    rows, _, nodes, _, strip, width = panel.shape
    vmem = pl.BlockSpec(memory_space=pltpu.VMEM)
    smem = pl.BlockSpec(memory_space=pltpu.SMEM)
    blocks = (nodes, width, width)
    return pl.pallas_call(
        functools.partial(corner_kernel, base, sizes, own_rows),
        out_shape=jax.ShapeDtypeStruct(blocks, jnp.float32),
        in_specs=[smem, smem, pl.BlockSpec(memory_space=pl.ANY)] + [vmem] * (len(totals) + len(ending)),
        out_specs=vmem,
        scratch_shapes=([pltpu.VMEM(blocks, jnp.float32)] if base else [])
        + [
            pltpu.VMEM((width, width), jnp.float32),
            pltpu.VMEM((sum(sizes), rows, strip, width), jnp.float32),
            pltpu.SemaphoreType.DMA((sum(sizes),)),
        ],
        compiler_params=pltpu.CompilerParams(vmem_limit_bytes=50 * MIB),
        cost_estimate=pl.CostEstimate(flops=6 * 8 * width**3, bytes_accessed=8 * MIB, transcendentals=0),
    )(spot, own_struct, panel, *totals, *ending)


def finish_kernel(sizes, shape, holder, rank, whole, *refs):
    nodes, entries, strip, width = shape
    arrived, (off, raw) = refs[: len(sizes)], refs[len(sizes) :]

    def per_node(node, carry):
        def pick(entry, carry):
            at = node * entries + entry
            first = 0
            for blocks, size in zip(arrived, sizes):
                slot = rank[at] - first

                @pl.when((slot >= 0) & (slot < size))
                def _(blocks=blocks, size=size, slot=slot):
                    raw[pl.ds(pl.multiple_of(entry * strip, strip), strip), :] = blocks[holder[at] * size + slot]

                first += size
            return carry

        lax.fori_loop(0, entries, pick, 0)
        off[node] = -triple_dot(raw[...], whole[node]).reshape(entries, strip, width)
        return carry

    lax.fori_loop(0, nodes, per_node, 0)


def finish(holder, rank, shape, whole, arrived, sizes):
    nodes, entries, strip, width = shape
    vmem = pl.BlockSpec(memory_space=pltpu.VMEM)
    smem = pl.BlockSpec(memory_space=pltpu.SMEM)
    return pl.pallas_call(
        functools.partial(finish_kernel, sizes, shape),
        out_shape=jax.ShapeDtypeStruct(shape, jnp.float32),
        in_specs=[smem] * 2 + [vmem] * (1 + len(arrived)),
        out_specs=vmem,
        scratch_shapes=[pltpu.VMEM((entries * strip, width), jnp.float32)],
        compiler_params=pltpu.CompilerParams(vmem_limit_bytes=50 * MIB),
        cost_estimate=pl.CostEstimate(flops=6 * nodes * entries * strip * width**2, bytes_accessed=8 * MIB, transcendentals=0),
    )(holder, rank, whole, *arrived)


def per_device(rows, homes, sigma_anc, panel, diag_inv, structure):
    nodes, entries, strip, width = panel.shape
    own_rows, own_cols = sigma_anc.shape[0] // width, sigma_anc.shape[1] // width
    chips = homes // 2

    struct = lax.all_gather(structure, "col", axis=0, tiled=True)
    every_panel = lax.all_gather(panel, ("row", "col"), axis=0, tiled=False)
    own_inverse, every_panel = lax.optimization_barrier((diag_inv, every_panel))
    inverse = lax.all_gather(own_inverse, "row", axis=1, tiled=True)
    every_panel = every_panel.reshape((rows, homes) + panel.shape)

    most = nodes * min(entries, own_rows)
    first_size = max(1, min(FIRST, most - 2))
    second_size = max(1, min(SECOND, most - first_size - 1))
    levels = sorted({min(slots, most) for slots in SLOTS + (most,)})
    holders = struct.reshape(homes, -1) // own_rows
    loads = jnp.sum(holders[:, :, None] == jnp.arange(rows, dtype=jnp.int32), axis=1)
    heaviest = jnp.max(loads)
    level = sum((heaviest > slots).astype(jnp.int32) for slots in levels[:-1])

    my_row = lax.axis_index("row").astype(jnp.int32)
    my_col = lax.axis_index("col").astype(jnp.int32)
    spot = jnp.stack([my_row, my_col])
    spans = ((0, first_size), (first_size, most - first_size))
    plan = make_plan(spot, struct, spans, nodes, own_rows, own_cols)

    holder = structure.reshape(-1) // own_rows
    pair = jnp.arange(nodes * entries, dtype=jnp.int32)
    earlier = (holder[:, None] == holder[None, :]) & (pair[None, :] < pair[:, None])
    rank = jnp.sum(earlier.astype(jnp.int32), axis=1)

    order = sorted(levels, key=lambda slots: abs(slots - USUAL))
    branch = jnp.asarray([order.index(slots) for slots in levels], jnp.int32)[level]
    plan, branch, holder, rank = lax.optimization_barrier((plan, branch, holder, rank))

    sibling = [(col, col ^ 1) for col in range(homes)]

    def to_rows(total):
        strips = total.reshape(-1, rows, strip, width).transpose(1, 0, 2, 3)
        landed = lax.all_to_all(strips, "row", split_axis=0, concat_axis=0, tiled=True)
        return landed.reshape(-1, strip, width)

    def between_cores(blocks):
        return [
            blocks[2 * away] + lax.ppermute(blocks[2 * away + 1], "col", sibling) for away in range(1, chips)
        ]

    def at_home(blocks):
        return blocks[0] + lax.ppermute(blocks[1], "col", sibling)

    def between_chips(sums):
        return [
            lax.ppermute(value, "col", [(col, (col + 2 * away) % homes) for col in range(homes)])
            for away, value in enumerate(sums, 1)
        ]

    def add(first, others):
        return functools.reduce(lambda left, right: left + right, others, first)

    planned = (homes * most, entries, len(spans))
    early = local_product(plan, sigma_anc, every_panel, homes, 0, planned, (first_size,))
    sums = between_cores(early)
    sums, plan = lax.optimization_barrier((sums, plan))
    crossed = between_chips(sums)
    late_sizes = (second_size, most - first_size - second_size)
    late = local_product(plan, sigma_anc, every_panel, homes, 1, planned, late_sizes)
    home = at_home(early)

    def with_slots(slots, every_panel, diag_inv, inverse, structure, spot, holder, rank, home, crossed, late):
        rest = slots - first_size - second_size
        count = -(-rest // LARGEST)
        sizes = [first_size, second_size] + [(rest + index) // count for index in reversed(range(count))]

        totals, start = [add(home, crossed)], 0
        for turn, size in enumerate(sizes[1:]):
            blocks = late[:homes] if turn == 0 else [more[start : start + size] for more in late[homes:]]
            start += size if turn else 0
            sums = between_cores(blocks)
            if turn:
                sums, crossed = lax.optimization_barrier((sums, crossed))
            else:
                totals[0], _ = lax.optimization_barrier((totals[0], sums))
            crossed = between_chips(sums)
            totals.append(add(at_home(blocks), crossed))

        arrived = [to_rows(total) for total in totals[:-1]]
        gram = corner(spot, structure, every_panel, totals[:-1], 0, sizes[:-1], own_rows)
        third, gram = lax.optimization_barrier((totals[-1], gram))
        sent, arrived[-1] = lax.optimization_barrier((third, arrived[-1]))
        arrived.append(to_rows(sent))
        part = corner(
            spot, structure, every_panel, (third,), slots - sizes[-1], sizes[-1:], own_rows, gram, inverse, diag_inv
        )
        off = finish(holder, rank, panel.shape, inverse, arrived, sizes)
        return off, lax.psum_scatter(part, "row", scatter_dimension=1, tiled=True)

    branches = [functools.partial(with_slots, slots) for slots in order]
    operands = (every_panel, diag_inv, inverse, structure, spot, holder, rank, home, crossed, list(late))
    if len(branches) == 1:
        return branches[0](*operands)
    return lax.switch(branch, branches, *operands)


def solution(mesh):
    placed = (
        P(("grp", "row"), "col"),
        P(("grp", "col"), None, "row", None),
        P(("grp", "col"), "row", None),
        P("col", None),
    )
    return jax.shard_map(
        functools.partial(per_device, mesh.shape["row"], mesh.shape["col"]),
        mesh=mesh,
        in_specs=placed,
        out_specs=(P(("grp", "col"), None, "row", None), P(("grp", "col"), "row", None)),
        check_vma=False,
    )
```
